256 devices in a mesh: ctx: 32 (over x, z_hi, y), tp: 8 (over z_lo, core).
Axes of the slice: x: 4, y: 4, z: 8 (z_hi: 2, z_lo: 4; z = z_hi * 4 + z_lo), core: 2. Of those that a mesh axis runs over, the one named last changes fastest.
Arguments:
- query_states: bfloat16 [8192, 8192], P('ctx', 'tp'), may hold values from -6 to 6
- key_states: bfloat16 [8192, 1024], P('ctx', 'tp'), may hold values from -6 to 6
- value_states: bfloat16 [8192, 1024], P('ctx', 'tp'), may hold values from -6 to 6
- head_kind: int32 [8], replicated, may hold values from 0 to 1, as said below
- page_owner: int32 [512], P('ctx'), may hold values from 0 to 31, as said below
Outputs:
- attn_out: bfloat16 [8192, 8192], P('ctx', 'tp')
- decode_cache: bfloat16 [2048, 16, 2048], P('ctx', None, 'tp')
The draws below stay inside these ranges and needn't reach their ends.
Inputs may be any that keep to these rules, and one draw needn't show every extreme that they name: `head_kind`: in every pair of KV heads 2 j and 2 j + 1 exactly one is a retrieval head. `page_owner`: the 16 pages of one token range send at most 2 pages to one owner, so an owner receives at most 64 pages; in every draw some owner receives 2 pages from every token range.
All inputs are finite; a program needn't handle non-finite values.
Results may differ from the reference program's by a relative error of at most 0.012.
Values may be sent and summed in bfloat16 or wider, within the bound.
No kernel may reach another device: no remote copies, remote signals or barrier semaphores. Data moves between devices by JAX's collectives and lax.ppermute only.
A program may use at most 64 MiB of HBM per device.

```python
import math
import jax
import jax.numpy as jnp
from jax import lax

KV_HEADS = 8
GROUP = 8
HD = 128
TOK_DEV = 256
SINK = 64
RECENT = 1024
PAGE = 16
TOKENS = 8192
PPD = 16
MOST = 2
SLOTS = 64
PAGES = 512
CACHE = 2048
N_CTX = 32


def draw_query_states(key, part):
    key = jax.random.fold_in(key, 11)
    shape_all = (TOKENS, KV_HEADS, GROUP, HD)
    values = jnp.clip(jax.random.normal(key, shape_all, jnp.float32), -6.0, 6.0)
    return values.reshape(TOKENS, KV_HEADS * GROUP * HD).astype(jnp.bfloat16)


def draw_key_states(key, part):
    key = jax.random.fold_in(key, 12)
    shape_all = (TOKENS, KV_HEADS, HD)
    values = jnp.clip(jax.random.normal(key, shape_all, jnp.float32), -6.0, 6.0)
    return values.reshape(TOKENS, KV_HEADS * HD).astype(jnp.bfloat16)


def draw_head_kind(key, part):
    key = jax.random.fold_in(key, 13)
    pair_bits = jax.random.randint(key, (KV_HEADS // 2,), 0, 2)
    return jnp.stack([pair_bits, 1 - pair_bits], axis=1).reshape(KV_HEADS).astype(jnp.int32)


def draw_page_owner(key, part):
    key = jax.random.fold_in(key, 14)
    hot_key, rest_key = jax.random.split(key)
    hot_owner = jax.random.randint(hot_key, (), 0, N_CTX)
    sender_keys = jax.random.split(rest_key, N_CTX)
    slot_ids = jnp.arange(SLOTS, dtype=jnp.int32)

    def one_sender(sender_key):
        first_key, second_key = jax.random.split(sender_key)
        ordering = jax.random.permutation(first_key, SLOTS).astype(jnp.int32)
        slot_score = ordering - SLOTS * (slot_ids // MOST == hot_owner).astype(jnp.int32)
        chosen = jnp.argsort(slot_score, stable=True)[:PPD]
        owners = (chosen // MOST).astype(jnp.int32)
        return jax.random.permutation(second_key, owners)
    return jax.vmap(one_sender)(sender_keys).reshape(PAGES).astype(jnp.int32)


def shard_levels(key, extent, shards, least, top_value):
    factor_of, own = 1.0, jax.random.fold_in(key, 6)
    for axis_at, parts in shards:
        draws = jnp.exp(jax.random.uniform(jax.random.fold_in(own, axis_at), (parts,), jnp.float32, least / len(shards), top_value / len(shards)))
        factor_of = factor_of * jnp.repeat(draws, extent[axis_at] // parts).reshape([-1 if axis == axis_at else 1 for axis in range(len(extent))])
    return factor_of


def bell_draw(rng, shape, deviation, reach, cuts=(), held_as=jnp.bfloat16):
    array = deviation * jax.random.normal(rng, shape, jnp.float32)
    if cuts:
        array = array * shard_levels(rng, shape, cuts, -0.22, 0.18)
    return jnp.clip(array, -reach, reach).astype(held_as)


def setup_inputs(seed: int = 0) -> dict:
    key_of = jax.random.split(jax.random.key(seed), 6)
    return {
        "query_states": draw_query_states(jax.random.fold_in(key_of[5], 71), 0),
        "key_states": draw_key_states(jax.random.fold_in(key_of[5], 71), 0),
        "value_states": bell_draw(key_of[2], (TOKENS, KV_HEADS * HD), 1.0, 6.0, ((0, 32), (1, 8))),
        "head_kind": draw_head_kind(jax.random.fold_in(key_of[5], 71), 0),
        "page_owner": draw_page_owner(jax.random.fold_in(key_of[5], 71), 0),
    }


def reference(query_states, key_states, value_states, head_kind, page_owner):
    score_scale = 1.0 / math.sqrt(HD)
    queries = query_states.astype(jnp.float32).reshape(TOKENS, KV_HEADS, GROUP, HD)
    key_heads = key_states.astype(jnp.float32).reshape(TOKENS, KV_HEADS, HD)
    value_heads = value_states.astype(jnp.float32).reshape(TOKENS, KV_HEADS, HD)
    key_pos = jnp.arange(TOKENS, dtype=jnp.int32)
    block_count = TOKENS // TOK_DEV

    def one_head(head_index):
        head_queries = lax.dynamic_index_in_dim(queries, head_index, 1, keepdims=False)
        head_keys = lax.dynamic_index_in_dim(key_heads, head_index, 1, keepdims=False)
        head_values = lax.dynamic_index_in_dim(value_heads, head_index, 1, keepdims=False)
        retrieval = lax.dynamic_index_in_dim(head_kind, head_index, 0, keepdims=False) == 1

        def one_block(block_index):
            block_queries = lax.dynamic_slice_in_dim(head_queries, block_index * TOK_DEV, TOK_DEV, 0)
            query_pos = block_index * TOK_DEV + jnp.arange(TOK_DEV, dtype=jnp.int32)
            scores = jnp.einsum('tgd,sd->gts', block_queries, head_keys, precision=lax.Precision.HIGHEST) * score_scale
            query_gap = query_pos[:, None] - key_pos[None, :]
            allowed = (query_gap >= 0) & (retrieval | (key_pos[None, :] < SINK) | (query_gap < RECENT))
            scores = jnp.where(allowed[None], scores, -jnp.inf)
            row_max = lax.optimization_barrier(jnp.max(scores, axis=-1, keepdims=True))
            weights = jnp.where(allowed[None], jnp.exp(scores - row_max), 0.0)
            denominator = lax.optimization_barrier(jnp.sum(weights, axis=-1))
            rounded = lax.optimization_barrier(weights.astype(jnp.bfloat16)).astype(jnp.float32)
            mixture = jnp.einsum('gts,sd->gtd', rounded, head_values, precision=lax.Precision.HIGHEST)
            return (mixture / denominator[..., None]).astype(jnp.bfloat16)
        return lax.map(one_block, jnp.arange(block_count, dtype=jnp.int32))
    per_head = lax.map(one_head, jnp.arange(KV_HEADS, dtype=jnp.int32))
    attn_out = per_head.transpose(1, 3, 0, 2, 4).reshape(TOKENS, KV_HEADS * GROUP * HD)
    kind_scale = head_kind.astype(jnp.bfloat16)
    key_flag = key_states.reshape(TOKENS, KV_HEADS, HD) * kind_scale[None, :, None]
    value_flag = value_states.reshape(TOKENS, KV_HEADS, HD) * kind_scale[None, :, None]
    paired = jnp.stack([key_flag, value_flag], axis=2).reshape(PAGES, PAGE, KV_HEADS * 2 * HD)
    owners = page_owner.reshape(N_CTX, PPD)
    same_owner = owners[:, :, None] == owners[:, None, :]
    earlier = jnp.arange(PPD, dtype=jnp.int32)[None, :] < jnp.arange(PPD, dtype=jnp.int32)[:, None]
    page_rank = lax.optimization_barrier(jnp.sum((same_owner & earlier[None]).astype(jnp.int32), axis=2))
    ranges = jnp.arange(N_CTX, dtype=jnp.int32)[:, None]
    target = (owners * SLOTS + ranges * MOST + page_rank).reshape(PAGES).astype(jnp.int32)
    decode_cache = jnp.zeros((CACHE, PAGE, KV_HEADS * 2 * HD), jnp.bfloat16).at[target].set(paired)
    return (attn_out, decode_cache)
```

```python
import functools
import math

import jax
import jax.numpy as jnp
from jax import lax
from jax.experimental import pallas as pl
from jax.experimental.pallas import tpu as pltpu
from jax.sharding import PartitionSpec as P

GROUP = 8
HD = 128
SINK = 64
RECENT = 1024
PAGE = 16
ROWS = 256
HALF = 128
QUART = 64
SINK_HALF = 32
NEG = -1e30
SCALE = math.log2(math.e) / math.sqrt(HD)
F32 = jnp.float32
BF16 = jnp.bfloat16


def ctx_of(x, z, y):
    return (x % 4) * 8 + (z % 2) * 4 + (y % 4)


CHIPS = [(x, z, y) for x in range(4) for z in range(2) for y in range(4)]
CORE_SWAP = [(i, i ^ 1) for i in range(8)]
Z_SWAP = [(ctx_of(x, z, y), ctx_of(x, z + 1, y)) for x, z, y in CHIPS]
X_SHIFT = {s: [(ctx_of(x, z, y), ctx_of(x + s, z, y)) for x, z, y in CHIPS] for s in (1, 2, 3)}
Y_SHIFT = {s: [(ctx_of(x, z, y), ctx_of(x, z, y + s)) for x, z, y in CHIPS] for s in (1, 2, 3)}


def half_row_pos(j, core):
    return ((j >> 3) << 4) + (core << 3) + (j & 7)


def nt_dot(a, b):
    return lax.dot_general(a, b, (((1,), (1,)), ((), ())), preferred_element_type=F32)


def fold_chunk(q, k, v_ext, m_old, acc_old, allowed):
    s = nt_dot(q, k)
    if allowed is not None:
        s = jnp.where(allowed, s, NEG)
    m_new = jnp.maximum(m_old, jnp.max(s, axis=1, keepdims=True))
    p = jnp.exp2((s - m_new) * SCALE)
    if allowed is not None:
        p = jnp.where(allowed, p, 0.0)
    update = jnp.dot(p.astype(BF16), v_ext, preferred_element_type=F32)
    return m_new, acc_old * jnp.exp2((m_old - m_new) * SCALE) + update


def finish_head(m, acc):
    total = acc[:, HD:HD + 1]
    out = acc[:, :HD] / jnp.maximum(acc[:, HD:], 1e-37)
    lse = jnp.where(total > 0.0, m * SCALE + jnp.log2(jnp.maximum(total, 1e-37)), NEG)
    return out.astype(BF16), lse


def pass_kernel(sc, q_own, q_other, own, p1, p2, p3, far, o_ref, lse_ref, k_s, v_s):
    y, core, c, is_r = sc[1], sc[3], sc[4], sc[5]
    v_s[:, HD:] = jnp.ones((6 * HALF, HD), BF16)
    pieces = (own, p1, p2, p3, far)
    for n, ref in enumerate(pieces):
        k_s[pl.ds(n * HALF, HALF), :] = ref[0:HALF, :]
        v_s[pl.ds(n * HALF, HALF), 0:HD] = ref[HALF:2 * HALF, :]
    base = 5 * HALF
    k_s[pl.ds(base, HALF), :] = jnp.zeros((HALF, HD), BF16)
    v_s[pl.ds(base, HALF), 0:HD] = jnp.zeros((HALF, HD), BF16)

    for n, (ref, off) in enumerate(((far, 256), (p1, 256), (p2, 256), (p3, 256))):
        @pl.when(y == n)
        def _(ref=ref, off=off):
            k_s[pl.ds(base, SINK_HALF), :] = ref[off:off + SINK_HALF, :]
            v_s[pl.ds(base, SINK_HALF), 0:HD] = ref[off + SINK_HALF:off + 2 * SINK_HALF, :]

    n = lax.broadcasted_iota(jnp.int32, (1, 6 * HALF), 1)
    slot = n >> 7
    j = n & (HALF - 1)
    is_sink = slot == 5
    rel = half_row_pos(j, core)
    pos = jnp.where(is_sink, rel, rel + (c - slot) * ROWS)
    qpos = c * ROWS + lax.broadcasted_iota(jnp.int32, (ROWS, 1), 0)
    gap = qpos - pos
    window = (gap >= 0) & (gap < RECENT) & (pos >= 0) & (slot < 5)
    sink = is_sink & (j < SINK_HALF) & (gap >= RECENT)
    allowed = window | sink
    bias = jnp.where(allowed, 0.0, NEG)
    lane = lax.broadcasted_iota(jnp.int32, (ROWS, HD), 1)
    lse_ref[...] = jnp.zeros((ROWS, HD), F32)

    def head(a, carry):
        col = pl.ds(pl.multiple_of(a * HD, HD), HD)
        q = jnp.where(is_r == 1, q_other[:, col], q_own[:, col])
        m0 = jnp.full((ROWS, 1), NEG, F32)
        m, acc = fold_chunk(q, k_s[...], v_s[...], m0, jnp.zeros((ROWS, 2 * HD), F32), bias == 0.0)
        out, lse = finish_head(m, acc)
        o_ref[:, col] = out
        lse_ref[...] = jnp.where(lane == a, lse, lse_ref[...])
        return carry

    lax.fori_loop(0, GROUP, head, 0)


def full_kernel(sc, q_own, q_other, a0, a1, a2, a3, b0, b1, b2, b3, op_ref, lsep_ref,
                keep_ref, keep_lse, send_ref, send_lse, k_s, v_s, m_s, acc_s):
    x, y, z, core, c, is_r = sc[0], sc[1], sc[2], sc[3], sc[4], sc[5]
    first = (a0, a1, a2, a3)
    second = (b0, b1, b2, b3)
    v_s[:, HD:] = jnp.ones((16 * QUART, HD), BF16)
    qpos = c * ROWS + lax.broadcasted_iota(jnp.int32, (ROWS, 1), 0)
    n = lax.broadcasted_iota(jnp.int32, (1, 16 * QUART), 1)
    dy = (n >> 7) & 3
    colour = (n >> 6) & 1
    j = (n & (QUART - 1)) + ((n >> 9) << 6)
    zz = jnp.where(colour == 0, z, 1 - z)
    yy = (y - dy) & 3
    pos = (x * 8 + zz * 4 + yy) * ROWS + half_row_pos(j, core)
    lane = lax.broadcasted_iota(jnp.int32, (ROWS, HD), 1)

    def run(dx):
        for d in range(4):
            for col in range(2):
                at = (d * 2 + col) * QUART
                k_s[pl.ds(at, QUART), :] = first[dx][d, col, 0:QUART, :]
                v_s[pl.ds(at, QUART), 0:HD] = first[dx][d, col, QUART:2 * QUART, :]
                at += 8 * QUART
                k_s[pl.ds(at, QUART), :] = second[d][dx, col, 0:QUART, :]
                v_s[pl.ds(at, QUART), 0:HD] = second[d][dx, col, QUART:2 * QUART, :]

        def head(a, carry):
            cols = pl.ds(pl.multiple_of(a * HD, HD), HD)
            q = jnp.where(is_r == 1, q_own[:, cols], q_other[:, cols])
            if dx == 0:
                m0 = jnp.full((ROWS, 1), NEG, F32)
                m, acc = fold_chunk(q, k_s[...], v_s[...], m0, jnp.zeros((ROWS, 2 * HD), F32), pos <= qpos)
            else:
                m, acc = fold_chunk(q, k_s[...], v_s[...], m_s[a][:, 0:1], acc_s[a], None)
            m_s[a] = jnp.broadcast_to(m, (ROWS, HD))
            acc_s[a] = acc
            return carry

        lax.fori_loop(0, GROUP, head, 0)

    run(0)
    for dx in (1, 2, 3):
        pl.when(x >= dx)(functools.partial(run, dx))

    keep_lse[...] = lsep_ref[...]
    send_lse[...] = lsep_ref[...]

    def finish(mine, mine_lse, other):
        mine_lse[...] = jnp.zeros((ROWS, HD), F32)

        def head(a, carry):
            cols = pl.ds(pl.multiple_of(a * HD, HD), HD)
            out, lse = finish_head(m_s[a][:, 0:1], acc_s[a])
            mine[:, cols] = out
            other[:, cols] = op_ref[:, cols]
            mine_lse[...] = jnp.where(lane == a, lse, mine_lse[...])
            return carry

        lax.fori_loop(0, GROUP, head, 0)

    @pl.when(is_r == 1)
    def _():
        finish(keep_ref, keep_lse, send_ref)

    @pl.when(is_r == 0)
    def _():
        finish(send_ref, send_lse, keep_ref)


def merge_kernel(o0, lse0, o1, lse1, out_ref):
    for a in range(GROUP):
        cols = slice(a * HD, (a + 1) * HD)
        l0, l1 = lse0[:, a:a + 1], lse1[:, a:a + 1]
        top = jnp.maximum(l0, l1)
        w0, w1 = jnp.exp2(l0 - top), jnp.exp2(l1 - top)
        scale = 1.0 / (w0 + w1)
        out = o0[:, cols].astype(F32) * (w0 * scale) + o1[:, cols].astype(F32) * (w1 * scale)
        out_ref[:, cols] = out.astype(BF16)


def pages_kernel(sc, a0, a1, a2, a3, b0, b1, b2, b3, out_ref):
    x, y, z, c = sc[0], sc[1], sc[2], sc[4]
    first = (a0, a1, a2, a3)
    second = (b0, b1, b2, b3)
    row = lax.broadcasted_iota(jnp.int32, (PAGE, HD), 0)
    lane = lax.broadcasted_iota(jnp.int32, (PAGE, HD), 1)
    same_row = (lane & 7) == (row & 7)
    want = (2 * c + (row >> 3)).astype(F32)
    for dx in range(4):
        for d in range(4):
            for col in range(2):
                f, s = first[dx], second[d]
                code = f[d, col, 2 * QUART:2 * QUART + 16, :].astype(F32)
                select = jnp.where(same_row & (code == want), 1.0, 0.0).astype(BF16)
                xx = (x - dx) & 3
                yy = (y - d) & 3
                zz = z if col == 0 else 1 - z
                block = xx * 8 + zz * 4 + yy
                for part in range(2):
                    rows = slice(part * QUART, (part + 1) * QUART)
                    pages = jnp.dot(select[:, :QUART], f[d, col, rows, :], preferred_element_type=F32)
                    pages += jnp.dot(select[:, QUART:], s[dx, col, rows, :], preferred_element_type=F32)
                    out_ref[block, :, part * HD:(part + 1) * HD] = pages.astype(BF16)


VMEM_SPEC = pl.BlockSpec(memory_space=pltpu.VMEM)
SMEM_SPEC = pl.BlockSpec(memory_space=pltpu.SMEM)


def call(kernel, out_shape, scratch, flops, sc, *args):
    many = isinstance(out_shape, tuple)
    specs = ([SMEM_SPEC] if sc is not None else []) + [VMEM_SPEC] * len(args)
    operands = ([sc] if sc is not None else []) + list(args)
    return pl.pallas_call(
        kernel,
        out_shape=out_shape,
        in_specs=specs,
        out_specs=(VMEM_SPEC,) * len(out_shape) if many else VMEM_SPEC,
        scratch_shapes=scratch,
        compiler_params=pltpu.CompilerParams(vmem_limit_bytes=40 * 1024 * 1024),
        cost_estimate=pl.CostEstimate(flops=flops, bytes_accessed=4 << 20, transcendentals=flops // 512),
    )(*operands)


def shards(q, k, v, head_kind, page_owner):
    c = lax.axis_index("ctx")
    tp = lax.axis_index("tp")
    x, z, y = c // 8, (c // 4) % 2, c % 4
    core = tp % 2
    is_r = lax.dynamic_index_in_dim(head_kind, tp, 0, keepdims=False) == 1
    sc = jnp.stack([x, y, z, core, c, is_r.astype(jnp.int32), tp, tp]).astype(jnp.int32)

    earlier = lax.iota(jnp.int32, 16)[None, :] < lax.iota(jnp.int32, 16)[:, None]
    rank = jnp.sum(((page_owner[:, None] == page_owner[None, :]) & earlier).astype(jnp.int32), axis=1)
    code = jnp.repeat((page_owner * 2 + rank).astype(BF16), 8)
    meta = jnp.broadcast_to(code[None, :], (16, HD))

    kv = jnp.stack([k, v]).reshape(2, 16, 2, 8, HD)
    stay = lax.dynamic_index_in_dim(kv, core, 2, keepdims=False).reshape(2, HALF, HD)
    leave = lax.dynamic_index_in_dim(kv, 1 - core, 2, keepdims=False).reshape(2, HALF, HD)
    came = lax.ppermute(leave, "tp", CORE_SWAP)
    q_other = lax.ppermute(q, "tp", CORE_SWAP)
    ret = jnp.where(is_r, stay, came)
    pas = jnp.where(is_r, came, stay)

    r1 = jnp.concatenate([ret[0, :QUART], ret[1, :QUART], meta])
    r2 = jnp.concatenate([ret[0, QUART:], ret[1, QUART:]])
    pas = pas.reshape(2 * HALF, HD)
    mine = jnp.concatenate([r1, r2, pas])
    theirs = lax.ppermute(mine, "ctx", Z_SWAP)
    n1, n2 = r1.shape[0], r1.shape[0] + r2.shape[0]
    r1 = jnp.stack([r1, theirs[:n1]])
    r2 = jnp.stack([r2, theirs[n1:n2]])
    pas_z = theirs[n2:]
    low = jnp.where(z == 0, pas, pas_z)
    sink = jnp.concatenate([low[:SINK_HALF], low[HALF:HALF + SINK_HALF]])

    pas_x = lax.ppermute(pas_z, "ctx", [(ctx_of(i, 0, j), ctx_of(i + 1, 0, j)) for i in range(3) for j in range(4)])
    h1 = jnp.stack([r1] + [lax.ppermute(r1, "ctx", Y_SHIFT[s]) for s in (1, 2, 3)])
    m2 = jnp.concatenate([r2.reshape(2 * HALF, HD), sink])
    got = [lax.ppermute(m2, "ctx", X_SHIFT[s]) for s in (1, 2, 3)]
    h2 = jnp.stack([r2] + [g[:2 * HALF].reshape(2, HALF, HD) for g in got])
    for s in (1, 2, 3):
        sink = jnp.where(x == s, got[s - 1][2 * HALF:], sink)

    far = jnp.where(z == 1, pas_z, pas_x)
    near_pas = {s: jnp.concatenate([jnp.where(y + s < 4, pas, far), sink]) for s in (1, 2, 3)}
    p = [lax.ppermute(near_pas[s], "ctx", Y_SHIFT[s]) for s in (1, 2, 3)]
    far = jnp.concatenate([far, sink])

    a = [h1] + [lax.ppermute(h1, "ctx", X_SHIFT[s]) for s in (1, 2, 3)]
    b = [h2] + [lax.ppermute(h2, "ctx", Y_SHIFT[s]) for s in (1, 2, 3)]

    o_shape = jax.ShapeDtypeStruct((ROWS, GROUP * HD), BF16)
    lse_shape = jax.ShapeDtypeStruct((ROWS, HD), F32)
    o_pas, lse_pas = call(
        pass_kernel, (o_shape, lse_shape),
        [pltpu.VMEM((6 * HALF, HD), BF16), pltpu.VMEM((6 * HALF, 2 * HD), BF16)],
        2 * 2048 * 768 * 384, sc, q, q_other, pas, *p, far)
    keep, keep_lse, send, send_lse = call(
        full_kernel, (o_shape, lse_shape, o_shape, lse_shape),
        [pltpu.VMEM((16 * QUART, HD), BF16), pltpu.VMEM((16 * QUART, 2 * HD), BF16),
         pltpu.VMEM((GROUP, ROWS, HD), F32), pltpu.VMEM((GROUP, ROWS, 2 * HD), F32)],
        2 * 2048 * 4096 * 384, sc, q, q_other, *a, *b, o_pas, lse_pas)
    pages = call(pages_kernel, jax.ShapeDtypeStruct((32, PAGE, 2 * HD), BF16), [], 1 << 26, sc, *a, *b)

    got_o = lax.ppermute(send, "tp", CORE_SWAP)
    got_lse = lax.ppermute(send_lse, "tp", CORE_SWAP)
    got_pages = lax.ppermute(pages, "tp", CORE_SWAP)
    attn_out = call(merge_kernel, o_shape, [], 1 << 24, None, keep, keep_lse, got_o, got_lse)
    here = pages.reshape(SINK, 1, 8, 2 * HD)
    there = got_pages.reshape(SINK, 1, 8, 2 * HD)
    both = jnp.where(core == 0, jnp.concatenate([here, there], 1), jnp.concatenate([there, here], 1))
    decode_cache = jnp.where(is_r, both.reshape(SINK, PAGE, 2 * HD), jnp.zeros((), BF16))
    return attn_out, decode_cache


def solution(mesh):
    return jax.shard_map(
        shards,
        mesh=mesh,
        in_specs=(P("ctx", "tp"), P("ctx", "tp"), P("ctx", "tp"), P(), P("ctx")),
        out_specs=(P("ctx", "tp"), P("ctx", None, "tp")),
        check_vma=False,
    )
```

```python
import math

import jax
import jax.numpy as jnp
from jax import lax
from jax.experimental import pallas as pl
from jax.experimental.pallas import tpu as pltpu
from jax.sharding import PartitionSpec as P

GROUP = 8
HD = 128
SINK = 64
RECENT = 1024
PAGE = 16
ROWS = 256
HALF = 128
QUART = 64
META = 16
FIRST = 2 * QUART + META
CHUNK = 512
NEG = -1e30
SCALE = math.log2(math.e) / math.sqrt(HD)
F32 = jnp.float32
BF16 = jnp.bfloat16


def ctx_of(x, z, y):
    return (x % 4) * 8 + (z % 2) * 4 + (y % 4)


CHIPS = [(x, z, y) for x in range(4) for z in range(2) for y in range(4)]
CORE_SWAP = [(i, i ^ 1) for i in range(8)]
Z_SWAP = [(ctx_of(x, z, y), ctx_of(x, z + 1, y)) for x, z, y in CHIPS]
FOUR_ON = [(i, i + 4) for i in range(28)]
X_SHIFT = {s: [(ctx_of(x, z, y), ctx_of(x + s, z, y)) for x, z, y in CHIPS] for s in (1, 2, 3)}
Y_SHIFT = {s: [(ctx_of(x, z, y), ctx_of(x, z, y + s)) for x, z, y in CHIPS] for s in (1, 2, 3)}


def nt_dot(a, b):
    return lax.dot_general(a, b, (((1,), (1,)), ((), ())), preferred_element_type=F32)


def iota(shape, axis):
    return lax.broadcasted_iota(jnp.int32, shape, axis)


def fold(state, q, k, v, left=None, right=None):
    m, l, o = state
    s = nt_dot(q, k)
    if left is not None:
        s = jnp.concatenate([s[:, :HD] + left, s[:, HD:]], axis=1) if s.shape[1] > HD else s + left
    if right is not None:
        s = jnp.concatenate([s[:, :-HD], s[:, -HD:] + right], axis=1)
    top = jnp.maximum(m, jnp.max(s, axis=1, keepdims=True))
    p = jnp.exp2((s - top) * SCALE).astype(BF16)
    up = jnp.dot(p, v, preferred_element_type=F32)
    keep = jnp.exp2((m - top) * SCALE)
    return top, l * keep + up[:, HD:HD + 1], o * keep + up[:, :HD]


def start():
    return jnp.full((ROWS, 1), NEG, F32), jnp.zeros((ROWS, 1), F32), jnp.zeros((ROWS, HD), F32)


def put_keys(k_s, v_s, at, ref, first, rows, gap):
    k_s[pl.ds(at, rows), 0:HD] = ref[first:first + rows, :]
    v_s[pl.ds(at, rows), 0:HD] = ref[first + gap:first + gap + rows, :]


def put_first(k_s, v_s, at, ref):
    for n in range(8):
        put_keys(k_s, v_s, at + n * QUART, ref, n * FIRST, QUART, QUART)


def put_second(k_s, v_s, at, ref):
    for n in range(8):
        put_keys(k_s, v_s, at + n * QUART, ref, n * 2 * QUART, QUART, QUART)


def put_bias(k_s, v_s, bias):
    lane = iota(bias.shape, 1)
    k_s[:, HD:] = jnp.where(lane == 0, bias, 0.0).astype(BF16)
    v_s[:, HD:] = jnp.ones(bias.shape, BF16)


def range_bias(sc, shape, chunks):
    x, y, z, c = sc[0], sc[1], sc[2], sc[4]
    n = iota(shape, 0)
    outer, far = (n >> 7) & 3, (n >> 6) & 1
    which = n >> 9
    dx, dy = outer, outer
    for i, (fixed_x, fixed_y) in enumerate(chunks):
        if fixed_x is not None:
            dx = jnp.where(which == i, fixed_x, dx)
        else:
            dy = jnp.where(which == i, fixed_y, dy)
    zz = jnp.where(far == 0, z, 1 - z)
    block = ((x - dx) & 3) * 8 + zz * 4 + ((y - dy) & 3)
    return jnp.where(block <= c, 0.0, NEG)


def load_head(q_a, q_b, flag, a):
    cols = pl.ds(pl.multiple_of(a * HD, HD), HD)
    q = jnp.where(flag == 1, q_a[:, cols], q_b[:, cols])
    one = jnp.where(iota((ROWS, HD), 1) == 0, 1.0, 0.0).astype(BF16)
    return jnp.concatenate([q, one], axis=1)


def load_state(acc, lm, a):
    lane = iota((ROWS, HD), 1)
    block = lm[...]
    m = jnp.max(jnp.where(lane == a, block, -jnp.inf), axis=1, keepdims=True)
    l = jnp.max(jnp.where(lane == a + GROUP, block, -jnp.inf), axis=1, keepdims=True)
    return m, l, acc[a]


def store_state(acc, lm, a, state):
    lane = iota((ROWS, HD), 1)
    m, l, o = state
    acc[a] = o
    lm[...] = jnp.where(lane == a, m, jnp.where(lane == a + GROUP, l, lm[...]))


def near_kernel(sc, q_own, q_other, pas, y1, y2, y3, far, h1, h2, acc_p, lm_p, acc_r, lm_r, kp, vp, kr, vr):
    core, c, is_r = sc[3], sc[4], sc[5]
    put_keys(kp, vp, 0, pas, 0, HALF, HALF)
    for n, ref in enumerate((y1, y2, y3)):
        put_keys(kp, vp, (n + 1) * HALF, ref, 2 * FIRST, HALF, HALF)
    put_keys(kp, vp, 4 * HALF, far, 0, HALF, HALF)
    put_bias(kp, vp, jnp.where((iota((5 * HALF, HD), 0) >> 7) <= c, 0.0, NEG))
    put_first(kr, vr, 0, h1)
    put_second(kr, vr, CHUNK, h2)
    put_bias(kr, vr, range_bias(sc, (2 * CHUNK, HD), ((0, None), (None, 0))))

    row = iota((ROWS, HD), 0)
    lane = iota((ROWS, HD), 1)
    key = core * HALF + lane
    own = jnp.where(key > row, NEG, 0.0)
    edge = jnp.where(key <= row, NEG, 0.0)
    first = jnp.where((lane < QUART) & (key > row), NEG, 0.0)
    second = jnp.where((lane < QUART) & (key + QUART > row), NEG, 0.0)
    lm_p[...] = jnp.zeros((ROWS, HD), F32)
    lm_r[...] = jnp.zeros((ROWS, HD), F32)

    def heads(i, carry):
        at = [2 * i, 2 * i + 1]
        qp = [load_head(q_other, q_own, is_r, a) for a in at]
        qr = [load_head(q_own, q_other, is_r, a) for a in at]
        sr = [start(), start()]
        sp = [start(), start()]
        for u in range(2):
            sr[u] = fold(sr[u], qr[u], kr[0:CHUNK, :], vr[0:CHUNK, :], left=first)
        for u in range(2):
            sp[u] = fold(sp[u], qp[u], kp[0:3 * HALF, :], vp[0:3 * HALF, :], left=own)
        for u in range(2):
            sr[u] = fold(sr[u], qr[u], kr[CHUNK:, :], vr[CHUNK:, :], left=second)
        for u in range(2):
            sp[u] = fold(sp[u], qp[u], kp[3 * HALF:, :], vp[3 * HALF:, :], right=edge)
        for u in range(2):
            store_state(acc_p, lm_p, at[u], sp[u])
            store_state(acc_r, lm_r, at[u], sr[u])
        return carry

    lax.fori_loop(0, GROUP // 2, heads, 0)


def middle_kernel(sc, q_own, q_other, x1, x3, y1, y3, acc_in, lm_in, acc_r, lm_r, kr, vr):
    is_r = sc[5]
    put_first(kr, vr, 0, x1)
    put_first(kr, vr, CHUNK, x3)
    put_second(kr, vr, 2 * CHUNK, y1)
    put_second(kr, vr, 3 * CHUNK, y3)
    put_bias(kr, vr, range_bias(sc, (4 * CHUNK, HD), ((1, None), (3, None), (None, 1), (None, 3))))
    lm_r[...] = jnp.zeros((ROWS, HD), F32)

    def heads(i, carry):
        at = [2 * i, 2 * i + 1]
        q = [load_head(q_own, q_other, is_r, a) for a in at]
        state = [load_state(acc_in, lm_in, a) for a in at]
        for n in range(4):
            rows = slice(n * CHUNK, (n + 1) * CHUNK)
            for u in range(2):
                state[u] = fold(state[u], q[u], kr[rows, :], vr[rows, :])
        for u in range(2):
            store_state(acc_r, lm_r, at[u], state[u])
        return carry

    lax.fori_loop(0, GROUP // 2, heads, 0)


def finish(state):
    m, l, o = state
    total = jnp.maximum(l, 1e-37)
    return o / total, m * SCALE + jnp.log2(total)


def last_kernel(sc, q_own, q_other, x2, y2, sink, acc_r, lm_r, acc_p, lm_p, keep, keep_lse, send, kr, vr, ks, vs):
    core, c, is_r = sc[3], sc[4], sc[5]
    put_first(kr, vr, 0, x2)
    put_second(kr, vr, CHUNK, y2)
    put_bias(kr, vr, range_bias(sc, (2 * CHUNK, HD), ((2, None), (None, 2))))
    ks[...] = jnp.zeros((HALF, 2 * HD), BF16)
    vs[...] = jnp.where(iota((HALF, 2 * HD), 1) >= HD, 1.0, 0.0).astype(BF16)
    put_keys(ks, vs, 0, sink, 0, SINK, SINK)
    row = iota((ROWS, HD), 0)
    lane = iota((ROWS, HD), 1)
    seen = (core == 0) & (lane < SINK) & (c * ROWS + row - lane >= RECENT)
    sink_bias = jnp.where(seen, 0.0, NEG)
    keep_lse[...] = jnp.zeros((ROWS, HD), F32)
    send[:, GROUP * HD:] = jnp.zeros((ROWS, HD), BF16)

    def heads(i, carry):
        at = [2 * i, 2 * i + 1]
        qp = [load_head(q_other, q_own, is_r, a) for a in at]
        qr = [load_head(q_own, q_other, is_r, a) for a in at]
        sr = [load_state(acc_r, lm_r, a) for a in at]
        sp = [load_state(acc_p, lm_p, a) for a in at]
        for n in range(2):
            rows = slice(n * CHUNK, (n + 1) * CHUNK)
            for u in range(2):
                sr[u] = fold(sr[u], qr[u], kr[rows, :], vr[rows, :])
        for u in range(2):
            sp[u] = fold(sp[u], qp[u], ks[...], vs[...], left=sink_bias)
        for u in range(2):
            cols = pl.ds(pl.multiple_of(at[u] * HD, HD), HD)
            out_r, lse_r = finish(sr[u])
            out_p, lse_p = finish(sp[u])
            keep[:, cols] = jnp.where(is_r == 1, out_r, out_p).astype(BF16)
            send[:, cols] = jnp.where(is_r == 1, out_p, out_r).astype(BF16)
            mine = jnp.where(is_r == 1, lse_r, lse_p)
            theirs = jnp.where(is_r == 1, lse_p, lse_r)
            keep_lse[...] = jnp.where(lane == at[u], mine, keep_lse[...])
            high = theirs.astype(BF16)
            rest = theirs - high.astype(F32)
            mid = rest.astype(BF16)
            low = (rest - mid.astype(F32)).astype(BF16)
            ext = send[:, GROUP * HD:].astype(F32)
            for n, part in enumerate((high, mid, low)):
                ext = jnp.where(lane == at[u] + n * GROUP, part.astype(F32), ext)
            send[:, GROUP * HD:] = ext.astype(BF16)
        return carry

    lax.fori_loop(0, GROUP // 2, heads, 0)


def merge_kernel(keep, keep_lse, got, out_ref):
    ext = got[:, GROUP * HD:].astype(F32)
    for a in range(GROUP):
        cols = slice(a * HD, (a + 1) * HD)
        l0 = keep_lse[:, a:a + 1]
        l1 = ext[:, a:a + 1] + ext[:, a + GROUP:a + GROUP + 1] + ext[:, a + 2 * GROUP:a + 2 * GROUP + 1]
        top = jnp.maximum(l0, l1)
        w0, w1 = jnp.exp2(l0 - top), jnp.exp2(l1 - top)
        scale = 1.0 / (w0 + w1)
        out = keep[:, cols].astype(F32) * (w0 * scale) + got[:, cols].astype(F32) * (w1 * scale)
        out_ref[:, cols] = out.astype(BF16)


def pages_kernel(sc, a0, a1, a2, a3, b0, b1, b2, b3, out_ref):
    x, y, z, c = sc[0], sc[1], sc[2], sc[4]
    first = (a0, a1, a2, a3)
    second = (b0, b1, b2, b3)
    row = iota((2 * PAGE, HD), 0)
    lane = iota((2 * PAGE, HD), 1)
    same_row = (lane & (PAGE - 1)) == (row & (PAGE - 1))
    want = (2 * c + (row >> 4)).astype(F32)
    for dx in range(4):
        for d in range(4):
            for col in range(2):
                f, at = first[dx], (d * 2 + col) * FIRST
                s, on = second[d], (dx * 2 + col) * 2 * QUART
                code = jnp.concatenate([f[at + 2 * QUART:at + FIRST, :]] * 2, axis=0).astype(F32)
                select = jnp.where(same_row & (code == want), 1.0, 0.0).astype(BF16)
                zz = z if col == 0 else 1 - z
                block = ((x - dx) & 3) * 8 + zz * 4 + ((y - d) & 3)
                for part in range(2):
                    k1 = f[at + part * QUART:at + (part + 1) * QUART, :]
                    k2 = s[on + part * QUART:on + (part + 1) * QUART, :]
                    pages = jnp.dot(select, jnp.concatenate([k1, k2], axis=0), preferred_element_type=F32)
                    out_ref[block, :, part * HD:(part + 1) * HD] = pages.astype(BF16)


VMEM_SPEC = pl.BlockSpec(memory_space=pltpu.VMEM)
SMEM_SPEC = pl.BlockSpec(memory_space=pltpu.SMEM)


def call(kernel, out_shape, scratch, flops, sc, *args):
    many = isinstance(out_shape, tuple)
    specs = ([SMEM_SPEC] if sc is not None else []) + [VMEM_SPEC] * len(args)
    operands = ([sc] if sc is not None else []) + list(args)
    return pl.pallas_call(
        kernel,
        out_shape=out_shape,
        in_specs=specs,
        out_specs=(VMEM_SPEC,) * len(out_shape) if many else VMEM_SPEC,
        scratch_shapes=scratch,
        compiler_params=pltpu.CompilerParams(vmem_limit_bytes=24 * 1024 * 1024),
        cost_estimate=pl.CostEstimate(flops=flops, bytes_accessed=4 << 20, transcendentals=flops // 512),
    )(*operands)


def keys(rows):
    return [pltpu.VMEM((rows, 2 * HD), BF16), pltpu.VMEM((rows, 2 * HD), BF16)]


def shards(q, k, v, head_kind, page_owner):
    c = lax.axis_index("ctx")
    tp = lax.axis_index("tp")
    x, z, y = c // 8, (c // 4) % 2, c % 4
    core = tp % 2
    is_r = lax.dynamic_index_in_dim(head_kind, tp, 0, keepdims=False) == 1
    sc = jnp.stack([x, y, z, core, c, is_r.astype(jnp.int32), tp, tp]).astype(jnp.int32)

    def half(which):
        return jnp.concatenate([lax.dynamic_slice_in_dim(t, which * HALF, HALF, 0) for t in (k, v)])

    stay = half(core)
    came = lax.ppermute(half(1 - core), "tp", CORE_SWAP)
    q_other = lax.ppermute(q, "tp", CORE_SWAP)
    ret = jnp.where(is_r, stay, came)
    pas = jnp.where(is_r, came, stay)

    earlier = lax.iota(jnp.int32, 16)[None, :] < lax.iota(jnp.int32, 16)[:, None]
    rank = jnp.sum(((page_owner[:, None] == page_owner[None, :]) & earlier).astype(jnp.int32), axis=1)
    code = lax.dynamic_slice_in_dim(page_owner * 2 + rank, core * 8, 8, 0).astype(BF16)
    meta = jnp.broadcast_to(jnp.repeat(code, PAGE)[None, :], (META, HD))

    r1 = jnp.concatenate([ret[:QUART], ret[HALF:HALF + QUART], meta])
    r2 = jnp.concatenate([ret[QUART:HALF], ret[HALF + QUART:]])
    theirs = lax.ppermute(jnp.concatenate([r1, r2]), "ctx", Z_SWAP)
    far = lax.ppermute(pas, "ctx", FOUR_ON)
    r1 = jnp.concatenate([r1, theirs[:FIRST]])
    r2 = jnp.concatenate([r2, theirs[FIRST:]])
    low = jnp.where(z == 0, pas, far)
    sink = jnp.concatenate([low[:SINK], low[HALF:HALF + SINK]])

    ys = {s: lax.ppermute(jnp.concatenate([r1, jnp.where(y + s < 4, pas, far)]), "ctx", Y_SHIFT[s]) for s in (1, 3, 2)}
    along_x = jnp.concatenate([r2, sink])
    xs = {s: lax.ppermute(along_x, "ctx", X_SHIFT[s]) for s in (1, 3, 2)}
    h1 = jnp.concatenate([r1] + [ys[s][:2 * FIRST] for s in (1, 2, 3)])
    for s in (1, 2, 3):
        sink = jnp.where(x == s, xs[s][2 * HALF:], sink)
    h2 = jnp.concatenate([r2] + [xs[s][:2 * HALF] for s in (1, 2, 3)] + [sink])

    a = {0: h1} | {s: lax.ppermute(h1, "ctx", X_SHIFT[s]) for s in (1, 3, 2)}
    b = {0: h2} | {s: lax.ppermute(h2, "ctx", Y_SHIFT[s]) for s in (1, 3, 2)}

    acc_shape = jax.ShapeDtypeStruct((GROUP, ROWS, HD), F32)
    lm_shape = jax.ShapeDtypeStruct((ROWS, HD), F32)
    unit = 2 * 2048 * 256 * 512
    acc_p, lm_p, acc_r, lm_r = call(
        near_kernel, (acc_shape, lm_shape, acc_shape, lm_shape), keys(5 * HALF) + keys(2 * CHUNK),
        7 * unit, sc, q, q_other, pas, ys[1], ys[2], ys[3], far, h1, h2)
    acc_r, lm_r = call(
        middle_kernel, (acc_shape, lm_shape), keys(4 * CHUNK),
        8 * unit, sc, q, q_other, a[1], a[3], b[1], b[3], acc_r, lm_r)
    for s in (1, 2, 3):
        sink = jnp.where(y == s, b[s][8 * HALF:], sink)
    keep, keep_lse, send = call(
        last_kernel,
        (jax.ShapeDtypeStruct((ROWS, GROUP * HD), BF16), lm_shape, jax.ShapeDtypeStruct((ROWS, (GROUP + 1) * HD), BF16)),
        keys(2 * CHUNK) + keys(HALF), 4 * unit, sc, q, q_other, a[2], b[2], sink, acc_r, lm_r, acc_p, lm_p)

    got = lax.ppermute(send, "tp", CORE_SWAP)
    pages = call(pages_kernel, jax.ShapeDtypeStruct((32, 2 * PAGE, 2 * HD), BF16), [], unit, sc, *[a[s] for s in range(4)], *[b[s] for s in range(4)])
    got_pages = lax.ppermute(pages, "tp", CORE_SWAP)
    attn_out = call(merge_kernel, jax.ShapeDtypeStruct((ROWS, GROUP * HD), BF16), [], unit, None, keep, keep_lse, got)
    decode_cache = jnp.where(is_r, pages + got_pages, jnp.zeros((), BF16)).reshape(64, PAGE, 2 * HD)
    return attn_out, decode_cache


def solution(mesh):
    return jax.shard_map(
        shards,
        mesh=mesh,
        in_specs=(P("ctx", "tp"), P("ctx", "tp"), P("ctx", "tp"), P(), P("ctx")),
        out_specs=(P("ctx", "tp"), P("ctx", None, "tp")),
        check_vma=False,
    )
```

```python
import math

import jax
import jax.numpy as jnp
from jax import lax
from jax.experimental import pallas as pl
from jax.experimental.pallas import tpu as pltpu
from jax.sharding import PartitionSpec as P

GROUP = 8
HD = 128
SINK = 64
RECENT = 1024
PAGE = 16
ROWS = 256
HALF = 128
QUART = 64
META = 16
FIRST = 2 * QUART + META
CHUNK = 512
WIDE = 2
PASSED = 8 * 2 * QUART + 2 * SINK
NEG = -1e30
SCALE = math.log2(math.e) / math.sqrt(HD)
F32 = jnp.float32
BF16 = jnp.bfloat16


def ctx_of(x, z, y):
    return (x % 4) * 8 + (z % 2) * 4 + (y % 4)


CHIPS = [(x, z, y) for x in range(4) for z in range(2) for y in range(4)]
CORE_SWAP = [(i, i ^ 1) for i in range(8)]
Z_SWAP = [(ctx_of(x, z, y), ctx_of(x, z + 1, y)) for x, z, y in CHIPS]
FOUR_ON = [(i, i + 4) for i in range(28)]
X_SHIFT = {s: [(ctx_of(x, z, y), ctx_of(x + s, z, y)) for x, z, y in CHIPS] for s in (1, 2, 3)}
Y_SHIFT = {s: [(ctx_of(x, z, y), ctx_of(x, z, y + s)) for x, z, y in CHIPS] for s in (1, 2, 3)}


def nt_dot(a, b):
    return lax.dot_general(a, b, (((1,), (1,)), ((), ())), preferred_element_type=F32)


def iota(shape, axis):
    return lax.broadcasted_iota(jnp.int32, shape, axis)


def fold(state, q, k, v, left=None, right=None):
    s = nt_dot(q, k)
    if left is not None:
        s = jnp.concatenate([s[:, :HD] + left, s[:, HD:]], axis=1) if s.shape[1] > HD else s + left
    if right is not None:
        s = jnp.concatenate([s[:, :-HD], s[:, -HD:] + right], axis=1)
    high = jnp.max(s, axis=1, keepdims=True)
    top = jnp.broadcast_to(high, (ROWS, HD)) if state is None else jnp.maximum(state[0], high)
    p = jnp.exp2((s - jnp.concatenate([top] * (s.shape[1] // HD), axis=1)) * SCALE).astype(BF16)
    up = jnp.dot(p, v, preferred_element_type=F32)
    if state is None:
        return top, up[:, HD:], up[:, :HD]
    keep = jnp.exp2((state[0] - top) * SCALE)
    return top, state[1] * keep + up[:, HD:], state[2] * keep + up[:, :HD]


def put_keys(k_s, v_s, at, ref, first, rows, gap):
    k_s[pl.ds(at, rows), 0:HD] = ref[first:first + rows, :]
    v_s[pl.ds(at, rows), 0:HD] = ref[first + gap:first + gap + rows, :]


def put_first(k_s, v_s, at, ref):
    for n in range(8):
        put_keys(k_s, v_s, at + n * QUART, ref, n * FIRST, QUART, QUART)


def put_second(k_s, v_s, at, ref):
    for n in range(8):
        put_keys(k_s, v_s, at + n * QUART, ref, n * 2 * QUART, QUART, QUART)


def put_bias(k_s, v_s, bias):
    lane = iota(bias.shape, 1)
    k_s[:, HD:] = jnp.where(lane == 0, bias, 0.0).astype(BF16)
    v_s[:, HD:] = jnp.ones(bias.shape, BF16)


def range_bias(sc, shape, chunks):
    x, y, z, c = sc[0], sc[1], sc[2], sc[4]
    n = iota(shape, 0)
    outer, far = (n >> 7) & 3, (n >> 6) & 1
    which = n >> 9
    dx, dy = outer, outer
    for i, (fixed_x, fixed_y) in enumerate(chunks):
        if fixed_x is not None:
            dx = jnp.where(which == i, fixed_x, dx)
        else:
            dy = jnp.where(which == i, fixed_y, dy)
    zz = jnp.where(far == 0, z, 1 - z)
    block = ((x - dx) & 3) * 8 + zz * 4 + ((y - dy) & 3)
    return jnp.where(block <= c, 0.0, NEG)


def load_head(q_a, q_b, flag, a):
    cols = slice(a * HD, (a + 1) * HD)
    q = jnp.where(flag == 1, q_a[:, cols], q_b[:, cols])
    one = jnp.where(iota((ROWS, HD), 1) == 0, 1.0, 0.0).astype(BF16)
    return jnp.concatenate([q, one], axis=1)


def near_kernel(sc, q_own, q_other, h1, h2, m_out, l_out, o_out, kr, vr):
    core, is_r = sc[3], sc[5]
    put_first(kr, vr, 0, h1)
    put_second(kr, vr, CHUNK, h2)
    put_bias(kr, vr, range_bias(sc, (2 * CHUNK, HD), ((0, None), (None, 0))))
    row = iota((ROWS, HD), 0)
    lane = iota((ROWS, HD), 1)
    key = core * HALF + lane
    first = jnp.where((lane < QUART) & (key > row), NEG, 0.0)
    second = jnp.where((lane < QUART) & (key + QUART > row), NEG, 0.0)

    def heads(i):
        at = [WIDE * i + u for u in range(WIDE)]
        q = [load_head(q_own, q_other, is_r, a) for a in at]
        state = [fold(None, q[u], kr[0:CHUNK, :], vr[0:CHUNK, :], left=first) for u in range(WIDE)]
        state = [fold(state[u], q[u], kr[CHUNK:, :], vr[CHUNK:, :], left=second) for u in range(WIDE)]
        for u in range(WIDE):
            m_out[at[u]], l_out[at[u]], o_out[at[u]] = state[u]

    for i in range(GROUP // WIDE):
        heads(i)


def middle_kernel(sc, q_own, q_other, x1, x3, y1, y3, m_in, l_in, o_in, m_out, l_out, o_out, kr, vr):
    is_r = sc[5]
    put_first(kr, vr, 0, x1)
    put_first(kr, vr, CHUNK, x3)
    put_second(kr, vr, 2 * CHUNK, y1)
    put_second(kr, vr, 3 * CHUNK, y3)
    put_bias(kr, vr, range_bias(sc, (4 * CHUNK, HD), ((1, None), (3, None), (None, 1), (None, 3))))

    def heads(i):
        at = [WIDE * i + u for u in range(WIDE)]
        q = [load_head(q_own, q_other, is_r, a) for a in at]
        state = [(m_in[a], l_in[a], o_in[a]) for a in at]
        for n in range(4):
            rows = slice(n * CHUNK, (n + 1) * CHUNK)
            state = [fold(state[u], q[u], kr[rows, :], vr[rows, :]) for u in range(WIDE)]
        for u in range(WIDE):
            m_out[at[u]], l_out[at[u]], o_out[at[u]] = state[u]

    for i in range(GROUP // WIDE):
        heads(i)


def finish(state):
    m, l, o = state
    return o / l, m * SCALE + jnp.log2(l)


def last_kernel(sc, q_own, q_other, x2, y1, y2, y3, pas, far, sink, m_in, l_in, o_in, keep, keep_lse, send,
                kr, vr, kp, vp, lse_s):
    core, c, is_r = sc[3], sc[4], sc[5]
    put_first(kr, vr, 0, x2)
    put_second(kr, vr, CHUNK, y2)
    put_bias(kr, vr, range_bias(sc, (2 * CHUNK, HD), ((2, None), (None, 2))))
    put_keys(kp, vp, 0, pas, 0, HALF, HALF)
    for n, ref in enumerate((y1, y2, y3)):
        put_keys(kp, vp, (n + 1) * HALF, ref, PASSED, HALF, HALF)
    kp[4 * HALF:5 * HALF, :] = jnp.zeros((HALF, 2 * HD), BF16)
    vp[4 * HALF:5 * HALF, :] = jnp.zeros((HALF, 2 * HD), BF16)
    put_keys(kp, vp, 4 * HALF, sink, 0, SINK, SINK)
    put_keys(kp, vp, 5 * HALF, far, 0, HALF, HALF)
    slot = iota((6 * HALF, HD), 0) >> 7
    put_bias(kp, vp, jnp.where((slot - (slot >> 2) <= c) | (slot == 4), 0.0, NEG))
    row = iota((ROWS, HD), 0)
    lane = iota((ROWS, HD), 1)
    key = core * HALF + lane
    own = jnp.where(key > row, NEG, 0.0)
    edge = jnp.where(key <= row, NEG, 0.0)
    seen = (core == 0) & (lane < SINK) & (c * ROWS + row - lane >= RECENT)
    sink_bias = jnp.where(seen, 0.0, NEG)
    lse_s[...] = jnp.zeros((ROWS, HD), F32)
    keep_lse[...] = jnp.zeros((ROWS, HD), F32)

    def heads(i):
        at = [WIDE * i + u for u in range(WIDE)]
        qp = [load_head(q_other, q_own, is_r, a) for a in at]
        qr = [load_head(q_own, q_other, is_r, a) for a in at]
        sr = [(m_in[a], l_in[a], o_in[a]) for a in at]
        sr = [fold(sr[u], qr[u], kr[0:CHUNK, :], vr[0:CHUNK, :]) for u in range(WIDE)]
        sp = [fold(None, qp[u], kp[0:4 * HALF, :], vp[0:4 * HALF, :], left=own) for u in range(WIDE)]
        sr = [fold(sr[u], qr[u], kr[CHUNK:, :], vr[CHUNK:, :]) for u in range(WIDE)]
        sp = [fold(sp[u], qp[u], kp[4 * HALF:, :], vp[4 * HALF:, :], left=sink_bias, right=edge) for u in range(WIDE)]
        for u in range(WIDE):
            cols = slice(at[u] * HD, (at[u] + 1) * HD)
            out_r, lse_r = finish(sr[u])
            out_p, lse_p = finish(sp[u])
            keep[:, cols] = jnp.where(is_r == 1, out_r, out_p).astype(BF16)
            send[:, cols] = jnp.where(is_r == 1, out_p, out_r).astype(BF16)
            keep_lse[...] = jnp.where(lane == at[u], jnp.where(is_r == 1, lse_r, lse_p), keep_lse[...])
            lse_s[...] = jnp.where(lane == at[u], jnp.where(is_r == 1, lse_p, lse_r), lse_s[...])

    for i in range(GROUP // WIDE):
        heads(i)
    lse = lse_s[...]
    high = lse.astype(BF16).astype(F32)
    mid = (lse - high).astype(BF16).astype(F32)
    low = lse - high - mid
    parts = high + pltpu.roll(mid, GROUP, 1) + pltpu.roll(low, 2 * GROUP, 1)
    send[:, GROUP * HD:] = parts.astype(BF16)


def merge_kernel(keep, keep_lse, got, out_ref):
    ext = got[:, GROUP * HD:].astype(F32)
    lse = ext + pltpu.roll(ext, HD - GROUP, 1) + pltpu.roll(ext, HD - 2 * GROUP, 1)
    lane = iota((ROWS, HD), 1)
    gap = jnp.where(lane < GROUP, lse - keep_lse[...], 0.0)
    weight = 1.0 / (1.0 + jnp.exp2(jnp.clip(gap, -126.0, 126.0)))
    for a in range(GROUP):
        cols = slice(a * HD, (a + 1) * HD)
        w = weight[:, a:a + 1]
        mine, theirs = keep[:, cols].astype(F32), got[:, cols].astype(F32)
        out_ref[:, cols] = (theirs + w * (mine - theirs)).astype(BF16)


def pages_kernel(sc, a0, a1, a2, a3, b0, b1, b2, b3, out_ref):
    x, y, z, c = sc[0], sc[1], sc[2], sc[4]
    first = (a0, a1, a2, a3)
    second = (b0, b1, b2, b3)
    row = iota((2 * PAGE, HD), 0)
    lane = iota((2 * PAGE, HD), 1)
    same_row = (lane & (PAGE - 1)) == (row & (PAGE - 1))
    want = (2 * c + (row >> 4)).astype(F32)
    for dx in range(4):
        for d in range(4):
            for col in range(2):
                f, at = first[dx], (d * 2 + col) * FIRST
                s, on = second[d], (dx * 2 + col) * 2 * QUART
                code = jnp.concatenate([f[at + 2 * QUART:at + FIRST, :]] * 2, axis=0).astype(F32)
                select = jnp.where(same_row & (code == want), 1.0, 0.0).astype(BF16)
                zz = z if col == 0 else 1 - z
                block = ((x - dx) & 3) * 8 + zz * 4 + ((y - d) & 3)
                for part in range(2):
                    k1 = f[at + part * QUART:at + (part + 1) * QUART, :]
                    k2 = s[on + part * QUART:on + (part + 1) * QUART, :]
                    pages = jnp.dot(select, jnp.concatenate([k1, k2], axis=0), preferred_element_type=F32)
                    out_ref[block, :, part * HD:(part + 1) * HD] = pages.astype(BF16)


VMEM_SPEC = pl.BlockSpec(memory_space=pltpu.VMEM)
SMEM_SPEC = pl.BlockSpec(memory_space=pltpu.SMEM)


def call(kernel, out_shape, scratch, flops, sc, *args):
    many = isinstance(out_shape, tuple)
    specs = ([SMEM_SPEC] if sc is not None else []) + [VMEM_SPEC] * len(args)
    operands = ([sc] if sc is not None else []) + list(args)
    return pl.pallas_call(
        kernel,
        out_shape=out_shape,
        in_specs=specs,
        out_specs=(VMEM_SPEC,) * len(out_shape) if many else VMEM_SPEC,
        scratch_shapes=scratch,
        compiler_params=pltpu.CompilerParams(vmem_limit_bytes=24 * 1024 * 1024),
        cost_estimate=pl.CostEstimate(flops=flops, bytes_accessed=4 << 20, transcendentals=flops // 512),
    )(*operands)


def keys(rows):
    return [pltpu.VMEM((rows, 2 * HD), BF16), pltpu.VMEM((rows, 2 * HD), BF16)]


def shards(q, k, v, head_kind, page_owner):
    c = lax.axis_index("ctx")
    tp = lax.axis_index("tp")
    x, z, y = c // 8, (c // 4) % 2, c % 4
    core = tp % 2
    is_r = lax.dynamic_index_in_dim(head_kind, tp, 0, keepdims=False) == 1
    sc = jnp.stack([x, y, z, core, c, is_r.astype(jnp.int32), tp, tp]).astype(jnp.int32)

    low = jnp.concatenate([k[:HALF], v[:HALF]])
    high = jnp.concatenate([k[HALF:], v[HALF:]])
    stay = jnp.where(core == 0, low, high)
    came = lax.ppermute(jnp.where(core == 0, high, low), "tp", CORE_SWAP)
    q_other = lax.ppermute(q, "tp", CORE_SWAP)
    ret = jnp.where(is_r, stay, came)
    pas = jnp.where(is_r, came, stay)

    earlier = lax.iota(jnp.int32, 16)[None, :] < lax.iota(jnp.int32, 16)[:, None]
    rank = jnp.sum(((page_owner[:, None] == page_owner[None, :]) & earlier).astype(jnp.int32), axis=1)
    code = page_owner * 2 + rank
    code = jnp.where(core == 0, code[:8], code[8:]).astype(BF16)
    meta = jnp.broadcast_to(jnp.repeat(code, PAGE)[None, :], (META, HD))

    r1 = jnp.concatenate([ret[:QUART], ret[HALF:HALF + QUART], meta])
    r2 = jnp.concatenate([ret[QUART:HALF], ret[HALF + QUART:]])
    sink = jnp.concatenate([pas[:SINK], pas[HALF:HALF + SINK]])
    theirs = lax.ppermute(jnp.concatenate([r1, r2, sink]), "ctx", Z_SWAP)
    theirs, q_other = lax.optimization_barrier((theirs, q_other))
    far = lax.ppermute(pas, "ctx", FOUR_ON)
    r1 = jnp.concatenate([r1, theirs[:FIRST]])
    r2 = jnp.concatenate([r2, theirs[FIRST:FIRST + HALF]])
    sink = jnp.where(z == 0, sink, theirs[FIRST + HALF:])

    along_x = jnp.concatenate([r2, sink])
    ys = {s: lax.ppermute(r1, "ctx", Y_SHIFT[s]) for s in (1, 3)}
    xs = {s: lax.ppermute(along_x, "ctx", X_SHIFT[s]) for s in (1, 3)}
    r1_late, x_late, far = lax.optimization_barrier((r1, along_x, far))
    ys[2] = lax.ppermute(r1_late, "ctx", Y_SHIFT[2])
    xs[2] = lax.ppermute(x_late, "ctx", X_SHIFT[2])
    h1 = jnp.concatenate([r1] + [ys[s] for s in (1, 2, 3)])
    for s in (1, 2, 3):
        sink = jnp.where(x == s, xs[s][2 * HALF:], sink)
    h2 = jnp.concatenate([r2] + [xs[s][:2 * HALF] for s in (1, 2, 3)] + [sink])

    a = {0: h1} | {s: lax.ppermute(h1, "ctx", X_SHIFT[s]) for s in (1, 3, 2)}
    b = {0: h2} | {
        s: lax.ppermute(jnp.concatenate([h2, jnp.where(y + s < 4, pas, far)]), "ctx", Y_SHIFT[s]) for s in (1, 3, 2)
    }

    state = (jax.ShapeDtypeStruct((GROUP, ROWS, HD), F32),) * 3
    unit = 2 * 2048 * 256 * 512
    now = call(near_kernel, state, keys(2 * CHUNK), 4 * unit, sc, q, q_other, h1, h2)
    now = call(middle_kernel, state, keys(4 * CHUNK), 8 * unit, sc, q, q_other, a[1], a[3], b[1], b[3], *now)
    for s in (1, 2, 3):
        sink = jnp.where(y == s, b[s][8 * HALF:8 * HALF + 2 * SINK], sink)
    keep, keep_lse, send = call(
        last_kernel,
        (
            jax.ShapeDtypeStruct((ROWS, GROUP * HD), BF16),
            jax.ShapeDtypeStruct((ROWS, HD), F32),
            jax.ShapeDtypeStruct((ROWS, (GROUP + 1) * HD), BF16),
        ),
        keys(2 * CHUNK) + keys(6 * HALF) + [pltpu.VMEM((ROWS, HD), F32)],
        7 * unit, sc, q, q_other, a[2], b[1], b[2], b[3], pas, far, sink, *now)

    got = lax.ppermute(send, "tp", CORE_SWAP)
    sc, _ = lax.optimization_barrier((sc, send))
    pages = call(
        pages_kernel, jax.ShapeDtypeStruct((32, 2 * PAGE, 2 * HD), BF16), [], unit // 4,
        sc, *[a[s] for s in range(4)], *[b[s] for s in range(4)])
    got_pages = lax.ppermute(pages, "tp", CORE_SWAP)
    attn_out = call(
        merge_kernel, jax.ShapeDtypeStruct((ROWS, GROUP * HD), BF16), [], unit // 4, None, keep, keep_lse, got)
    decode_cache = jnp.where(is_r, pages + got_pages, jnp.zeros((), BF16)).reshape(64, PAGE, 2 * HD)
    return attn_out, decode_cache


def solution(mesh):
    return jax.shard_map(
        shards,
        mesh=mesh,
        in_specs=(P("ctx", "tp"), P("ctx", "tp"), P("ctx", "tp"), P(), P("ctx")),
        out_specs=(P("ctx", "tp"), P("ctx", None, "tp")),
        check_vma=False,
    )
```

```python
import math

import jax
import jax.numpy as jnp
from jax import lax
from jax.experimental import pallas as pl
from jax.experimental.pallas import tpu as pltpu
from jax.sharding import PartitionSpec as P

GROUP = 8
HD = 128
SINK = 64
RECENT = 1024
PAGE = 16
ROWS = 256
HALF = 128
QUART = 64
META = 16
PAIR = 2 * QUART
CHUNK = 512
WIDE = 2
PASSED = 2 * PAIR + META
NEG = -1e30
SCALE = math.log2(math.e) / math.sqrt(HD)
F32 = jnp.float32
BF16 = jnp.bfloat16


def ctx_of(x, z, y):
    return (x % 4) * 8 + (z % 2) * 4 + (y % 4)


CHIPS = [(x, z, y) for x in range(4) for z in range(2) for y in range(4)]
CORE_SWAP = [(i, i ^ 1) for i in range(8)]
Z_SWAP = [(ctx_of(x, z, y), ctx_of(x, z + 1, y)) for x, z, y in CHIPS]
FOUR_ON = [(i, i + 4) for i in range(28)]
X_SHIFT = {s: [(ctx_of(x, z, y), ctx_of(x + s, z, y)) for x, z, y in CHIPS] for s in (1, 2, 3)}
Y_SHIFT = {s: [(ctx_of(x, z, y), ctx_of(x, z, y + s)) for x, z, y in CHIPS] for s in (1, 2, 3)}


def nt_dot(a, b):
    return lax.dot_general(a, b, (((1,), (1,)), ((), ())), preferred_element_type=F32)


def iota(shape, axis):
    return lax.broadcasted_iota(jnp.int32, shape, axis)


def fold(state, q, k, v, left=None, right=None):
    s = nt_dot(q, k)
    if left is not None:
        s = jnp.concatenate([s[:, :HD] + left, s[:, HD:]], axis=1) if s.shape[1] > HD else s + left
    if right is not None:
        s = jnp.concatenate([s[:, :-HD], s[:, -HD:] + right], axis=1)
    high = jnp.max(s, axis=1, keepdims=True)
    top = jnp.broadcast_to(high, (ROWS, HD)) if state is None else jnp.maximum(state[0], high)
    p = jnp.exp2((s - jnp.concatenate([top] * (s.shape[1] // HD), axis=1)) * SCALE).astype(BF16)
    up = jnp.dot(p, v, preferred_element_type=F32)
    if state is None:
        return top, up[:, HD:], up[:, :HD]
    keep = jnp.exp2((state[0] - top) * SCALE)
    return top, state[1] * keep + up[:, HD:], state[2] * keep + up[:, :HD]


def put_keys(k_s, v_s, at, ref, first, rows, gap):
    k_s[pl.ds(at, rows), 0:HD] = ref[first:first + rows, :]
    v_s[pl.ds(at, rows), 0:HD] = ref[first + gap:first + gap + rows, :]


def put_ranges(k_s, v_s, at, ref):
    for n in range(8):
        put_keys(k_s, v_s, at + n * QUART, ref, n * PAIR, QUART, QUART)


def put_bias(k_s, v_s, bias):
    lane = iota(bias.shape, 1)
    k_s[:, HD:] = jnp.where(lane == 0, bias, 0.0).astype(BF16)
    v_s[:, HD:] = jnp.ones(bias.shape, BF16)


def range_bias(sc, shape, chunks):
    x, y, z, c = sc[0], sc[1], sc[2], sc[4]
    n = iota(shape, 0)
    outer, far = (n >> 7) & 3, (n >> 6) & 1
    which = n >> 9
    dx, dy = outer, outer
    for i, (fixed_x, fixed_y) in enumerate(chunks):
        if fixed_x is not None:
            dx = jnp.where(which == i, fixed_x, dx)
        else:
            dy = jnp.where(which == i, fixed_y, dy)
    zz = jnp.where(far == 0, z, 1 - z)
    block = ((x - dx) & 3) * 8 + zz * 4 + ((y - dy) & 3)
    return jnp.where(block <= c, 0.0, NEG)


def load_head(q_a, q_b, flag, a):
    cols = slice(a * HD, (a + 1) * HD)
    q = jnp.where(flag == 1, q_a[:, cols], q_b[:, cols])
    one = jnp.where(iota((ROWS, HD), 1) == 0, 1.0, 0.0).astype(BF16)
    return jnp.concatenate([q, one], axis=1)


def near_kernel(sc, q_own, q_other, pas, y1, y2, y3, far, h1, h2, mp_out, lp_out, op_out, m_out, l_out, o_out,
                kp, vp, kr, vr):
    core, c, is_r = sc[3], sc[4], sc[5]
    put_keys(kp, vp, 0, pas, 0, HALF, HALF)
    for n, ref in enumerate((y1, y2, y3)):
        put_keys(kp, vp, (n + 1) * HALF, ref, PASSED, HALF, HALF)
    put_keys(kp, vp, 4 * HALF, far, 0, HALF, HALF)
    put_bias(kp, vp, jnp.where((iota((5 * HALF, HD), 0) >> 7) <= c, 0.0, NEG))
    put_ranges(kr, vr, 0, h1)
    put_ranges(kr, vr, CHUNK, h2)
    put_bias(kr, vr, range_bias(sc, (2 * CHUNK, HD), ((0, None), (None, 0))))
    row = iota((ROWS, HD), 0)
    lane = iota((ROWS, HD), 1)
    key = core * HALF + lane
    own = jnp.where(key > row, NEG, 0.0)
    edge = jnp.where(key <= row, NEG, 0.0)
    first = jnp.where((lane < QUART) & (key > row), NEG, 0.0)
    second = jnp.where((lane < QUART) & (key + QUART > row), NEG, 0.0)

    def heads(i):
        at = [WIDE * i + u for u in range(WIDE)]
        qp = [load_head(q_other, q_own, is_r, a) for a in at]
        q = [load_head(q_own, q_other, is_r, a) for a in at]
        sr = [fold(None, q[u], kr[0:CHUNK, :], vr[0:CHUNK, :], left=first) for u in range(WIDE)]
        sp = [fold(None, qp[u], kp[0:3 * HALF, :], vp[0:3 * HALF, :], left=own) for u in range(WIDE)]
        sr = [fold(sr[u], q[u], kr[CHUNK:, :], vr[CHUNK:, :], left=second) for u in range(WIDE)]
        sp = [fold(sp[u], qp[u], kp[3 * HALF:, :], vp[3 * HALF:, :], right=edge) for u in range(WIDE)]
        for u in range(WIDE):
            m_out[at[u]], l_out[at[u]], o_out[at[u]] = sr[u]
            mp_out[at[u]], lp_out[at[u]], op_out[at[u]] = sp[u]

    for i in range(GROUP // WIDE):
        heads(i)


def middle_kernel(sc, q_own, q_other, x1, x3, y1, y3, m_in, l_in, o_in, m_out, l_out, o_out, kr, vr):
    is_r = sc[5]
    put_ranges(kr, vr, 0, x1)
    put_ranges(kr, vr, CHUNK, x3)
    put_ranges(kr, vr, 2 * CHUNK, y1)
    put_ranges(kr, vr, 3 * CHUNK, y3)
    put_bias(kr, vr, range_bias(sc, (4 * CHUNK, HD), ((1, None), (3, None), (None, 1), (None, 3))))

    def heads(i):
        at = [WIDE * i + u for u in range(WIDE)]
        q = [load_head(q_own, q_other, is_r, a) for a in at]
        state = [(m_in[a], l_in[a], o_in[a]) for a in at]
        for n in range(4):
            rows = slice(n * CHUNK, (n + 1) * CHUNK)
            state = [fold(state[u], q[u], kr[rows, :], vr[rows, :]) for u in range(WIDE)]
        for u in range(WIDE):
            m_out[at[u]], l_out[at[u]], o_out[at[u]] = state[u]

    for i in range(GROUP // WIDE):
        heads(i)


def finish(state):
    m, l, o = state
    return o / l, m * SCALE + jnp.log2(l)


def last_kernel(sc, q_own, q_other, x2, y2, sink, m_in, l_in, o_in, mp_in, lp_in, op_in, keep, keep_lse, send,
                kr, vr, ks, vs, lse_s):
    core, c, is_r = sc[3], sc[4], sc[5]
    put_ranges(kr, vr, 0, x2)
    put_ranges(kr, vr, CHUNK, y2)
    put_bias(kr, vr, range_bias(sc, (2 * CHUNK, HD), ((2, None), (None, 2))))
    ks[...] = jnp.zeros((HALF, 2 * HD), BF16)
    vs[...] = jnp.zeros((HALF, 2 * HD), BF16)
    put_keys(ks, vs, 0, sink, 0, SINK, SINK)
    put_bias(ks, vs, jnp.zeros((HALF, HD), F32))
    row = iota((ROWS, HD), 0)
    lane = iota((ROWS, HD), 1)
    seen = (core == 0) & (lane < SINK) & (c * ROWS + row - lane >= RECENT)
    sink_bias = jnp.where(seen, 0.0, NEG)
    lse_s[...] = jnp.zeros((ROWS, HD), F32)
    keep_lse[...] = jnp.zeros((ROWS, HD), F32)

    def heads(i):
        at = [WIDE * i + u for u in range(WIDE)]
        qp = [load_head(q_other, q_own, is_r, a) for a in at]
        qr = [load_head(q_own, q_other, is_r, a) for a in at]
        sr = [(m_in[a], l_in[a], o_in[a]) for a in at]
        sp = [(mp_in[a], lp_in[a], op_in[a]) for a in at]
        sr = [fold(sr[u], qr[u], kr[0:CHUNK, :], vr[0:CHUNK, :]) for u in range(WIDE)]
        sp = [fold(sp[u], qp[u], ks[...], vs[...], left=sink_bias) for u in range(WIDE)]
        sr = [fold(sr[u], qr[u], kr[CHUNK:, :], vr[CHUNK:, :]) for u in range(WIDE)]
        for u in range(WIDE):
            cols = slice(at[u] * HD, (at[u] + 1) * HD)
            out_r, lse_r = finish(sr[u])
            out_p, lse_p = finish(sp[u])
            keep[:, cols] = jnp.where(is_r == 1, out_r, out_p).astype(BF16)
            send[:, cols] = jnp.where(is_r == 1, out_p, out_r).astype(BF16)
            keep_lse[...] = jnp.where(lane == at[u], jnp.where(is_r == 1, lse_r, lse_p), keep_lse[...])
            lse_s[...] = jnp.where(lane == at[u], jnp.where(is_r == 1, lse_p, lse_r), lse_s[...])

    for i in range(GROUP // WIDE):
        heads(i)
    lse = lse_s[...]
    high = lse.astype(BF16).astype(F32)
    mid = (lse - high).astype(BF16).astype(F32)
    low = lse - high - mid
    parts = high + pltpu.roll(mid, GROUP, 1) + pltpu.roll(low, 2 * GROUP, 1)
    send[:, GROUP * HD:] = parts.astype(BF16)


def merge_kernel(keep, keep_lse, got, out_ref):
    ext = got[:, GROUP * HD:].astype(F32)
    lse = ext + pltpu.roll(ext, HD - GROUP, 1) + pltpu.roll(ext, HD - 2 * GROUP, 1)
    lane = iota((ROWS, HD), 1)
    gap = jnp.where(lane < GROUP, lse - keep_lse[...], 0.0)
    weight = 1.0 / (1.0 + jnp.exp2(jnp.clip(gap, -126.0, 126.0)))
    for a in range(GROUP):
        cols = slice(a * HD, (a + 1) * HD)
        w = weight[:, a:a + 1]
        mine, theirs = keep[:, cols].astype(F32), got[:, cols].astype(F32)
        out_ref[:, cols] = (theirs + w * (mine - theirs)).astype(BF16)


def pages_kernel(sc, a0, a1, a2, a3, b0, b1, b2, b3, out_ref):
    x, y, z, c = sc[0], sc[1], sc[2], sc[4]
    first = (a0, a1, a2, a3)
    second = (b0, b1, b2, b3)
    row = iota((2 * PAGE, HD), 0)
    lane = iota((2 * PAGE, HD), 1)
    same_row = (lane & (PAGE - 1)) == (row & (PAGE - 1))
    want = (2 * c + (row >> 4)).astype(F32)
    codes = [f[8 * PAIR:8 * PAIR + META, :].astype(F32) for f in first]
    for dx in range(4):
        for d in range(4):
            for col in range(2):
                n = d * 2 + col
                f, at = first[dx], n * PAIR
                s, on = second[d], (dx * 2 + col) * PAIR
                code = codes[dx][n:n + 1, :]
                select = jnp.where(same_row & (code == want), 1.0, 0.0).astype(BF16)
                zz = z if col == 0 else 1 - z
                block = ((x - dx) & 3) * 8 + zz * 4 + ((y - d) & 3)
                for part in range(2):
                    k1 = f[at + part * QUART:at + (part + 1) * QUART, :]
                    k2 = s[on + part * QUART:on + (part + 1) * QUART, :]
                    pages = jnp.dot(select, jnp.concatenate([k1, k2], axis=0), preferred_element_type=F32)
                    out_ref[block, :, part * HD:(part + 1) * HD] = pages.astype(BF16)


VMEM_SPEC = pl.BlockSpec(memory_space=pltpu.VMEM)
SMEM_SPEC = pl.BlockSpec(memory_space=pltpu.SMEM)


def call(kernel, out_shape, scratch, flops, sc, *args):
    many = isinstance(out_shape, tuple)
    specs = ([SMEM_SPEC] if sc is not None else []) + [VMEM_SPEC] * len(args)
    operands = ([sc] if sc is not None else []) + list(args)
    return pl.pallas_call(
        kernel,
        out_shape=out_shape,
        in_specs=specs,
        out_specs=(VMEM_SPEC,) * len(out_shape) if many else VMEM_SPEC,
        scratch_shapes=scratch,
        compiler_params=pltpu.CompilerParams(vmem_limit_bytes=24 * 1024 * 1024),
        cost_estimate=pl.CostEstimate(flops=flops, bytes_accessed=4 << 20, transcendentals=flops // 512),
    )(*operands)


def keys(rows):
    return [pltpu.VMEM((rows, 2 * HD), BF16), pltpu.VMEM((rows, 2 * HD), BF16)]


def shards(q, k, v, head_kind, page_owner):
    c = lax.axis_index("ctx")
    tp = lax.axis_index("tp")
    x, z, y = c // 8, (c // 4) % 2, c % 4
    core = tp % 2
    is_r = lax.dynamic_index_in_dim(head_kind, tp, 0, keepdims=False) == 1
    sc = jnp.stack([x, y, z, core, c, is_r.astype(jnp.int32), tp, tp]).astype(jnp.int32)

    low = jnp.concatenate([k[:HALF], v[:HALF]])
    high = jnp.concatenate([k[HALF:], v[HALF:]])
    stay = jnp.where(core == 0, low, high)
    came = lax.ppermute(jnp.where(core == 0, high, low), "tp", CORE_SWAP)
    q_other = lax.ppermute(q, "tp", CORE_SWAP)
    ret = jnp.where(is_r, stay, came)
    pas = jnp.where(is_r, came, stay)

    earlier = lax.iota(jnp.int32, 16)[None, :] < lax.iota(jnp.int32, 16)[:, None]
    rank = jnp.sum(((page_owner[:, None] == page_owner[None, :]) & earlier).astype(jnp.int32), axis=1)
    code = page_owner * 2 + rank
    code = jnp.where(core == 0, code[:8], code[8:]).astype(BF16)
    meta = jnp.broadcast_to(jnp.repeat(code, PAGE)[None, :], (META, HD))

    r1 = jnp.concatenate([ret[:QUART], ret[HALF:HALF + QUART]])
    r2 = jnp.concatenate([ret[QUART:HALF], ret[HALF + QUART:]])
    sink = jnp.concatenate([pas[:SINK], pas[HALF:HALF + SINK]])
    mine = jnp.concatenate([r1, r2, sink, meta])
    theirs = lax.ppermute(mine, "ctx", Z_SWAP)
    theirs, q_other = lax.optimization_barrier((theirs, q_other))
    far = lax.ppermute(jnp.concatenate([pas, mine[-META:]]), "ctx", FOUR_ON)[:2 * HALF]
    r1 = jnp.concatenate([r1, theirs[:PAIR]])
    r2 = jnp.concatenate([r2, theirs[PAIR:2 * PAIR]])
    sink = jnp.where(z == 0, sink, theirs[2 * PAIR:2 * PAIR + 2 * SINK])
    line = iota((META, HD), 0)
    meta = jnp.where((line & 1) == 0, meta, theirs[2 * PAIR + 2 * SINK:])

    along_x = jnp.concatenate([r2, sink])
    xs = {s: lax.ppermute(along_x, "ctx", X_SHIFT[s]) for s in (1, 3, 2)}
    ys = {
        s: lax.ppermute(jnp.concatenate([r1, meta, jnp.where(y + s < 4, pas, far)]), "ctx", Y_SHIFT[s])
        for s in (1, 3, 2)
    }
    for s in (1, 2, 3):
        meta = jnp.where((line >> 1) == s, ys[s][2 * PAIR:2 * PAIR + META], meta)
        sink = jnp.where(x == s, xs[s][2 * PAIR:], sink)
    h1 = jnp.concatenate([r1] + [ys[s][:2 * PAIR] for s in (1, 2, 3)] + [meta])
    h2 = jnp.concatenate([r2] + [xs[s][:2 * PAIR] for s in (1, 2, 3)] + [sink])

    a = {0: h1} | {s: lax.ppermute(h1, "ctx", X_SHIFT[s]) for s in (1, 3)}
    b = {0: h2} | {s: lax.ppermute(h2, "ctx", Y_SHIFT[s]) for s in (1, 3)}
    state = (jax.ShapeDtypeStruct((GROUP, ROWS, HD), F32),) * 3
    unit = 2 * 2048 * 256 * 512
    now = call(
        near_kernel, state + state, keys(5 * HALF) + keys(2 * CHUNK), 7 * unit,
        sc, q, q_other, pas, ys[1], ys[2], ys[3], far, h1, h2)
    h1_late, h2_late, *now = lax.optimization_barrier((h1, h2, *now))
    now_p, now_r = now[:3], now[3:]
    a[2] = lax.ppermute(h1_late, "ctx", X_SHIFT[2])
    b[2] = lax.ppermute(h2_late, "ctx", Y_SHIFT[2])
    now_r = call(middle_kernel, state, keys(4 * CHUNK), 8 * unit, sc, q, q_other, a[1], a[3], b[1], b[3], *now_r)
    for s in (1, 2, 3):
        sink = jnp.where(y == s, b[s][8 * PAIR:], sink)
    pages = call(
        pages_kernel, jax.ShapeDtypeStruct((32, 2 * PAGE, 2 * HD), BF16), [], unit // 4,
        sc, *[a[s] for s in range(4)], *[b[s] for s in range(4)])
    got_pages = lax.ppermute(pages, "tp", CORE_SWAP)
    keep, keep_lse, send = call(
        last_kernel,
        (
            jax.ShapeDtypeStruct((ROWS, GROUP * HD), BF16),
            jax.ShapeDtypeStruct((ROWS, HD), F32),
            jax.ShapeDtypeStruct((ROWS, (GROUP + 1) * HD), BF16),
        ),
        keys(2 * CHUNK) + keys(HALF) + [pltpu.VMEM((ROWS, HD), F32)],
        5 * unit, sc, q, q_other, a[2], b[2], sink, *now_r, *now_p)

    got = lax.ppermute(send, "tp", CORE_SWAP)
    attn_out = call(
        merge_kernel, jax.ShapeDtypeStruct((ROWS, GROUP * HD), BF16), [], unit // 4, None, keep, keep_lse, got)
    decode_cache = jnp.where(is_r, pages + got_pages, jnp.zeros((), BF16)).reshape(64, PAGE, 2 * HD)
    return attn_out, decode_cache


def solution(mesh):
    return jax.shard_map(
        shards,
        mesh=mesh,
        in_specs=(P("ctx", "tp"), P("ctx", "tp"), P("ctx", "tp"), P(), P("ctx")),
        out_specs=(P("ctx", "tp"), P("ctx", None, "tp")),
        check_vma=False,
    )
```

```python
import math

import jax
import jax.numpy as jnp
from jax import lax
from jax.experimental import pallas as pl
from jax.experimental.pallas import tpu as pltpu
from jax.sharding import PartitionSpec as P

GROUP = 8
HD = 128
SINK = 64
RECENT = 1024
PAGE = 16
ROWS = 256
HALF = 128
META = 16
CHUNK = 512
WIDE = 2
NEG = -1e30
SCALE = math.log2(math.e) / math.sqrt(HD)
F32 = jnp.float32
BF16 = jnp.bfloat16


def ctx_of(x, z, y):
    return (x % 4) * 8 + (z % 2) * 4 + (y % 4)


CHIPS = [(x, z, y) for x in range(4) for z in range(2) for y in range(4)]
CORE_SWAP = [(i, i ^ 1) for i in range(8)]
Z_SWAP = [(ctx_of(x, z, y), ctx_of(x, z + 1, y)) for x, z, y in CHIPS]
FOUR_ON = [(i, i + 4) for i in range(28)]
Y_SHIFT = {s: [(ctx_of(x, z, y), ctx_of(x, z, y + s)) for x, z, y in CHIPS] for s in (1, 2, 3)}


def two_ways(s, along_y):
    pairs = []
    for x, z, y in CHIPS:
        for tp in range(8):
            there = ctx_of(x, z, y + s) if tp % 2 == along_y else ctx_of(x + s, z, y)
            pairs.append((ctx_of(x, z, y) * 8 + tp, there * 8 + tp))
    return pairs


STAGE_1 = {s: two_ways(s, 0) for s in (1, 2, 3)}
STAGE_2 = {s: two_ways(s, 1) for s in (1, 2, 3)}


def nt_dot(a, b):
    return lax.dot_general(a, b, (((1,), (1,)), ((), ())), preferred_element_type=F32)


def iota(shape, axis):
    return lax.broadcasted_iota(jnp.int32, shape, axis)


def fold(state, q, k, v, left=None, right=None):
    s = nt_dot(q, k)
    if left is not None:
        s = jnp.concatenate([s[:, :HD] + left, s[:, HD:]], axis=1) if s.shape[1] > HD else s + left
    if right is not None:
        s = jnp.concatenate([s[:, :-HD], s[:, -HD:] + right], axis=1)
    high = jnp.max(s, axis=1, keepdims=True)
    top = jnp.broadcast_to(high, (ROWS, HD)) if state is None else jnp.maximum(state[0], high)
    p = jnp.exp2((s - jnp.concatenate([top] * (s.shape[1] // HD), axis=1)) * SCALE).astype(BF16)
    up = jnp.dot(p, v, preferred_element_type=F32)
    if state is None:
        return top, up[:, HD:], up[:, :HD]
    keep = jnp.exp2((state[0] - top) * SCALE)
    return top, state[1] * keep + up[:, HD:], state[2] * keep + up[:, :HD]


def put_keys(k_s, v_s, at, ref, first, rows, gap):
    k_s[pl.ds(at, rows), 0:HD] = ref[first:first + rows, :]
    v_s[pl.ds(at, rows), 0:HD] = ref[first + gap:first + gap + rows, :]


def put_ranges(k_s, v_s, at, ref):
    for n in range(8):
        put_keys(k_s, v_s, at + n * HALF, ref, n * ROWS, HALF, HALF)


def put_bias(k_s, v_s, bias):
    lane = iota(bias.shape, 1)
    k_s[:, HD:] = jnp.where(lane == 0, bias, 0.0).astype(BF16)
    v_s[:, HD:] = jnp.ones(bias.shape, BF16)


def range_of(sc, inner, outer, far):
    x, y, z, core = sc[0], sc[1], sc[2], sc[3]
    dx = jnp.where(core == 0, outer, inner)
    dy = jnp.where(core == 0, inner, outer)
    zz = jnp.where(far == 0, z, 1 - z)
    return ((x - dx) & 3) * 8 + zz * 4 + ((y - dy) & 3)


def range_bias(sc, outers):
    n = iota((len(outers) * 8 * HALF, HD), 0)
    outer = jnp.full(n.shape, outers[0], jnp.int32)
    for i, distance in enumerate(outers[1:], 1):
        outer = jnp.where(n >> 10 == i, distance, outer)
    return jnp.where(range_of(sc, (n >> 8) & 3, outer, (n >> 7) & 1) <= sc[4], 0.0, NEG)


def load_head(q_a, q_b, flag, a):
    cols = slice(a * HD, (a + 1) * HD)
    q = jnp.where(flag == 1, q_a[:, cols], q_b[:, cols])
    one = jnp.where(iota((ROWS, HD), 1) == 0, 1.0, 0.0).astype(BF16)
    return jnp.concatenate([q, one], axis=1)


def near_kernel(sc, q_own, q_other, here, m_out, l_out, o_out, kr, vr):
    core, is_r = sc[3], sc[5]
    put_ranges(kr, vr, 0, here)
    put_bias(kr, vr, range_bias(sc, (0,)))
    own = jnp.where(core * HALF + iota((ROWS, HD), 1) > iota((ROWS, HD), 0), NEG, 0.0)

    def heads(i):
        at = [WIDE * i + u for u in range(WIDE)]
        q = [load_head(q_own, q_other, is_r, a) for a in at]
        state = [fold(None, q[u], kr[0:CHUNK, :], vr[0:CHUNK, :], left=own) for u in range(WIDE)]
        state = [fold(state[u], q[u], kr[CHUNK:, :], vr[CHUNK:, :]) for u in range(WIDE)]
        for u in range(WIDE):
            m_out[at[u]], l_out[at[u]], o_out[at[u]] = state[u]

    for i in range(GROUP // WIDE):
        heads(i)


def passing_kernel(sc, q_own, q_other, pas, p1, p2, p3, far, m_out, l_out, o_out, kp, vp):
    core, c, is_r = sc[3], sc[4], sc[5]
    for n, ref in enumerate((pas, p1, p2, p3, far)):
        put_keys(kp, vp, n * HALF, ref, 0, HALF, HALF)
    put_bias(kp, vp, jnp.where((iota((5 * HALF, HD), 0) >> 7) <= c, 0.0, NEG))
    row = iota((ROWS, HD), 0)
    key = core * HALF + iota((ROWS, HD), 1)
    own = jnp.where(key > row, NEG, 0.0)
    edge = jnp.where(key <= row, NEG, 0.0)

    def heads(i):
        at = [WIDE * i + u for u in range(WIDE)]
        q = [load_head(q_other, q_own, is_r, a) for a in at]
        state = [fold(None, q[u], kp[0:3 * HALF, :], vp[0:3 * HALF, :], left=own) for u in range(WIDE)]
        state = [fold(state[u], q[u], kp[3 * HALF:, :], vp[3 * HALF:, :], right=edge) for u in range(WIDE)]
        for u in range(WIDE):
            m_out[at[u]], l_out[at[u]], o_out[at[u]] = state[u]

    for i in range(GROUP // WIDE):
        heads(i)


def middle_kernel(sc, q_own, q_other, r1, r3, m_in, l_in, o_in, m_out, l_out, o_out, kr, vr):
    is_r = sc[5]
    put_ranges(kr, vr, 0, r1)
    put_ranges(kr, vr, 8 * HALF, r3)
    put_bias(kr, vr, range_bias(sc, (1, 3)))

    def heads(i):
        at = [WIDE * i + u for u in range(WIDE)]
        q = [load_head(q_own, q_other, is_r, a) for a in at]
        state = [(m_in[a], l_in[a], o_in[a]) for a in at]
        for n in range(4):
            rows = slice(n * CHUNK, (n + 1) * CHUNK)
            state = [fold(state[u], q[u], kr[rows, :], vr[rows, :]) for u in range(WIDE)]
        for u in range(WIDE):
            m_out[at[u]], l_out[at[u]], o_out[at[u]] = state[u]

    for i in range(GROUP // WIDE):
        heads(i)


def finish(state):
    m, l, o = state
    return o / l, m * SCALE + jnp.log2(l)


def last_kernel(sc, q_own, q_other, r2, sink, m_in, l_in, o_in, mp_in, lp_in, op_in, keep, keep_lse, send,
                kr, vr, ks, vs, lse_s):
    core, c, is_r = sc[3], sc[4], sc[5]
    put_ranges(kr, vr, 0, r2)
    put_bias(kr, vr, range_bias(sc, (2,)))
    ks[...] = jnp.zeros((HALF, 2 * HD), BF16)
    vs[...] = jnp.zeros((HALF, 2 * HD), BF16)
    put_keys(ks, vs, 0, sink, 0, SINK, SINK)
    put_bias(ks, vs, jnp.zeros((HALF, HD), F32))
    row = iota((ROWS, HD), 0)
    lane = iota((ROWS, HD), 1)
    seen = (core == 0) & (lane < SINK) & (c * ROWS + row - lane >= RECENT)
    sink_bias = jnp.where(seen, 0.0, NEG)
    lse_s[...] = jnp.zeros((ROWS, HD), F32)
    keep_lse[...] = jnp.zeros((ROWS, HD), F32)

    def heads(i):
        at = [WIDE * i + u for u in range(WIDE)]
        qp = [load_head(q_other, q_own, is_r, a) for a in at]
        qr = [load_head(q_own, q_other, is_r, a) for a in at]
        sr = [(m_in[a], l_in[a], o_in[a]) for a in at]
        sp = [(mp_in[a], lp_in[a], op_in[a]) for a in at]
        sr = [fold(sr[u], qr[u], kr[0:CHUNK, :], vr[0:CHUNK, :]) for u in range(WIDE)]
        sp = [fold(sp[u], qp[u], ks[...], vs[...], left=sink_bias) for u in range(WIDE)]
        sr = [fold(sr[u], qr[u], kr[CHUNK:, :], vr[CHUNK:, :]) for u in range(WIDE)]
        for u in range(WIDE):
            cols = slice(at[u] * HD, (at[u] + 1) * HD)
            out_r, lse_r = finish(sr[u])
            out_p, lse_p = finish(sp[u])
            keep[:, cols] = jnp.where(is_r == 1, out_r, out_p).astype(BF16)
            send[:, cols] = jnp.where(is_r == 1, out_p, out_r).astype(BF16)
            keep_lse[...] = jnp.where(lane == at[u], jnp.where(is_r == 1, lse_r, lse_p), keep_lse[...])
            lse_s[...] = jnp.where(lane == at[u], jnp.where(is_r == 1, lse_p, lse_r), lse_s[...])

    for i in range(GROUP // WIDE):
        heads(i)
    lse = lse_s[...]
    high = lse.astype(BF16).astype(F32)
    mid = (lse - high).astype(BF16).astype(F32)
    low = lse - high - mid
    parts = high + pltpu.roll(mid, GROUP, 1) + pltpu.roll(low, 2 * GROUP, 1)
    send[:, GROUP * HD:] = parts.astype(BF16)


def merge_kernel(keep, keep_lse, got, out_ref):
    ext = got[:, GROUP * HD:].astype(F32)
    lse = ext + pltpu.roll(ext, HD - GROUP, 1) + pltpu.roll(ext, HD - 2 * GROUP, 1)
    lane = iota((ROWS, HD), 1)
    gap = jnp.where(lane < GROUP, lse - keep_lse[...], 0.0)
    weight = 1.0 / (1.0 + jnp.exp2(jnp.clip(gap, -126.0, 126.0)))
    for a in range(GROUP):
        cols = slice(a * HD, (a + 1) * HD)
        w = weight[:, a:a + 1]
        mine, theirs = keep[:, cols].astype(F32), got[:, cols].astype(F32)
        out_ref[:, cols] = (theirs + w * (mine - theirs)).astype(BF16)


def pages_kernel(sc, r0, r1, r2, r3, out_ref):
    c = sc[4]
    row = iota((2 * PAGE, HD), 0)
    lane = iota((2 * PAGE, HD), 1)
    same_row = (lane & (PAGE - 1)) == (row & (PAGE - 1))
    want = (2 * c + (row >> 4)).astype(F32)
    for outer, ref in enumerate((r0, r1, r2, r3)):
        codes = ref[8 * ROWS:8 * ROWS + META, :].astype(F32)
        for n in range(8):
            select = jnp.where(same_row & (codes[n:n + 1, :] == want), 1.0, 0.0).astype(BF16)
            block = range_of(sc, n >> 1, outer, n & 1)
            for part in range(2):
                at = n * ROWS + part * HALF
                pages = jnp.dot(select, ref[at:at + HALF, :], preferred_element_type=F32)
                out_ref[block, :, part * HD:(part + 1) * HD] = pages.astype(BF16)


VMEM_SPEC = pl.BlockSpec(memory_space=pltpu.VMEM)
SMEM_SPEC = pl.BlockSpec(memory_space=pltpu.SMEM)


def call(kernel, out_shape, scratch, flops, sc, *args):
    many = isinstance(out_shape, tuple)
    specs = ([SMEM_SPEC] if sc is not None else []) + [VMEM_SPEC] * len(args)
    operands = ([sc] if sc is not None else []) + list(args)
    return pl.pallas_call(
        kernel,
        out_shape=out_shape,
        in_specs=specs,
        out_specs=(VMEM_SPEC,) * len(out_shape) if many else VMEM_SPEC,
        scratch_shapes=scratch,
        compiler_params=pltpu.CompilerParams(vmem_limit_bytes=24 * 1024 * 1024),
        cost_estimate=pl.CostEstimate(flops=flops, bytes_accessed=4 << 20, transcendentals=flops // 512),
    )(*operands)


def keys(rows):
    return [pltpu.VMEM((rows, 2 * HD), BF16), pltpu.VMEM((rows, 2 * HD), BF16)]


def shards(q, k, v, head_kind, page_owner):
    c = lax.axis_index("ctx")
    tp = lax.axis_index("tp")
    x, z, y = c // 8, (c // 4) % 2, c % 4
    core = tp % 2
    is_r = lax.dynamic_index_in_dim(head_kind, tp, 0, keepdims=False) == 1
    sc = jnp.stack([x, y, z, core, c, is_r.astype(jnp.int32), tp, tp]).astype(jnp.int32)

    low = jnp.concatenate([k[:HALF], v[:HALF]])
    high = jnp.concatenate([k[HALF:], v[HALF:]])
    stay = jnp.where(core == 0, low, high)
    came = lax.ppermute(jnp.where(core == 0, high, low), "tp", CORE_SWAP)
    q_other = lax.ppermute(q, "tp", CORE_SWAP)
    ret = jnp.where(is_r, stay, came)
    pas = jnp.where(is_r, came, stay)

    earlier = lax.iota(jnp.int32, 16)[None, :] < lax.iota(jnp.int32, 16)[:, None]
    rank = jnp.sum(((page_owner[:, None] == page_owner[None, :]) & earlier).astype(jnp.int32), axis=1)
    code = page_owner * 2 + rank
    code = jnp.where(core == 0, code[:8], code[8:]).astype(BF16)
    meta = jnp.broadcast_to(jnp.repeat(code, PAGE)[None, :], (META, HD))

    sink = jnp.concatenate([pas[:SINK], pas[HALF:HALF + SINK]])
    theirs = lax.ppermute(jnp.concatenate([ret, sink, meta]), "ctx", Z_SWAP)
    theirs, q_other = lax.optimization_barrier((theirs, q_other))
    both = jnp.concatenate([ret, theirs[:ROWS]])
    sink = jnp.where(z == 0, sink, theirs[ROWS:ROWS + 2 * SINK])
    line = iota((META, HD), 0)
    meta = jnp.where((line & 1) == 0, meta, theirs[ROWS + 2 * SINK:])

    axes = ("ctx", "tp")
    message = jnp.concatenate([both, sink, meta])
    got = {s: lax.ppermute(message, axes, STAGE_1[s]) for s in (1, 3, 2)}
    for s in (1, 2, 3):
        meta = jnp.where((line >> 1) == s, got[s][2 * ROWS + 2 * SINK:], meta)
        sink = jnp.where(y == s, got[s][2 * ROWS:2 * ROWS + 2 * SINK], sink)
    message = jnp.concatenate([both] + [got[s][:2 * ROWS] for s in (1, 2, 3)] + [meta, sink])

    far = lax.ppermute(jnp.concatenate([pas, theirs[-META:]]), "ctx", FOUR_ON)[:ROWS]

    r = {0: message} | {s: lax.ppermute(message, axes, STAGE_2[s]) for s in (1, 3)}
    p = {s: lax.ppermute(jnp.where(y + s < 4, pas, far), "ctx", Y_SHIFT[s]) for s in (1, 3, 2)}

    state = (jax.ShapeDtypeStruct((GROUP, ROWS, HD), F32),) * 3
    unit = 2 * 2048 * 256 * 512
    now = call(near_kernel, state, keys(8 * HALF), 4 * unit, sc, q, q_other, message)
    late, sc_p, *now = lax.optimization_barrier((message, sc, *now))
    r[2] = lax.ppermute(late, axes, STAGE_2[2])
    now_p = call(passing_kernel, state, keys(5 * HALF), 3 * unit, sc_p, q, q_other, pas, p[1], p[2], p[3], far)
    sc_m, now_p0 = lax.optimization_barrier((sc_p, now_p[0]))
    now = call(middle_kernel, state, keys(16 * HALF), 8 * unit, sc_m, q, q_other, r[1], r[3], *now)
    sc_l, now_0 = lax.optimization_barrier((sc_m, now[0]))
    for s in (1, 2, 3):
        sink = jnp.where(x == s, r[s][8 * ROWS + META:], sink)
    pages = call(
        pages_kernel, jax.ShapeDtypeStruct((32, 2 * PAGE, 2 * HD), BF16), [], unit // 4,
        sc_l, *[r[s] for s in range(4)])
    got_pages = lax.ppermute(pages, "tp", CORE_SWAP)
    keep, keep_lse, send = call(
        last_kernel,
        (
            jax.ShapeDtypeStruct((ROWS, GROUP * HD), BF16),
            jax.ShapeDtypeStruct((ROWS, HD), F32),
            jax.ShapeDtypeStruct((ROWS, (GROUP + 1) * HD), BF16),
        ),
        keys(8 * HALF) + keys(HALF) + [pltpu.VMEM((ROWS, HD), F32)],
        5 * unit, sc_l, q, q_other, r[2], sink, now_0, *now[1:], now_p0, *now_p[1:])

    got = lax.ppermute(send, "tp", CORE_SWAP)
    attn_out = call(
        merge_kernel, jax.ShapeDtypeStruct((ROWS, GROUP * HD), BF16), [], unit // 4, None, keep, keep_lse, got)
    decode_cache = jnp.where(is_r, pages + got_pages, jnp.zeros((), BF16)).reshape(64, PAGE, 2 * HD)
    return attn_out, decode_cache


def solution(mesh):
    return jax.shard_map(
        shards,
        mesh=mesh,
        in_specs=(P("ctx", "tp"), P("ctx", "tp"), P("ctx", "tp"), P(), P("ctx")),
        out_specs=(P("ctx", "tp"), P("ctx", None, "tp")),
        check_vma=False,
    )
```

```python
import math

import jax
import jax.numpy as jnp
from jax import lax
from jax.experimental import pallas as pl
from jax.experimental.pallas import tpu as pltpu
from jax.sharding import PartitionSpec as P

GROUP = 8
HD = 128
SINK = 64
RECENT = 1024
PAGE = 16
ROWS = 256
HALF = 128
META = 16
CHUNK = 512
WIDE = 2
NEG = -1e30
SCALE = math.log2(math.e) / math.sqrt(HD)
F32 = jnp.float32
BF16 = jnp.bfloat16


def ctx_of(x, z, y):
    return (x % 4) * 8 + (z % 2) * 4 + (y % 4)


CHIPS = [(x, z, y) for x in range(4) for z in range(2) for y in range(4)]
CORE_SWAP = [(i, i ^ 1) for i in range(8)]
Z_SWAP = [(ctx_of(x, z, y), ctx_of(x, z + 1, y)) for x, z, y in CHIPS]
FOUR_ON = [(i, i + 4) for i in range(28)]
Y_SHIFT = {s: [(ctx_of(x, z, y), ctx_of(x, z, y + s)) for x, z, y in CHIPS] for s in (1, 2, 3)}


def two_ways(s, along_y):
    pairs = []
    for x, z, y in CHIPS:
        for tp in range(8):
            there = ctx_of(x, z, y + s) if tp % 2 == along_y else ctx_of(x + s, z, y)
            pairs.append((ctx_of(x, z, y) * 8 + tp, there * 8 + tp))
    return pairs


STAGE_1 = {s: two_ways(s, 0) for s in (1, 2, 3)}
STAGE_2 = {s: two_ways(s, 1) for s in (1, 2, 3)}


def nt_dot(a, b):
    return lax.dot_general(a, b, (((1,), (1,)), ((), ())), preferred_element_type=F32)


def iota(shape, axis):
    return lax.broadcasted_iota(jnp.int32, shape, axis)


def fold(state, q, k, v, left=None, right=None):
    s = nt_dot(q, k)
    if left is not None:
        s = jnp.concatenate([s[:, :HD] + left, s[:, HD:]], axis=1) if s.shape[1] > HD else s + left
    if right is not None:
        s = jnp.concatenate([s[:, :-HD], s[:, -HD:] + right], axis=1)
    high = jnp.max(s, axis=1, keepdims=True)
    top = jnp.broadcast_to(high, (ROWS, HD)) if state is None else jnp.maximum(state[0], high)
    p = jnp.exp2((s - jnp.concatenate([top] * (s.shape[1] // HD), axis=1)) * SCALE).astype(BF16)
    up = jnp.dot(p, v, preferred_element_type=F32)
    if state is None:
        return top, up[:, HD:], up[:, :HD]
    keep = jnp.exp2((state[0] - top) * SCALE)
    return top, state[1] * keep + up[:, HD:], state[2] * keep + up[:, :HD]


def put_keys(k_s, v_s, at, ref, first, rows, gap):
    k_s[pl.ds(at, rows), 0:HD] = ref[first:first + rows, :]
    v_s[pl.ds(at, rows), 0:HD] = ref[first + gap:first + gap + rows, :]


def put_ranges(k_s, v_s, at, ref):
    for n in range(8):
        put_keys(k_s, v_s, at + n * HALF, ref, n * ROWS, HALF, HALF)


def put_bias(k_s, v_s, bias):
    lane = iota(bias.shape, 1)
    k_s[:, HD:] = jnp.where(lane == 0, bias, 0.0).astype(BF16)
    v_s[:, HD:] = jnp.ones(bias.shape, BF16)


def range_of(sc, inner, outer, far):
    x, y, z, core = sc[0], sc[1], sc[2], sc[3]
    dx = jnp.where(core == 0, outer, inner)
    dy = jnp.where(core == 0, inner, outer)
    zz = jnp.where(far == 0, z, 1 - z)
    return ((x - dx) & 3) * 8 + zz * 4 + ((y - dy) & 3)


def range_bias(sc, outers):
    n = iota((len(outers) * 8 * HALF, HD), 0)
    outer = jnp.full(n.shape, outers[0], jnp.int32)
    for i, distance in enumerate(outers[1:], 1):
        outer = jnp.where(n >> 10 == i, distance, outer)
    return jnp.where(range_of(sc, (n >> 8) & 3, outer, (n >> 7) & 1) <= sc[4], 0.0, NEG)


def load_head(q_a, q_b, flag, a):
    cols = slice(a * HD, (a + 1) * HD)
    q = jnp.where(flag == 1, q_a[:, cols], q_b[:, cols])
    one = jnp.where(iota((ROWS, HD), 1) == 0, 1.0, 0.0).astype(BF16)
    return jnp.concatenate([q, one], axis=1)


def near_kernel(sc, q_own, q_other, here, pas, p1, p2, p3, far, mp_out, lp_out, op_out, m_out, l_out, o_out,
                kp, vp, kr, vr):
    core, c, is_r = sc[3], sc[4], sc[5]
    put_ranges(kr, vr, 0, here)
    put_bias(kr, vr, range_bias(sc, (0,)))
    for n, ref in enumerate((pas, p1, p2, p3, far)):
        put_keys(kp, vp, n * HALF, ref, 0, HALF, HALF)
    put_bias(kp, vp, jnp.where((iota((5 * HALF, HD), 0) >> 7) <= c, 0.0, NEG))
    row = iota((ROWS, HD), 0)
    key = core * HALF + iota((ROWS, HD), 1)
    own = jnp.where(key > row, NEG, 0.0)
    edge = jnp.where(key <= row, NEG, 0.0)

    def heads(i):
        at = [WIDE * i + u for u in range(WIDE)]
        qp = [load_head(q_other, q_own, is_r, a) for a in at]
        q = [load_head(q_own, q_other, is_r, a) for a in at]
        sr = [fold(None, q[u], kr[0:CHUNK, :], vr[0:CHUNK, :], left=own) for u in range(WIDE)]
        sp = [fold(None, qp[u], kp[0:3 * HALF, :], vp[0:3 * HALF, :], left=own) for u in range(WIDE)]
        sr = [fold(sr[u], q[u], kr[CHUNK:, :], vr[CHUNK:, :]) for u in range(WIDE)]
        sp = [fold(sp[u], qp[u], kp[3 * HALF:, :], vp[3 * HALF:, :], right=edge) for u in range(WIDE)]
        for u in range(WIDE):
            m_out[at[u]], l_out[at[u]], o_out[at[u]] = sr[u]
            mp_out[at[u]], lp_out[at[u]], op_out[at[u]] = sp[u]

    for i in range(GROUP // WIDE):
        heads(i)


def middle_kernel(sc, q_own, q_other, r1, r3, m_in, l_in, o_in, m_out, l_out, o_out, kr, vr):
    is_r = sc[5]
    put_ranges(kr, vr, 0, r1)
    put_ranges(kr, vr, 8 * HALF, r3)
    put_bias(kr, vr, range_bias(sc, (1, 3)))

    def heads(i):
        at = [WIDE * i + u for u in range(WIDE)]
        q = [load_head(q_own, q_other, is_r, a) for a in at]
        state = [(m_in[a], l_in[a], o_in[a]) for a in at]
        for n in range(4):
            rows = slice(n * CHUNK, (n + 1) * CHUNK)
            state = [fold(state[u], q[u], kr[rows, :], vr[rows, :]) for u in range(WIDE)]
        for u in range(WIDE):
            m_out[at[u]], l_out[at[u]], o_out[at[u]] = state[u]

    for i in range(GROUP // WIDE):
        heads(i)


def finish(state):
    m, l, o = state
    return o / l, m * SCALE + jnp.log2(l)


def last_kernel(sc, q_own, q_other, r2, sink, m_in, l_in, o_in, mp_in, lp_in, op_in, keep, keep_lse, send,
                kr, vr, ks, vs, lse_s):
    core, c, is_r = sc[3], sc[4], sc[5]
    put_ranges(kr, vr, 0, r2)
    put_bias(kr, vr, range_bias(sc, (2,)))
    ks[...] = jnp.zeros((HALF, 2 * HD), BF16)
    vs[...] = jnp.zeros((HALF, 2 * HD), BF16)
    put_keys(ks, vs, 0, sink, 0, SINK, SINK)
    put_bias(ks, vs, jnp.zeros((HALF, HD), F32))
    row = iota((ROWS, HD), 0)
    lane = iota((ROWS, HD), 1)
    seen = (core == 0) & (lane < SINK) & (c * ROWS + row - lane >= RECENT)
    sink_bias = jnp.where(seen, 0.0, NEG)
    lse_s[...] = jnp.zeros((ROWS, HD), F32)
    keep_lse[...] = jnp.zeros((ROWS, HD), F32)

    def heads(i):
        at = [WIDE * i + u for u in range(WIDE)]
        qp = [load_head(q_other, q_own, is_r, a) for a in at]
        qr = [load_head(q_own, q_other, is_r, a) for a in at]
        sr = [(m_in[a], l_in[a], o_in[a]) for a in at]
        sp = [(mp_in[a], lp_in[a], op_in[a]) for a in at]
        sr = [fold(sr[u], qr[u], kr[0:CHUNK, :], vr[0:CHUNK, :]) for u in range(WIDE)]
        sp = [fold(sp[u], qp[u], ks[...], vs[...], left=sink_bias) for u in range(WIDE)]
        sr = [fold(sr[u], qr[u], kr[CHUNK:, :], vr[CHUNK:, :]) for u in range(WIDE)]
        for u in range(WIDE):
            cols = slice(at[u] * HD, (at[u] + 1) * HD)
            out_r, lse_r = finish(sr[u])
            out_p, lse_p = finish(sp[u])
            keep[:, cols] = jnp.where(is_r == 1, out_r, out_p).astype(BF16)
            send[:, cols] = jnp.where(is_r == 1, out_p, out_r).astype(BF16)
            keep_lse[...] = jnp.where(lane == at[u], jnp.where(is_r == 1, lse_r, lse_p), keep_lse[...])
            lse_s[...] = jnp.where(lane == at[u], jnp.where(is_r == 1, lse_p, lse_r), lse_s[...])

    for i in range(GROUP // WIDE):
        heads(i)
    lse = lse_s[...]
    high = lse.astype(BF16).astype(F32)
    mid = (lse - high).astype(BF16).astype(F32)
    low = lse - high - mid
    parts = high + pltpu.roll(mid, GROUP, 1) + pltpu.roll(low, 2 * GROUP, 1)
    send[:, GROUP * HD:] = parts.astype(BF16)


def merge_kernel(keep, keep_lse, got, out_ref):
    ext = got[:, GROUP * HD:].astype(F32)
    lse = ext + pltpu.roll(ext, HD - GROUP, 1) + pltpu.roll(ext, HD - 2 * GROUP, 1)
    lane = iota((ROWS, HD), 1)
    gap = jnp.where(lane < GROUP, lse - keep_lse[...], 0.0)
    weight = 1.0 / (1.0 + jnp.exp2(jnp.clip(gap, -126.0, 126.0)))
    for a in range(GROUP):
        cols = slice(a * HD, (a + 1) * HD)
        w = weight[:, a:a + 1]
        mine, theirs = keep[:, cols].astype(F32), got[:, cols].astype(F32)
        out_ref[:, cols] = (theirs + w * (mine - theirs)).astype(BF16)


def pages_kernel(sc, r0, r1, r2, r3, out_ref):
    c = sc[4]
    row = iota((2 * PAGE, HD), 0)
    lane = iota((2 * PAGE, HD), 1)
    same_row = (lane & (PAGE - 1)) == (row & (PAGE - 1))
    want = (2 * c + (row >> 4)).astype(F32)
    for outer, ref in enumerate((r0, r1, r2, r3)):
        codes = ref[8 * ROWS:8 * ROWS + META, :].astype(F32)
        for n in range(8):
            select = jnp.where(same_row & (codes[n:n + 1, :] == want), 1.0, 0.0).astype(BF16)
            block = range_of(sc, n >> 1, outer, n & 1)
            for part in range(2):
                at = n * ROWS + part * HALF
                pages = jnp.dot(select, ref[at:at + HALF, :], preferred_element_type=F32)
                out_ref[block, :, part * HD:(part + 1) * HD] = pages.astype(BF16)


VMEM_SPEC = pl.BlockSpec(memory_space=pltpu.VMEM)
SMEM_SPEC = pl.BlockSpec(memory_space=pltpu.SMEM)


def call(kernel, out_shape, scratch, flops, sc, *args):
    many = isinstance(out_shape, tuple)
    specs = ([SMEM_SPEC] if sc is not None else []) + [VMEM_SPEC] * len(args)
    operands = ([sc] if sc is not None else []) + list(args)
    return pl.pallas_call(
        kernel,
        out_shape=out_shape,
        in_specs=specs,
        out_specs=(VMEM_SPEC,) * len(out_shape) if many else VMEM_SPEC,
        scratch_shapes=scratch,
        compiler_params=pltpu.CompilerParams(vmem_limit_bytes=24 * 1024 * 1024),
        cost_estimate=pl.CostEstimate(flops=flops, bytes_accessed=4 << 20, transcendentals=flops // 512),
    )(*operands)


def keys(rows):
    return [pltpu.VMEM((rows, 2 * HD), BF16), pltpu.VMEM((rows, 2 * HD), BF16)]


def shards(q, k, v, head_kind, page_owner):
    c = lax.axis_index("ctx")
    tp = lax.axis_index("tp")
    x, z, y = c // 8, (c // 4) % 2, c % 4
    core = tp % 2
    is_r = lax.dynamic_index_in_dim(head_kind, tp, 0, keepdims=False) == 1
    sc = jnp.stack([x, y, z, core, c, is_r.astype(jnp.int32), tp, tp]).astype(jnp.int32)

    low = jnp.concatenate([k[:HALF], v[:HALF]])
    high = jnp.concatenate([k[HALF:], v[HALF:]])
    stay = jnp.where(core == 0, low, high)
    came = lax.ppermute(jnp.where(core == 0, high, low), "tp", CORE_SWAP)
    q_other = lax.ppermute(q, "tp", CORE_SWAP)
    ret = jnp.where(is_r, stay, came)
    pas = jnp.where(is_r, came, stay)

    earlier = lax.iota(jnp.int32, 16)[None, :] < lax.iota(jnp.int32, 16)[:, None]
    rank = jnp.sum(((page_owner[:, None] == page_owner[None, :]) & earlier).astype(jnp.int32), axis=1)
    code = page_owner * 2 + rank
    code = jnp.where(core == 0, code[:8], code[8:]).astype(BF16)
    meta = jnp.broadcast_to(jnp.repeat(code, PAGE)[None, :], (META, HD))

    sink = jnp.concatenate([pas[:SINK], pas[HALF:HALF + SINK]])
    message = jnp.concatenate([ret, sink, meta])
    theirs = lax.ppermute(message, "ctx", Z_SWAP)
    far = lax.ppermute(jnp.concatenate([pas, message[-META:]]), "ctx", FOUR_ON)[:ROWS]
    theirs, far, q_other = lax.optimization_barrier((theirs, far, q_other))
    both = jnp.concatenate([ret, theirs[:ROWS]])
    sink = jnp.where(z == 0, sink, theirs[ROWS:ROWS + 2 * SINK])
    line = iota((META, HD), 0)
    meta = jnp.where((line & 1) == 0, meta, theirs[ROWS + 2 * SINK:])

    axes = ("ctx", "tp")
    message = jnp.concatenate([both, sink, meta])
    got = {s: lax.ppermute(message, axes, STAGE_1[s]) for s in (1, 3, 2)}
    pas, far, got[1] = lax.optimization_barrier((pas, far, got[1]))
    p = {s: lax.ppermute(jnp.where(y + s < 4, pas, far), "ctx", Y_SHIFT[s]) for s in (1, 3, 2)}

    for s in (1, 2, 3):
        meta = jnp.where((line >> 1) == s, got[s][2 * ROWS + 2 * SINK:], meta)
        sink = jnp.where(y == s, got[s][2 * ROWS:2 * ROWS + 2 * SINK], sink)
    message = jnp.concatenate([both] + [got[s][:2 * ROWS] for s in (1, 2, 3)] + [meta, sink])

    r = {0: message} | {s: lax.ppermute(message, axes, STAGE_2[s]) for s in (1, 3)}
    state = (jax.ShapeDtypeStruct((GROUP, ROWS, HD), F32),) * 3
    unit = 2 * 2048 * 256 * 512
    now = call(
        near_kernel, state + state, keys(5 * HALF) + keys(8 * HALF), 7 * unit,
        sc, q, q_other, message, pas, p[1], p[2], p[3], far)
    late, *now = lax.optimization_barrier((message, *now))
    now_p, now = now[:3], now[3:]
    r[2] = lax.ppermute(late, axes, STAGE_2[2])
    now = call(middle_kernel, state, keys(16 * HALF), 8 * unit, sc, q, q_other, r[1], r[3], *now)
    sc_l, now_0 = lax.optimization_barrier((sc, now[0]))
    for s in (1, 2, 3):
        sink = jnp.where(x == s, r[s][8 * ROWS + META:], sink)
    pages = call(
        pages_kernel, jax.ShapeDtypeStruct((32, 2 * PAGE, 2 * HD), BF16), [], unit // 4,
        sc_l, *[r[s] for s in range(4)])
    got_pages = lax.ppermute(pages, "tp", CORE_SWAP)
    keep, keep_lse, send = call(
        last_kernel,
        (
            jax.ShapeDtypeStruct((ROWS, GROUP * HD), BF16),
            jax.ShapeDtypeStruct((ROWS, HD), F32),
            jax.ShapeDtypeStruct((ROWS, (GROUP + 1) * HD), BF16),
        ),
        keys(8 * HALF) + keys(HALF) + [pltpu.VMEM((ROWS, HD), F32)],
        5 * unit, sc_l, q, q_other, r[2], sink, now_0, *now[1:], *now_p)

    got = lax.ppermute(send, "tp", CORE_SWAP)
    attn_out = call(
        merge_kernel, jax.ShapeDtypeStruct((ROWS, GROUP * HD), BF16), [], unit // 4, None, keep, keep_lse, got)
    decode_cache = jnp.where(is_r, pages + got_pages, jnp.zeros((), BF16)).reshape(64, PAGE, 2 * HD)
    return attn_out, decode_cache


def solution(mesh):
    return jax.shard_map(
        shards,
        mesh=mesh,
        in_specs=(P("ctx", "tp"), P("ctx", "tp"), P("ctx", "tp"), P(), P("ctx")),
        out_specs=(P("ctx", "tp"), P("ctx", None, "tp")),
        check_vma=False,
    )
```

```python
import math

import jax
import jax.numpy as jnp
from jax import lax
from jax.experimental import pallas as pl
from jax.experimental.pallas import tpu as pltpu
from jax.sharding import PartitionSpec as P

GROUP = 8
HD = 128
SINK = 64
RECENT = 1024
PAGE = 16
ROWS = 256
HALF = 128
META = 16
CHUNK = 512
WIDE = 2
NEG = -1e30
SCALE = math.log2(math.e) / math.sqrt(HD)
F32 = jnp.float32
BF16 = jnp.bfloat16


def ctx_of(x, z, y):
    return (x % 4) * 8 + (z % 2) * 4 + (y % 4)


CHIPS = [(x, z, y) for x in range(4) for z in range(2) for y in range(4)]
CORE_SWAP = [(i, i ^ 1) for i in range(8)]
Z_SWAP = [(ctx_of(x, z, y), ctx_of(x, z + 1, y)) for x, z, y in CHIPS]
X_STEP = [(ctx_of(x, 0, y), ctx_of(x + 1, 0, y)) for x in range(3) for y in range(4)]
Y_SHIFT = {s: [(ctx_of(x, z, y), ctx_of(x, z, y + s)) for x, z, y in CHIPS] for s in (1, 2, 3)}


def two_ways(s, along_y):
    pairs = []
    for x, z, y in CHIPS:
        for tp in range(8):
            there = ctx_of(x, z, y + s) if tp % 2 == along_y else ctx_of(x + s, z, y)
            pairs.append((ctx_of(x, z, y) * 8 + tp, there * 8 + tp))
    return pairs


STAGE_1 = {s: two_ways(s, 0) for s in (1, 2, 3)}
STAGE_2 = {s: two_ways(s, 1) for s in (1, 2, 3)}


def nt_dot(a, b):
    return lax.dot_general(a, b, (((1,), (1,)), ((), ())), preferred_element_type=F32)


def iota(shape, axis):
    return lax.broadcasted_iota(jnp.int32, shape, axis)


def fold(state, q, k, v, left=None, right=None):
    s = nt_dot(q, k)
    if left is not None:
        s = jnp.concatenate([s[:, :HD] + left, s[:, HD:]], axis=1) if s.shape[1] > HD else s + left
    if right is not None:
        s = jnp.concatenate([s[:, :-HD], s[:, -HD:] + right], axis=1)
    high = jnp.max(s, axis=1, keepdims=True)
    top = jnp.broadcast_to(high, (ROWS, HD)) if state is None else jnp.maximum(state[0], high)
    p = jnp.exp2((s - jnp.concatenate([top] * (s.shape[1] // HD), axis=1)) * SCALE).astype(BF16)
    up = jnp.dot(p, v, preferred_element_type=F32)
    if state is None:
        return top, up[:, HD:], up[:, :HD]
    keep = jnp.exp2((state[0] - top) * SCALE)
    return top, state[1] * keep + up[:, HD:], state[2] * keep + up[:, :HD]


def put_keys(k_s, v_s, at, ref, first, rows, gap):
    k_s[pl.ds(at, rows), 0:HD] = ref[first:first + rows, :]
    v_s[pl.ds(at, rows), 0:HD] = ref[first + gap:first + gap + rows, :]


def put_ranges(k_s, v_s, at, ref):
    for n in range(8):
        put_keys(k_s, v_s, at + n * HALF, ref, n * ROWS, HALF, HALF)


def put_bias(k_s, v_s, bias):
    lane = iota(bias.shape, 1)
    k_s[:, HD:] = jnp.where(lane == 0, bias, 0.0).astype(BF16)
    v_s[:, HD:] = jnp.ones(bias.shape, BF16)


def range_of(sc, inner, outer, far):
    x, y, z, core = sc[0], sc[1], sc[2], sc[3]
    dx = jnp.where(core == 0, outer, inner)
    dy = jnp.where(core == 0, inner, outer)
    zz = jnp.where(far == 0, z, 1 - z)
    return ((x - dx) & 3) * 8 + zz * 4 + ((y - dy) & 3)


def range_bias(sc, outers):
    n = iota((len(outers) * 8 * HALF, HD), 0)
    outer = jnp.full(n.shape, outers[0], jnp.int32)
    for i, distance in enumerate(outers[1:], 1):
        outer = jnp.where(n >> 10 == i, distance, outer)
    return jnp.where(range_of(sc, (n >> 8) & 3, outer, (n >> 7) & 1) <= sc[4], 0.0, NEG)


def load_head(q_a, q_b, flag, a):
    cols = slice(a * HD, (a + 1) * HD)
    q = jnp.where(flag == 1, q_a[:, cols], q_b[:, cols])
    one = jnp.where(iota((ROWS, HD), 1) == 0, 1.0, 0.0).astype(BF16)
    return jnp.concatenate([q, one], axis=1)


def pack(m, l):
    return jnp.where(iota((ROWS, HD), 1) < HD // 2, m, l)


def unpack(both):
    low = iota((ROWS, HD), 1) < HD // 2
    turned = pltpu.roll(both, HD // 2, 1)
    return jnp.where(low, both, turned), jnp.where(low, turned, both)


def near_kernel(sc, q_own, q_other, here, ml_out, o_out, kr, vr):
    core, is_r = sc[3], sc[5]
    put_ranges(kr, vr, 0, here)
    put_bias(kr, vr, range_bias(sc, (0,)))
    own = jnp.where(core * HALF + iota((ROWS, HD), 1) > iota((ROWS, HD), 0), NEG, 0.0)

    def heads(i):
        at = [WIDE * i + u for u in range(WIDE)]
        q = [load_head(q_own, q_other, is_r, a) for a in at]
        state = [fold(None, q[u], kr[0:CHUNK, :], vr[0:CHUNK, :], left=own) for u in range(WIDE)]
        state = [fold(state[u], q[u], kr[CHUNK:, :], vr[CHUNK:, :]) for u in range(WIDE)]
        for u in range(WIDE):
            ml_out[at[u]], o_out[at[u]] = pack(*state[u][:2]), state[u][2]

    for i in range(GROUP // WIDE):
        heads(i)


def finish(state):
    m, l, o = state
    return o / l, m * SCALE + jnp.log2(l)


def rest_kernel(sc, q_own, q_other, r1, r3, r2, sink, pas, p1, p2, p3, far, ml_in, o_in, keep, keep_lse, send,
                kr, vr, kp, vp, lse_s):
    core, c, is_r = sc[3], sc[4], sc[5]
    for n, ref in enumerate((r1, r3, r2)):
        put_ranges(kr, vr, n * 8 * HALF, ref)
    put_bias(kr, vr, range_bias(sc, (1, 3, 2)))
    for n, ref in enumerate((pas, p1, p2, p3)):
        put_keys(kp, vp, n * HALF, ref, 0, HALF, HALF)
    kp[4 * HALF:5 * HALF, :] = jnp.zeros((HALF, 2 * HD), BF16)
    vp[4 * HALF:5 * HALF, :] = jnp.zeros((HALF, 2 * HD), BF16)
    put_keys(kp, vp, 4 * HALF, sink, 0, SINK, SINK)
    put_keys(kp, vp, 5 * HALF, far, 0, HALF, HALF)
    slot = iota((6 * HALF, HD), 0) >> 7
    put_bias(kp, vp, jnp.where((slot - (slot >> 2) <= c) | (slot == 4), 0.0, NEG))
    row = iota((ROWS, HD), 0)
    lane = iota((ROWS, HD), 1)
    key = core * HALF + lane
    own = jnp.where(key > row, NEG, 0.0)
    edge = jnp.where(key <= row, NEG, 0.0)
    seen = (core == 0) & (lane < SINK) & (c * ROWS + row - lane >= RECENT)
    sink_bias = jnp.where(seen, 0.0, NEG)
    lse_s[...] = jnp.zeros((ROWS, HD), F32)
    keep_lse[...] = jnp.zeros((ROWS, HD), F32)

    def heads(i):
        at = [WIDE * i + u for u in range(WIDE)]
        qp = [load_head(q_other, q_own, is_r, a) for a in at]
        qr = [load_head(q_own, q_other, is_r, a) for a in at]
        sr = [(*unpack(ml_in[a]), o_in[a]) for a in at]
        for n in range(6):
            rows = slice(n * CHUNK, (n + 1) * CHUNK)
            sr = [fold(sr[u], qr[u], kr[rows, :], vr[rows, :]) for u in range(WIDE)]
            if n == 1:
                sp = [fold(None, qp[u], kp[0:4 * HALF, :], vp[0:4 * HALF, :], left=own) for u in range(WIDE)]
            if n == 3:
                sp = [fold(sp[u], qp[u], kp[4 * HALF:, :], vp[4 * HALF:, :], left=sink_bias, right=edge) for u in range(WIDE)]
        for u in range(WIDE):
            cols = slice(at[u] * HD, (at[u] + 1) * HD)
            out_r, lse_r = finish(sr[u])
            out_p, lse_p = finish(sp[u])
            keep[:, cols] = jnp.where(is_r == 1, out_r, out_p).astype(BF16)
            send[:, cols] = jnp.where(is_r == 1, out_p, out_r).astype(BF16)
            keep_lse[...] = jnp.where(lane == at[u], jnp.where(is_r == 1, lse_r, lse_p), keep_lse[...])
            lse_s[...] = jnp.where(lane == at[u], jnp.where(is_r == 1, lse_p, lse_r), lse_s[...])

    for i in range(GROUP // WIDE):
        heads(i)
    lse = lse_s[...]
    high = lse.astype(BF16).astype(F32)
    mid = (lse - high).astype(BF16).astype(F32)
    low = lse - high - mid
    parts = high + pltpu.roll(mid, GROUP, 1) + pltpu.roll(low, 2 * GROUP, 1)
    send[:, GROUP * HD:] = parts.astype(BF16)


def merge_kernel(keep, keep_lse, got, out_ref):
    ext = got[:, GROUP * HD:].astype(F32)
    lse = ext + pltpu.roll(ext, HD - GROUP, 1) + pltpu.roll(ext, HD - 2 * GROUP, 1)
    lane = iota((ROWS, HD), 1)
    gap = jnp.where(lane < GROUP, lse - keep_lse[...], 0.0)
    weight = 1.0 / (1.0 + jnp.exp2(jnp.clip(gap, -126.0, 126.0)))
    for a in range(GROUP):
        cols = slice(a * HD, (a + 1) * HD)
        w = weight[:, a:a + 1]
        mine, theirs = keep[:, cols].astype(F32), got[:, cols].astype(F32)
        out_ref[:, cols] = (theirs + w * (mine - theirs)).astype(BF16)


def pages_kernel(sc, r0, r1, r2, r3, out_ref):
    c = sc[4]
    row = iota((2 * PAGE, HD), 0)
    lane = iota((2 * PAGE, HD), 1)
    same_row = (lane & (PAGE - 1)) == (row & (PAGE - 1))
    want = (2 * c + (row >> 4)).astype(F32)
    for outer, ref in enumerate((r0, r1, r2, r3)):
        codes = ref[8 * ROWS:8 * ROWS + META, :].astype(F32)
        for n in range(8):
            select = jnp.where(same_row & (codes[n:n + 1, :] == want), 1.0, 0.0).astype(BF16)
            block = range_of(sc, n >> 1, outer, n & 1)
            for part in range(2):
                at = n * ROWS + part * HALF
                pages = jnp.dot(select, ref[at:at + HALF, :], preferred_element_type=F32)
                out_ref[block, :, part * HD:(part + 1) * HD] = pages.astype(BF16)


VMEM_SPEC = pl.BlockSpec(memory_space=pltpu.VMEM)
SMEM_SPEC = pl.BlockSpec(memory_space=pltpu.SMEM)


def call(kernel, out_shape, scratch, flops, sc, *args):
    many = isinstance(out_shape, tuple)
    specs = ([SMEM_SPEC] if sc is not None else []) + [VMEM_SPEC] * len(args)
    operands = ([sc] if sc is not None else []) + list(args)
    return pl.pallas_call(
        kernel,
        out_shape=out_shape,
        in_specs=specs,
        out_specs=(VMEM_SPEC,) * len(out_shape) if many else VMEM_SPEC,
        scratch_shapes=scratch,
        compiler_params=pltpu.CompilerParams(vmem_limit_bytes=16 * 1024 * 1024),
        cost_estimate=pl.CostEstimate(flops=flops, bytes_accessed=4 << 20, transcendentals=flops // 512),
    )(*operands)


def keys(rows):
    return [pltpu.VMEM((rows, 2 * HD), BF16), pltpu.VMEM((rows, 2 * HD), BF16)]


def shards(q, k, v, head_kind, page_owner):
    c = lax.axis_index("ctx")
    tp = lax.axis_index("tp")
    x, z, y = c // 8, (c // 4) % 2, c % 4
    core = tp % 2
    is_r = lax.dynamic_index_in_dim(head_kind, tp, 0, keepdims=False) == 1
    sc = jnp.stack([x, y, z, core, c, is_r.astype(jnp.int32), tp, tp]).astype(jnp.int32)

    low = jnp.concatenate([k[:HALF], v[:HALF]])
    high = jnp.concatenate([k[HALF:], v[HALF:]])
    stay = jnp.where(core == 0, low, high)
    came = lax.ppermute(jnp.where(core == 0, high, low), "tp", CORE_SWAP)
    q_other = lax.ppermute(q, "tp", CORE_SWAP)
    ret = jnp.where(is_r, stay, came)
    pas = jnp.where(is_r, came, stay)

    earlier = lax.iota(jnp.int32, 16)[None, :] < lax.iota(jnp.int32, 16)[:, None]
    rank = jnp.sum(((page_owner[:, None] == page_owner[None, :]) & earlier).astype(jnp.int32), axis=1)
    code = page_owner * 2 + rank
    code = jnp.where(core == 0, code[:8], code[8:]).astype(BF16)
    meta = jnp.broadcast_to(jnp.repeat(code, PAGE)[None, :], (META, HD))

    theirs = lax.ppermute(jnp.concatenate([ret, pas, meta]), "ctx", Z_SWAP)
    theirs, q_other = lax.optimization_barrier((theirs, q_other))
    from_x = lax.ppermute(theirs[ROWS:2 * ROWS], "ctx", X_STEP)
    both = jnp.concatenate([ret, theirs[:ROWS]])
    low = jnp.where(z == 0, pas, theirs[ROWS:2 * ROWS])
    sink = jnp.concatenate([low[:SINK], low[HALF:HALF + SINK]])
    line = iota((META, HD), 0)
    meta = jnp.where((line & 1) == 0, meta, theirs[2 * ROWS:])

    axes = ("ctx", "tp")
    message = jnp.concatenate([both, sink, meta])
    got = {s: lax.ppermute(message, axes, STAGE_1[s]) for s in (1, 3, 2)}
    pas, from_x, got[1] = lax.optimization_barrier((pas, from_x, got[1]))
    far = jnp.where(z == 1, theirs[ROWS:2 * ROWS], from_x)
    p = {s: lax.ppermute(jnp.where(y + s < 4, pas, far), "ctx", Y_SHIFT[s]) for s in (1, 3, 2)}

    for s in (1, 2, 3):
        meta = jnp.where((line >> 1) == s, got[s][2 * ROWS + 2 * SINK:], meta)
        sink = jnp.where(y == s, got[s][2 * ROWS:2 * ROWS + 2 * SINK], sink)
    message = jnp.concatenate([both] + [got[s][:2 * ROWS] for s in (1, 2, 3)] + [meta, sink])

    r = {0: message} | {s: lax.ppermute(message, axes, STAGE_2[s]) for s in (1, 3, 2)}
    state = (jax.ShapeDtypeStruct((GROUP, ROWS, HD), F32),) * 2
    unit = 2 * 2048 * 256 * 512
    now_ml, now_o = call(near_kernel, state, keys(8 * HALF), 4 * unit, sc, q, q_other, message)
    for s in (1, 2, 3):
        sink = jnp.where(x == s, r[s][8 * ROWS + META:], sink)
    sc_l, now_ml = lax.optimization_barrier((sc, now_ml))
    pages = call(
        pages_kernel, jax.ShapeDtypeStruct((32, 2 * PAGE, 2 * HD), BF16), [], unit // 4,
        sc_l, *[r[s] for s in range(4)])
    got_pages = lax.ppermute(pages, "tp", CORE_SWAP)
    keep, keep_lse, send = call(
        rest_kernel,
        (
            jax.ShapeDtypeStruct((ROWS, GROUP * HD), BF16),
            jax.ShapeDtypeStruct((ROWS, HD), F32),
            jax.ShapeDtypeStruct((ROWS, (GROUP + 1) * HD), BF16),
        ),
        keys(24 * HALF) + keys(6 * HALF) + [pltpu.VMEM((ROWS, HD), F32)],
        16 * unit, sc_l, q, q_other, r[1], r[3], r[2], sink, pas, p[1], p[2], p[3], far, now_ml, now_o)

    got = lax.ppermute(send, "tp", CORE_SWAP)
    attn_out = call(
        merge_kernel, jax.ShapeDtypeStruct((ROWS, GROUP * HD), BF16), [], unit // 4, None, keep, keep_lse, got)
    decode_cache = jnp.where(is_r, pages + got_pages, jnp.zeros((), BF16)).reshape(64, PAGE, 2 * HD)
    return attn_out, decode_cache


def solution(mesh):
    return jax.shard_map(
        shards,
        mesh=mesh,
        in_specs=(P("ctx", "tp"), P("ctx", "tp"), P("ctx", "tp"), P(), P("ctx")),
        out_specs=(P("ctx", "tp"), P("ctx", None, "tp")),
        check_vma=False,
    )
```

```python
import math

import jax
import jax.numpy as jnp
from jax import lax
from jax.experimental import pallas as pl
from jax.experimental.pallas import tpu as pltpu
from jax.sharding import PartitionSpec as P

GROUP = 8
HD = 128
SINK = 64
RECENT = 1024
PAGE = 16
ROWS = 256
HALF = 128
META = 16
CHUNK = 512
WIDE = 2
NEG = -1e30
SCALE = math.log2(math.e) / math.sqrt(HD)
F32 = jnp.float32
BF16 = jnp.bfloat16


def ctx_of(x, z, y):
    return (x % 4) * 8 + (z % 2) * 4 + (y % 4)


CHIPS = [(x, z, y) for x in range(4) for z in range(2) for y in range(4)]
CORE_SWAP = [(i, i ^ 1) for i in range(8)]
Z_SWAP = [(ctx_of(x, z, y), ctx_of(x, z + 1, y)) for x, z, y in CHIPS]
X_STEP = [(ctx_of(x, 0, y), ctx_of(x + 1, 0, y)) for x in range(3) for y in range(4)]
Y_SHIFT = {s: [(ctx_of(x, z, y), ctx_of(x, z, y + s)) for x, z, y in CHIPS] for s in (1, 2, 3)}


def two_ways(s, along_y):
    pairs = []
    for x, z, y in CHIPS:
        for tp in range(8):
            there = ctx_of(x, z, y + s) if tp % 2 == along_y else ctx_of(x + s, z, y)
            pairs.append((ctx_of(x, z, y) * 8 + tp, there * 8 + tp))
    return pairs


STAGE_1 = {s: two_ways(s, 0) for s in (1, 2, 3)}
STAGE_2 = {s: two_ways(s, 1) for s in (1, 2, 3)}


def nt_dot(a, b):
    return lax.dot_general(a, b, (((1,), (1,)), ((), ())), preferred_element_type=F32)


def iota(shape, axis):
    return lax.broadcasted_iota(jnp.int32, shape, axis)


def fold(state, q, k, v, left=None, right=None):
    s = nt_dot(q, k)
    if left is not None:
        s = jnp.concatenate([s[:, :HD] + left, s[:, HD:]], axis=1) if s.shape[1] > HD else s + left
    if right is not None:
        s = jnp.concatenate([s[:, :-HD], s[:, -HD:] + right], axis=1)
    high = jnp.max(s, axis=1, keepdims=True)
    top = jnp.broadcast_to(high, (ROWS, HD)) if state is None else jnp.maximum(state[0], high)
    p = jnp.exp2((s - jnp.concatenate([top] * (s.shape[1] // HD), axis=1)) * SCALE).astype(BF16)
    up = jnp.dot(p, v, preferred_element_type=F32)
    if state is None:
        return top, up[:, HD:], up[:, :HD]
    keep = jnp.exp2((state[0] - top) * SCALE)
    return top, state[1] * keep + up[:, HD:], state[2] * keep + up[:, :HD]


def put_keys(k_s, v_s, at, ref, first, rows, gap):
    k_s[pl.ds(at, rows), 0:HD] = ref[first:first + rows, :]
    v_s[pl.ds(at, rows), 0:HD] = ref[first + gap:first + gap + rows, :]


def put_ranges(k_s, v_s, at, ref):
    for n in range(8):
        put_keys(k_s, v_s, at + n * HALF, ref, n * ROWS, HALF, HALF)


def range_of(sc, inner, outer, far):
    x, y, z, core = sc[0], sc[1], sc[2], sc[3]
    dx = jnp.where(core == 0, outer, inner)
    dy = jnp.where(core == 0, inner, outer)
    zz = jnp.where(far == 0, z, 1 - z)
    return ((x - dx) & 3) * 8 + zz * 4 + ((y - dy) & 3)


def put_range_bias(k_s, v_s, sc, outers):
    first = jnp.where(iota((HALF, HD), 1) == 0, 1.0, 0.0)
    for i, outer in enumerate(outers):
        for n in range(8):
            bias = jnp.where(range_of(sc, n >> 1, outer, n & 1) <= sc[4], 0.0, NEG)
            k_s[pl.ds((i * 8 + n) * HALF, HALF), HD:] = (first * bias).astype(BF16)
    v_s[:, HD:] = jnp.ones((len(outers) * 8 * HALF, HD), BF16)


def put_slot_bias(k_s, v_s, biases):
    first = jnp.where(iota((HALF, HD), 1) == 0, 1.0, 0.0)
    for i, bias in enumerate(biases):
        k_s[pl.ds(i * HALF, HALF), HD:] = (first * bias).astype(BF16)
    v_s[:, HD:] = jnp.ones((len(biases) * HALF, HD), BF16)


def load_head(q_a, q_b, flag, a):
    cols = slice(a * HD, (a + 1) * HD)
    q = jnp.where(flag == 1, q_a[:, cols], q_b[:, cols])
    one = jnp.where(iota((ROWS, HD), 1) == 0, 1.0, 0.0).astype(BF16)
    return jnp.concatenate([q, one], axis=1)


def pack(m, l):
    return jnp.where(iota((ROWS, HD), 1) < HD // 2, m, l)


def unpack(both):
    low = iota((ROWS, HD), 1) < HD // 2
    turned = pltpu.roll(both, HD // 2, 1)
    return jnp.where(low, both, turned), jnp.where(low, turned, both)


def near_kernel(sc, q_own, q_other, here, pas, p1, p2, p3, far, mlp_out, op_out, ml_out, o_out, kp, vp, kr, vr):
    core, c, is_r = sc[3], sc[4], sc[5]
    put_ranges(kr, vr, 0, here)
    put_range_bias(kr, vr, sc, (0,))
    for n, ref in enumerate((pas, p1, p2, p3, far)):
        put_keys(kp, vp, n * HALF, ref, 0, HALF, HALF)
    put_slot_bias(kp, vp, [jnp.where(n <= c, 0.0, NEG) for n in range(5)])
    row = iota((ROWS, HD), 0)
    key = core * HALF + iota((ROWS, HD), 1)
    own = jnp.where(key > row, NEG, 0.0)
    edge = jnp.where(key <= row, NEG, 0.0)

    def heads(i):
        at = [WIDE * i + u for u in range(WIDE)]
        qp = [load_head(q_other, q_own, is_r, a) for a in at]
        q = [load_head(q_own, q_other, is_r, a) for a in at]
        sr = [fold(None, q[u], kr[0:CHUNK, :], vr[0:CHUNK, :], left=own) for u in range(WIDE)]
        sp = [fold(None, qp[u], kp[0:3 * HALF, :], vp[0:3 * HALF, :], left=own) for u in range(WIDE)]
        sr = [fold(sr[u], q[u], kr[CHUNK:, :], vr[CHUNK:, :]) for u in range(WIDE)]
        sp = [fold(sp[u], qp[u], kp[3 * HALF:, :], vp[3 * HALF:, :], right=edge) for u in range(WIDE)]
        for u in range(WIDE):
            ml_out[at[u]], o_out[at[u]] = pack(*sr[u][:2]), sr[u][2]
            mlp_out[at[u]], op_out[at[u]] = pack(*sp[u][:2]), sp[u][2]

    for i in range(GROUP // WIDE):
        heads(i)


def finish(state):
    m, l, o = state
    return o / l, m * SCALE + jnp.log2(l)


def rest_kernel(sc, q_own, q_other, r1, r3, r2, sink, mlp_in, op_in, ml_in, o_in, keep, keep_lse, send,
                kr, vr, ks, vs, lse_s):
    core, c, is_r = sc[3], sc[4], sc[5]
    for n, ref in enumerate((r1, r3, r2)):
        put_ranges(kr, vr, n * 8 * HALF, ref)
    put_range_bias(kr, vr, sc, (1, 3, 2))
    ks[...] = jnp.zeros((HALF, 2 * HD), BF16)
    vs[...] = jnp.zeros((HALF, 2 * HD), BF16)
    put_keys(ks, vs, 0, sink, 0, SINK, SINK)
    put_slot_bias(ks, vs, [0.0])
    row = iota((ROWS, HD), 0)
    lane = iota((ROWS, HD), 1)
    seen = (core == 0) & (lane < SINK) & (c * ROWS + row - lane >= RECENT)
    sink_bias = jnp.where(seen, 0.0, NEG)
    lse_s[...] = jnp.zeros((ROWS, HD), F32)
    keep_lse[...] = jnp.zeros((ROWS, HD), F32)

    def heads(i):
        at = [WIDE * i + u for u in range(WIDE)]
        qp = [load_head(q_other, q_own, is_r, a) for a in at]
        qr = [load_head(q_own, q_other, is_r, a) for a in at]
        sr = [(*unpack(ml_in[a]), o_in[a]) for a in at]
        sp = [(*unpack(mlp_in[a]), op_in[a]) for a in at]
        for n in range(6):
            rows = slice(n * CHUNK, (n + 1) * CHUNK)
            sr = [fold(sr[u], qr[u], kr[rows, :], vr[rows, :]) for u in range(WIDE)]
            if n == 2:
                sp = [fold(sp[u], qp[u], ks[...], vs[...], left=sink_bias) for u in range(WIDE)]
        for u in range(WIDE):
            cols = slice(at[u] * HD, (at[u] + 1) * HD)
            out_r, lse_r = finish(sr[u])
            out_p, lse_p = finish(sp[u])
            keep[:, cols] = jnp.where(is_r == 1, out_r, out_p).astype(BF16)
            send[:, cols] = jnp.where(is_r == 1, out_p, out_r).astype(BF16)
            keep_lse[...] = jnp.where(lane == at[u], jnp.where(is_r == 1, lse_r, lse_p), keep_lse[...])
            lse_s[...] = jnp.where(lane == at[u], jnp.where(is_r == 1, lse_p, lse_r), lse_s[...])

    for i in range(GROUP // WIDE):
        heads(i)
    lse = lse_s[...]
    high = lse.astype(BF16).astype(F32)
    mid = (lse - high).astype(BF16).astype(F32)
    low = lse - high - mid
    parts = high + pltpu.roll(mid, GROUP, 1) + pltpu.roll(low, 2 * GROUP, 1)
    send[:, GROUP * HD:] = parts.astype(BF16)


def merge_kernel(keep, keep_lse, got, out_ref):
    ext = got[:, GROUP * HD:].astype(F32)
    lse = ext + pltpu.roll(ext, HD - GROUP, 1) + pltpu.roll(ext, HD - 2 * GROUP, 1)
    lane = iota((ROWS, HD), 1)
    gap = jnp.where(lane < GROUP, lse - keep_lse[...], 0.0)
    weight = 1.0 / (1.0 + jnp.exp2(jnp.clip(gap, -126.0, 126.0)))
    for a in range(GROUP):
        cols = slice(a * HD, (a + 1) * HD)
        w = weight[:, a:a + 1]
        mine, theirs = keep[:, cols].astype(F32), got[:, cols].astype(F32)
        out_ref[:, cols] = (theirs + w * (mine - theirs)).astype(BF16)


def pages_kernel(sc, r0, r1, r2, r3, out_ref):
    c = sc[4]
    row = iota((2 * PAGE, HD), 0)
    lane = iota((2 * PAGE, HD), 1)
    same_row = (lane & (PAGE - 1)) == (row & (PAGE - 1))
    want = (2 * c + (row >> 4)).astype(F32)
    for outer, ref in enumerate((r0, r1, r2, r3)):
        codes = ref[8 * ROWS:8 * ROWS + META, :].astype(F32)
        for n in range(8):
            select = jnp.where(same_row & (codes[n:n + 1, :] == want), 1.0, 0.0).astype(BF16)
            block = range_of(sc, n >> 1, outer, n & 1)
            for part in range(2):
                at = n * ROWS + part * HALF
                pages = jnp.dot(select, ref[at:at + HALF, :], preferred_element_type=F32)
                out_ref[block, :, part * HD:(part + 1) * HD] = pages.astype(BF16)


VMEM_SPEC = pl.BlockSpec(memory_space=pltpu.VMEM)
SMEM_SPEC = pl.BlockSpec(memory_space=pltpu.SMEM)


def call(kernel, out_shape, scratch, flops, sc, *args):
    many = isinstance(out_shape, tuple)
    specs = ([SMEM_SPEC] if sc is not None else []) + [VMEM_SPEC] * len(args)
    operands = ([sc] if sc is not None else []) + list(args)
    return pl.pallas_call(
        kernel,
        out_shape=out_shape,
        in_specs=specs,
        out_specs=(VMEM_SPEC,) * len(out_shape) if many else VMEM_SPEC,
        scratch_shapes=scratch,
        compiler_params=pltpu.CompilerParams(vmem_limit_bytes=16 * 1024 * 1024),
        cost_estimate=pl.CostEstimate(flops=flops, bytes_accessed=4 << 20, transcendentals=flops // 512),
    )(*operands)


def keys(rows):
    return [pltpu.VMEM((rows, 2 * HD), BF16), pltpu.VMEM((rows, 2 * HD), BF16)]


def shards(q, k, v, head_kind, page_owner):
    c = lax.axis_index("ctx")
    tp = lax.axis_index("tp")
    x, z, y = c // 8, (c // 4) % 2, c % 4
    core = tp % 2
    is_r = lax.dynamic_index_in_dim(head_kind, tp, 0, keepdims=False) == 1
    sc = jnp.stack([x, y, z, core, c, is_r.astype(jnp.int32), tp, tp]).astype(jnp.int32)

    low = jnp.concatenate([k[:HALF], v[:HALF]])
    high = jnp.concatenate([k[HALF:], v[HALF:]])
    stay = jnp.where(core == 0, low, high)
    came = lax.ppermute(jnp.where(core == 0, high, low), "tp", CORE_SWAP)
    q_other = lax.ppermute(q, "tp", CORE_SWAP)
    ret = jnp.where(is_r, stay, came)
    pas = jnp.where(is_r, came, stay)

    earlier = lax.iota(jnp.int32, 16)[None, :] < lax.iota(jnp.int32, 16)[:, None]
    rank = jnp.sum(((page_owner[:, None] == page_owner[None, :]) & earlier).astype(jnp.int32), axis=1)
    code = page_owner * 2 + rank
    code = jnp.where(core == 0, code[:8], code[8:]).astype(BF16)
    meta = jnp.broadcast_to(jnp.repeat(code, PAGE)[None, :], (META, HD))

    theirs = lax.ppermute(jnp.concatenate([ret, pas, meta]), "ctx", Z_SWAP)
    theirs, q_other = lax.optimization_barrier((theirs, q_other))
    from_x = lax.ppermute(theirs[ROWS:2 * ROWS], "ctx", X_STEP)
    both = jnp.concatenate([ret, theirs[:ROWS]])
    low = jnp.where(z == 0, pas, theirs[ROWS:2 * ROWS])
    sink = jnp.concatenate([low[:SINK], low[HALF:HALF + SINK]])
    line = iota((META, HD), 0)
    meta = jnp.where((line & 1) == 0, meta, theirs[2 * ROWS:])

    axes = ("ctx", "tp")
    message = jnp.concatenate([both, sink, meta])
    got = {s: lax.ppermute(message, axes, STAGE_1[s]) for s in (1, 3, 2)}
    pas, from_x, got[1] = lax.optimization_barrier((pas, from_x, got[1]))
    far = jnp.where(z == 1, theirs[ROWS:2 * ROWS], from_x)
    p = {s: lax.ppermute(jnp.where(y + s < 4, pas, far), "ctx", Y_SHIFT[s]) for s in (1, 3, 2)}

    for s in (1, 2, 3):
        meta = jnp.where((line >> 1) == s, got[s][2 * ROWS + 2 * SINK:], meta)
        sink = jnp.where(y == s, got[s][2 * ROWS:2 * ROWS + 2 * SINK], sink)
    message = jnp.concatenate([both] + [got[s][:2 * ROWS] for s in (1, 2, 3)] + [meta, sink])

    r = {0: message} | {s: lax.ppermute(message, axes, STAGE_2[s]) for s in (1, 3, 2)}
    state = (jax.ShapeDtypeStruct((GROUP, ROWS, HD), F32),) * 2
    unit = 2 * 2048 * 256 * 512
    *now_p, now_ml, now_o = call(
        near_kernel, state + state, keys(5 * HALF) + keys(8 * HALF), 60 * unit,
        sc, q, q_other, message, pas, p[1], p[2], p[3], far)
    for s in (1, 2, 3):
        sink = jnp.where(x == s, r[s][8 * ROWS + META:], sink)
    sc_l, now_ml = lax.optimization_barrier((sc, now_ml))
    pages = call(
        pages_kernel, jax.ShapeDtypeStruct((32, 2 * PAGE, 2 * HD), BF16), [], unit // 4,
        sc_l, *[r[s] for s in range(4)])
    got_pages = lax.ppermute(pages, "tp", CORE_SWAP)
    keep, keep_lse, send = call(
        rest_kernel,
        (
            jax.ShapeDtypeStruct((ROWS, GROUP * HD), BF16),
            jax.ShapeDtypeStruct((ROWS, HD), F32),
            jax.ShapeDtypeStruct((ROWS, (GROUP + 1) * HD), BF16),
        ),
        keys(24 * HALF) + keys(HALF) + [pltpu.VMEM((ROWS, HD), F32)],
        13 * unit, sc_l, q, q_other, r[1], r[3], r[2], sink, *now_p, now_ml, now_o)

    got = lax.ppermute(send, "tp", CORE_SWAP)
    attn_out = call(
        merge_kernel, jax.ShapeDtypeStruct((ROWS, GROUP * HD), BF16), [], unit // 4, None, keep, keep_lse, got)
    decode_cache = jnp.where(is_r, pages + got_pages, jnp.zeros((), BF16)).reshape(64, PAGE, 2 * HD)
    return attn_out, decode_cache


def solution(mesh):
    return jax.shard_map(
        shards,
        mesh=mesh,
        in_specs=(P("ctx", "tp"), P("ctx", "tp"), P("ctx", "tp"), P(), P("ctx")),
        out_specs=(P("ctx", "tp"), P("ctx", None, "tp")),
        check_vma=False,
    )
```

```python
import math

import jax
import jax.numpy as jnp
from jax import lax
from jax.experimental import pallas as pl
from jax.experimental.pallas import tpu as pltpu
from jax.sharding import PartitionSpec as P

GROUP = 8
HD = 128
SINK = 64
RECENT = 1024
PAGE = 16
ROWS = 256
HALF = 128
META = 16
CHUNK = 512
WIDE = 2
NEG = -1e30
SCALE = math.log2(math.e) / math.sqrt(HD)
F32 = jnp.float32
BF16 = jnp.bfloat16


def ctx_of(x, z, y):
    return (x % 4) * 8 + (z % 2) * 4 + (y % 4)


CHIPS = [(x, z, y) for x in range(4) for z in range(2) for y in range(4)]
CORE_SWAP = [(i, i ^ 1) for i in range(8)]
Z_SWAP = [(ctx_of(x, z, y), ctx_of(x, z + 1, y)) for x, z, y in CHIPS]
X_STEP = [(ctx_of(x, 0, y), ctx_of(x + 1, 0, y)) for x in range(3) for y in range(4)]
Y_SHIFT = {s: [(ctx_of(x, z, y), ctx_of(x, z, y + s)) for x, z, y in CHIPS] for s in (1, 2, 3)}


def two_ways(s, along_y):
    pairs = []
    for x, z, y in CHIPS:
        for tp in range(8):
            there = ctx_of(x, z, y + s) if tp % 2 == along_y else ctx_of(x + s, z, y)
            pairs.append((ctx_of(x, z, y) * 8 + tp, there * 8 + tp))
    return pairs


STAGE_1 = {s: two_ways(s, 0) for s in (1, 2, 3)}
STAGE_2 = {s: two_ways(s, 1) for s in (1, 2, 3)}


def nt_dot(a, b):
    return lax.dot_general(a, b, (((1,), (1,)), ((), ())), preferred_element_type=F32)


def iota(shape, axis):
    return lax.broadcasted_iota(jnp.int32, shape, axis)


def fold(state, q, k, v, left=None, right=None):
    s = nt_dot(q, k)
    if left is not None:
        s = jnp.concatenate([s[:, :HD] + left, s[:, HD:]], axis=1) if s.shape[1] > HD else s + left
    if right is not None:
        s = jnp.concatenate([s[:, :-HD], s[:, -HD:] + right], axis=1)
    high = jnp.max(s, axis=1, keepdims=True)
    top = jnp.broadcast_to(high, (ROWS, HD)) if state is None else jnp.maximum(state[0], high)
    p = jnp.exp2((s - jnp.concatenate([top] * (s.shape[1] // HD), axis=1)) * SCALE).astype(BF16)
    up = jnp.dot(p, v, preferred_element_type=F32)
    if state is None:
        return top, up[:, HD:], up[:, :HD]
    keep = jnp.exp2((state[0] - top) * SCALE)
    return top, state[1] * keep + up[:, HD:], state[2] * keep + up[:, :HD]


def put_keys(k_s, v_s, at, ref, first, rows, gap):
    k_s[pl.ds(at, rows), 0:HD] = ref[first:first + rows, :]
    v_s[pl.ds(at, rows), 0:HD] = ref[first + gap:first + gap + rows, :]


def put_ranges(k_s, v_s, at, ref):
    for n in range(8):
        put_keys(k_s, v_s, at + n * HALF, ref, n * ROWS, HALF, HALF)


def range_of(sc, inner, outer, far):
    x, y, z, core = sc[0], sc[1], sc[2], sc[3]
    dx = jnp.where(core == 0, outer, inner)
    dy = jnp.where(core == 0, inner, outer)
    zz = jnp.where(far == 0, z, 1 - z)
    return ((x - dx) & 3) * 8 + zz * 4 + ((y - dy) & 3)


def put_range_bias(k_s, v_s, sc, outers):
    first = jnp.where(iota((HALF, HD), 1) == 0, 1.0, 0.0)
    for i, outer in enumerate(outers):
        for n in range(8):
            bias = jnp.where(range_of(sc, n >> 1, outer, n & 1) <= sc[4], 0.0, NEG)
            k_s[pl.ds((i * 8 + n) * HALF, HALF), HD:] = (first * bias).astype(BF16)
    v_s[:, HD:] = jnp.ones((len(outers) * 8 * HALF, HD), BF16)


def put_slot_bias(k_s, v_s, biases):
    first = jnp.where(iota((HALF, HD), 1) == 0, 1.0, 0.0)
    for i, bias in enumerate(biases):
        k_s[pl.ds(i * HALF, HALF), HD:] = (first * bias).astype(BF16)
    v_s[:, HD:] = jnp.ones((len(biases) * HALF, HD), BF16)


def load_head(q_a, q_b, flag, a):
    cols = slice(a * HD, (a + 1) * HD)
    q = jnp.where(flag == 1, q_a[:, cols], q_b[:, cols])
    one = jnp.where(iota((ROWS, HD), 1) == 0, 1.0, 0.0).astype(BF16)
    return jnp.concatenate([q, one], axis=1)


def pack(m, l):
    return jnp.where(iota((ROWS, HD), 1) < HD // 2, m, l)


def unpack(both):
    low = iota((ROWS, HD), 1) < HD // 2
    turned = pltpu.roll(both, HD // 2, 1)
    return jnp.where(low, both, turned), jnp.where(low, turned, both)


def near_kernel(sc, q_own, q_other, here, pas, p1, p2, p3, far, mlp_out, op_out, ml_out, o_out, kp, vp, kr, vr):
    core, c, is_r = sc[3], sc[4], sc[5]
    put_ranges(kr, vr, 0, here)
    put_range_bias(kr, vr, sc, (0,))
    for n, ref in enumerate((pas, p1, p2, p3, far)):
        put_keys(kp, vp, n * HALF, ref, 0, HALF, HALF)
    put_slot_bias(kp, vp, [jnp.where(n <= c, 0.0, NEG) for n in range(5)])
    row = iota((ROWS, HD), 0)
    key = core * HALF + iota((ROWS, HD), 1)
    own = jnp.where(key > row, NEG, 0.0)
    edge = jnp.where(key <= row, NEG, 0.0)

    def heads(i):
        at = [WIDE * i + u for u in range(WIDE)]
        qp = [load_head(q_other, q_own, is_r, a) for a in at]
        q = [load_head(q_own, q_other, is_r, a) for a in at]
        sr = [fold(None, q[u], kr[0:CHUNK, :], vr[0:CHUNK, :], left=own) for u in range(WIDE)]
        sp = [fold(None, qp[u], kp[0:3 * HALF, :], vp[0:3 * HALF, :], left=own) for u in range(WIDE)]
        sr = [fold(sr[u], q[u], kr[CHUNK:, :], vr[CHUNK:, :]) for u in range(WIDE)]
        sp = [fold(sp[u], qp[u], kp[3 * HALF:, :], vp[3 * HALF:, :], right=edge) for u in range(WIDE)]
        for u in range(WIDE):
            ml_out[at[u]], o_out[at[u]] = pack(*sr[u][:2]), sr[u][2]
            mlp_out[at[u]], op_out[at[u]] = pack(*sp[u][:2]), sp[u][2]

    for i in range(GROUP // WIDE):
        heads(i)


def middle_kernel(sc, q_own, q_other, r1, r3, ml_in, o_in, ml_out, o_out, kr, vr):
    is_r = sc[5]
    put_ranges(kr, vr, 0, r1)
    put_ranges(kr, vr, 8 * HALF, r3)
    put_range_bias(kr, vr, sc, (1, 3))

    def heads(i):
        at = [WIDE * i + u for u in range(WIDE)]
        q = [load_head(q_own, q_other, is_r, a) for a in at]
        state = [(*unpack(ml_in[a]), o_in[a]) for a in at]
        for n in range(4):
            rows = slice(n * CHUNK, (n + 1) * CHUNK)
            state = [fold(state[u], q[u], kr[rows, :], vr[rows, :]) for u in range(WIDE)]
        for u in range(WIDE):
            ml_out[at[u]], o_out[at[u]] = pack(*state[u][:2]), state[u][2]

    for i in range(GROUP // WIDE):
        heads(i)


def last_kernel(sc, q_own, q_other, r2, sink, mlp_in, op_in, ml_in, o_in, keep, keep_ml, send,
                kr, vr, ks, vs, mlr_s, mlp_s):
    core, c, is_r = sc[3], sc[4], sc[5]
    put_ranges(kr, vr, 0, r2)
    put_range_bias(kr, vr, sc, (2,))
    ks[...] = jnp.zeros((HALF, 2 * HD), BF16)
    vs[...] = jnp.zeros((HALF, 2 * HD), BF16)
    put_keys(ks, vs, 0, sink, 0, SINK, SINK)
    put_slot_bias(ks, vs, [0.0])
    row = iota((ROWS, HD), 0)
    lane = iota((ROWS, HD), 1)
    seen = (core == 0) & (lane < SINK) & (c * ROWS + row - lane >= RECENT)
    sink_bias = jnp.where(seen, 0.0, NEG)
    mlr_s[...] = jnp.zeros((ROWS, HD), F32)
    mlp_s[...] = jnp.zeros((ROWS, HD), F32)

    def heads(i):
        at = [WIDE * i + u for u in range(WIDE)]
        qp = [load_head(q_other, q_own, is_r, a) for a in at]
        qr = [load_head(q_own, q_other, is_r, a) for a in at]
        sr = [(*unpack(ml_in[a]), o_in[a]) for a in at]
        sp = [(*unpack(mlp_in[a]), op_in[a]) for a in at]
        sr = [fold(sr[u], qr[u], kr[0:CHUNK, :], vr[0:CHUNK, :]) for u in range(WIDE)]
        sp = [fold(sp[u], qp[u], ks[...], vs[...], left=sink_bias) for u in range(WIDE)]
        sr = [fold(sr[u], qr[u], kr[CHUNK:, :], vr[CHUNK:, :]) for u in range(WIDE)]
        for u in range(WIDE):
            cols = slice(at[u] * HD, (at[u] + 1) * HD)
            keep[:, cols] = jnp.where(is_r == 1, sr[u][2], sp[u][2]).astype(BF16)
            send[:, cols] = jnp.where(is_r == 1, sp[u][2], sr[u][2]).astype(BF16)
            for ref, (m, l, _) in ((mlr_s, sr[u]), (mlp_s, sp[u])):
                ref[...] = jnp.where(lane == at[u], m, jnp.where(lane == at[u] + GROUP, l, ref[...]))

    for i in range(GROUP // WIDE):
        heads(i)
    keep_ml[...] = jnp.where(is_r == 1, mlr_s[...], mlp_s[...])
    ml = jnp.where(is_r == 1, mlp_s[...], mlr_s[...])
    high = ml.astype(BF16).astype(F32)
    mid = (ml - high).astype(BF16).astype(F32)
    low = ml - high - mid
    parts = high + pltpu.roll(mid, 2 * GROUP, 1) + pltpu.roll(low, 4 * GROUP, 1)
    send[:, GROUP * HD:] = parts.astype(BF16)


def merge_kernel(keep, keep_ml, got, out_ref):
    ext = got[:, GROUP * HD:].astype(F32)
    theirs = ext + pltpu.roll(ext, HD - 2 * GROUP, 1) + pltpu.roll(ext, HD - 4 * GROUP, 1)
    mine = keep_ml[...]
    used = iota((ROWS, HD), 1) < GROUP
    m0, m1 = jnp.where(used, mine, 0.0), jnp.where(used, theirs, 0.0)
    l0, l1 = pltpu.roll(mine, HD - GROUP, 1), pltpu.roll(theirs, HD - GROUP, 1)
    top = jnp.maximum(m0, m1)
    w0, w1 = jnp.exp2((m0 - top) * SCALE), jnp.exp2((m1 - top) * SCALE)
    scale = 1.0 / jnp.where(used, l0 * w0 + l1 * w1, 1.0)
    w0, w1 = w0 * scale, w1 * scale
    for a in range(GROUP):
        cols = slice(a * HD, (a + 1) * HD)
        out = keep[:, cols].astype(F32) * w0[:, a:a + 1] + got[:, cols].astype(F32) * w1[:, a:a + 1]
        out_ref[:, cols] = out.astype(BF16)


def pages_kernel(sc, r0, r1, r2, r3, out_ref):
    c = sc[4]
    row = iota((2 * PAGE, HD), 0)
    lane = iota((2 * PAGE, HD), 1)
    same_row = (lane & (PAGE - 1)) == (row & (PAGE - 1))
    want = (2 * c + (row >> 4)).astype(F32)
    for outer, ref in enumerate((r0, r1, r2, r3)):
        codes = ref[8 * ROWS:8 * ROWS + META, :].astype(F32)
        for n in range(8):
            select = jnp.where(same_row & (codes[n:n + 1, :] == want), 1.0, 0.0).astype(BF16)
            block = range_of(sc, n >> 1, outer, n & 1)
            for part in range(2):
                at = n * ROWS + part * HALF
                pages = jnp.dot(select, ref[at:at + HALF, :], preferred_element_type=F32)
                out_ref[block, :, part * HD:(part + 1) * HD] = pages.astype(BF16)


VMEM_SPEC = pl.BlockSpec(memory_space=pltpu.VMEM)
SMEM_SPEC = pl.BlockSpec(memory_space=pltpu.SMEM)


def call(kernel, out_shape, scratch, flops, sc, *args):
    many = isinstance(out_shape, tuple)
    specs = ([SMEM_SPEC] if sc is not None else []) + [VMEM_SPEC] * len(args)
    operands = ([sc] if sc is not None else []) + list(args)
    return pl.pallas_call(
        kernel,
        out_shape=out_shape,
        in_specs=specs,
        out_specs=(VMEM_SPEC,) * len(out_shape) if many else VMEM_SPEC,
        scratch_shapes=scratch,
        compiler_params=pltpu.CompilerParams(vmem_limit_bytes=16 * 1024 * 1024),
        cost_estimate=pl.CostEstimate(flops=flops, bytes_accessed=4 << 20, transcendentals=flops // 512),
    )(*operands)


def keys(rows):
    return [pltpu.VMEM((rows, 2 * HD), BF16), pltpu.VMEM((rows, 2 * HD), BF16)]


def shards(q, k, v, head_kind, page_owner):
    c = lax.axis_index("ctx")
    tp = lax.axis_index("tp")
    x, z, y = c // 8, (c // 4) % 2, c % 4
    core = tp % 2
    is_r = lax.dynamic_index_in_dim(head_kind, tp, 0, keepdims=False) == 1
    sc = jnp.stack([x, y, z, core, c, is_r.astype(jnp.int32), tp, tp]).astype(jnp.int32)

    low = jnp.concatenate([k[:HALF], v[:HALF]])
    high = jnp.concatenate([k[HALF:], v[HALF:]])
    stay = jnp.where(core == 0, low, high)
    came = lax.ppermute(jnp.where(core == 0, high, low), "tp", CORE_SWAP)
    q_other = lax.ppermute(q, "tp", CORE_SWAP)
    ret = jnp.where(is_r, stay, came)
    pas = jnp.where(is_r, came, stay)

    earlier = lax.iota(jnp.int32, 16)[None, :] < lax.iota(jnp.int32, 16)[:, None]
    rank = jnp.sum(((page_owner[:, None] == page_owner[None, :]) & earlier).astype(jnp.int32), axis=1)
    code = page_owner * 2 + rank
    code = jnp.where(core == 0, code[:8], code[8:]).astype(BF16)
    meta = jnp.broadcast_to(jnp.repeat(code, PAGE)[None, :], (META, HD))

    theirs = lax.ppermute(jnp.concatenate([ret, pas, meta]), "ctx", Z_SWAP)
    theirs, q_other = lax.optimization_barrier((theirs, q_other))
    from_x = lax.ppermute(theirs[ROWS:2 * ROWS], "ctx", X_STEP)
    both = jnp.concatenate([ret, theirs[:ROWS]])
    low = jnp.where(z == 0, pas, theirs[ROWS:2 * ROWS])
    sink = jnp.concatenate([low[:SINK], low[HALF:HALF + SINK]])
    line = iota((META, HD), 0)
    meta = jnp.where((line & 1) == 0, meta, theirs[2 * ROWS:])

    axes = ("ctx", "tp")
    message = jnp.concatenate([both, sink, meta])
    got = {s: lax.ppermute(message, axes, STAGE_1[s]) for s in (1, 3, 2)}
    pas, from_x, got[1] = lax.optimization_barrier((pas, from_x, got[1]))
    far = jnp.where(z == 1, theirs[ROWS:2 * ROWS], from_x)
    p = {s: lax.ppermute(jnp.where(y + s < 4, pas, far), "ctx", Y_SHIFT[s]) for s in (1, 3, 2)}

    for s in (1, 2, 3):
        meta = jnp.where((line >> 1) == s, got[s][2 * ROWS + 2 * SINK:], meta)
        sink = jnp.where(y == s, got[s][2 * ROWS:2 * ROWS + 2 * SINK], sink)
    message = jnp.concatenate([both] + [got[s][:2 * ROWS] for s in (1, 2, 3)] + [meta, sink])

    r = {0: message} | {s: lax.ppermute(message, axes, STAGE_2[s]) for s in (1, 3, 2)}
    state = (jax.ShapeDtypeStruct((GROUP, ROWS, HD), F32),) * 2
    unit = 2 * 2048 * 256 * 512
    *now_p, now_ml, now_o = call(
        near_kernel, state + state, keys(5 * HALF) + keys(8 * HALF), 60 * unit,
        sc, q, q_other, message, pas, p[1], p[2], p[3], far)
    for s in (1, 2, 3):
        sink = jnp.where(x == s, r[s][8 * ROWS + META:], sink)
    now_ml, now_o = call(
        middle_kernel, state, keys(16 * HALF), 8 * unit, sc, q, q_other, r[1], r[3], now_ml, now_o)
    sc_l, now_ml = lax.optimization_barrier((sc, now_ml))
    pages = call(
        pages_kernel, jax.ShapeDtypeStruct((32, 2 * PAGE, 2 * HD), BF16), [], unit // 4,
        sc_l, *[r[s] for s in range(4)])
    got_pages = lax.ppermute(pages, "tp", CORE_SWAP)
    keep, keep_ml, send = call(
        last_kernel,
        (
            jax.ShapeDtypeStruct((ROWS, GROUP * HD), BF16),
            jax.ShapeDtypeStruct((ROWS, HD), F32),
            jax.ShapeDtypeStruct((ROWS, (GROUP + 1) * HD), BF16),
        ),
        keys(8 * HALF) + keys(HALF) + [pltpu.VMEM((ROWS, HD), F32)] * 2,
        5 * unit, sc_l, q, q_other, r[2], sink, *now_p, now_ml, now_o)

    got = lax.ppermute(send, "tp", CORE_SWAP)
    attn_out = call(
        merge_kernel, jax.ShapeDtypeStruct((ROWS, GROUP * HD), BF16), [], unit // 4, None, keep, keep_ml, got)
    decode_cache = jnp.where(is_r, pages + got_pages, jnp.zeros((), BF16)).reshape(64, PAGE, 2 * HD)
    return attn_out, decode_cache


def solution(mesh):
    return jax.shard_map(
        shards,
        mesh=mesh,
        in_specs=(P("ctx", "tp"), P("ctx", "tp"), P("ctx", "tp"), P(), P("ctx")),
        out_specs=(P("ctx", "tp"), P("ctx", None, "tp")),
        check_vma=False,
    )
```

```python
import math

import jax
import jax.numpy as jnp
from jax import lax
from jax.experimental import pallas as pl
from jax.experimental.pallas import tpu as pltpu
from jax.sharding import PartitionSpec as P

GROUP = 8
HD = 128
SINK = 64
RECENT = 1024
PAGE = 16
ROWS = 256
HALF = 128
META = 16
CHUNK = 1024
WIDE = 2
NEG = -1e30
SCALE = math.log2(math.e) / math.sqrt(HD)
F32 = jnp.float32
BF16 = jnp.bfloat16


def ctx_of(x, z, y):
    return (x % 4) * 8 + (z % 2) * 4 + (y % 4)


CHIPS = [(x, z, y) for x in range(4) for z in range(2) for y in range(4)]
CORE_SWAP = [(i, i ^ 1) for i in range(8)]
Z_SWAP = [(ctx_of(x, z, y), ctx_of(x, z + 1, y)) for x, z, y in CHIPS]
X_STEP = [(ctx_of(x, 0, y), ctx_of(x + 1, 0, y)) for x in range(3) for y in range(4)]
Y_SHIFT = {s: [(ctx_of(x, z, y), ctx_of(x, z, y + s)) for x, z, y in CHIPS] for s in (1, 2, 3)}


def two_ways(s, along_y):
    pairs = []
    for x, z, y in CHIPS:
        for tp in range(8):
            there = ctx_of(x, z, y + s) if tp % 2 == along_y else ctx_of(x + s, z, y)
            pairs.append((ctx_of(x, z, y) * 8 + tp, there * 8 + tp))
    return pairs


STAGE_1 = {s: two_ways(s, 0) for s in (1, 2, 3)}
STAGE_2 = {s: two_ways(s, 1) for s in (1, 2, 3)}


def nt_dot(a, b):
    return lax.dot_general(a, b, (((1,), (1,)), ((), ())), preferred_element_type=F32)


def iota(shape, axis):
    return lax.broadcasted_iota(jnp.int32, shape, axis)


def fold(state, q, k, v, left=None, right=None):
    s = nt_dot(q, k)
    if left is not None:
        s = jnp.concatenate([s[:, :HD] + left, s[:, HD:]], axis=1) if s.shape[1] > HD else s + left
    if right is not None:
        s = jnp.concatenate([s[:, :-HD], s[:, -HD:] + right], axis=1)
    high = jnp.max(s, axis=1, keepdims=True)
    top = jnp.broadcast_to(high, (ROWS, HD)) if state is None else jnp.maximum(state[0], high)
    p = jnp.exp2((s - jnp.concatenate([top] * (s.shape[1] // HD), axis=1)) * SCALE).astype(BF16)
    up = jnp.dot(p, v, preferred_element_type=F32)
    if state is None:
        return top, up[:, HD:], up[:, :HD]
    keep = jnp.exp2((state[0] - top) * SCALE)
    return top, state[1] * keep + up[:, HD:], state[2] * keep + up[:, :HD]


def put_keys(k_s, v_s, at, ref, first, rows, gap):
    k_s[pl.ds(at, rows), 0:HD] = ref[first:first + rows, :]
    v_s[pl.ds(at, rows), 0:HD] = ref[first + gap:first + gap + rows, :]


def put_ranges(k_s, v_s, at, ref):
    for n in range(8):
        put_keys(k_s, v_s, at + n * HALF, ref, n * ROWS, HALF, HALF)


def range_of(sc, inner, outer, far):
    x, y, z, core = sc[0], sc[1], sc[2], sc[3]
    dx = jnp.where(core == 0, outer, inner)
    dy = jnp.where(core == 0, inner, outer)
    zz = jnp.where(far == 0, z, 1 - z)
    return ((x - dx) & 3) * 8 + zz * 4 + ((y - dy) & 3)


def put_range_bias(k_s, v_s, sc, outers):
    first = jnp.where(iota((HALF, HD), 1) == 0, 1.0, 0.0)
    for i, outer in enumerate(outers):
        for n in range(8):
            bias = jnp.where(range_of(sc, n >> 1, outer, n & 1) <= sc[4], 0.0, NEG)
            k_s[pl.ds((i * 8 + n) * HALF, HALF), HD:] = (first * bias).astype(BF16)
    v_s[:, HD:] = jnp.ones((len(outers) * 8 * HALF, HD), BF16)


def put_slot_bias(k_s, v_s, biases):
    first = jnp.where(iota((HALF, HD), 1) == 0, 1.0, 0.0)
    for i, bias in enumerate(biases):
        k_s[pl.ds(i * HALF, HALF), HD:] = (first * bias).astype(BF16)
    v_s[:, HD:] = jnp.ones((len(biases) * HALF, HD), BF16)


def load_head(q_a, q_b, flag, a):
    cols = slice(a * HD, (a + 1) * HD)
    q = jnp.where(flag == 1, q_a[:, cols], q_b[:, cols])
    one = jnp.where(iota((ROWS, HD), 1) == 0, 1.0, 0.0).astype(BF16)
    return jnp.concatenate([q, one], axis=1)


def near_kernel(sc, q_own, q_other, here, pas, p1, p2, p3, far, mp_out, lp_out, op_out,
                m_out, l_out, o_out, kp, vp, kr, vr):
    core, c, is_r = sc[3], sc[4], sc[5]
    put_ranges(kr, vr, 0, here)
    put_range_bias(kr, vr, sc, (0,))
    for n, ref in enumerate((pas, p1, p2, p3, far)):
        put_keys(kp, vp, n * HALF, ref, 0, HALF, HALF)
    put_slot_bias(kp, vp, [jnp.where(n <= c, 0.0, NEG) for n in range(5)])
    row = iota((ROWS, HD), 0)
    key = core * HALF + iota((ROWS, HD), 1)
    own = jnp.where(key > row, NEG, 0.0)
    edge = jnp.where(key <= row, NEG, 0.0)

    def heads(i):
        at = [WIDE * i + u for u in range(WIDE)]
        qp = [load_head(q_other, q_own, is_r, a) for a in at]
        q = [load_head(q_own, q_other, is_r, a) for a in at]
        sp = [fold(None, qp[u], kp[...], vp[...], left=own, right=edge) for u in range(WIDE)]
        sr = [fold(None, q[u], kr[...], vr[...], left=own) for u in range(WIDE)]
        for u in range(WIDE):
            m_out[at[u]], l_out[at[u]], o_out[at[u]] = sr[u]
            mp_out[at[u]], lp_out[at[u]], op_out[at[u]] = sp[u]

    for i in range(GROUP // WIDE):
        heads(i)


def middle_kernel(sc, q_own, q_other, r1, r3, m_in, l_in, o_in, m_out, l_out, o_out, kr, vr):
    is_r = sc[5]
    put_ranges(kr, vr, 0, r1)
    put_ranges(kr, vr, 8 * HALF, r3)
    put_range_bias(kr, vr, sc, (1, 3))

    def heads(i):
        at = [WIDE * i + u for u in range(WIDE)]
        q = [load_head(q_own, q_other, is_r, a) for a in at]
        state = [(m_in[a], l_in[a], o_in[a]) for a in at]
        for n in range(2):
            rows = slice(n * CHUNK, (n + 1) * CHUNK)
            state = [fold(state[u], q[u], kr[rows, :], vr[rows, :]) for u in range(WIDE)]
        for u in range(WIDE):
            m_out[at[u]], l_out[at[u]], o_out[at[u]] = state[u]

    for i in range(GROUP // WIDE):
        heads(i)


def last_kernel(sc, q_own, q_other, r2, sink, mp_in, lp_in, op_in, m_in, l_in, o_in, keep, keep_ml, send,
                kr, vr, ks, vs, mlr_s, mlp_s):
    core, c, is_r = sc[3], sc[4], sc[5]
    put_ranges(kr, vr, 0, r2)
    put_range_bias(kr, vr, sc, (2,))
    ks[...] = jnp.zeros((HALF, 2 * HD), BF16)
    vs[...] = jnp.zeros((HALF, 2 * HD), BF16)
    put_keys(ks, vs, 0, sink, 0, SINK, SINK)
    put_slot_bias(ks, vs, [0.0])
    row = iota((ROWS, HD), 0)
    lane = iota((ROWS, HD), 1)
    seen = (core == 0) & (lane < SINK) & (c * ROWS + row - lane >= RECENT)
    sink_bias = jnp.where(seen, 0.0, NEG)
    mlr_s[...] = jnp.zeros((ROWS, HD), F32)
    mlp_s[...] = jnp.zeros((ROWS, HD), F32)

    def heads(i):
        at = [WIDE * i + u for u in range(WIDE)]
        qp = [load_head(q_other, q_own, is_r, a) for a in at]
        qr = [load_head(q_own, q_other, is_r, a) for a in at]
        sr = [(m_in[a], l_in[a], o_in[a]) for a in at]
        sp = [(mp_in[a], lp_in[a], op_in[a]) for a in at]
        sp = [fold(sp[u], qp[u], ks[...], vs[...], left=sink_bias) for u in range(WIDE)]
        sr = [fold(sr[u], qr[u], kr[...], vr[...]) for u in range(WIDE)]
        for u in range(WIDE):
            cols = slice(at[u] * HD, (at[u] + 1) * HD)
            keep[:, cols] = jnp.where(is_r == 1, sr[u][2], sp[u][2]).astype(BF16)
            send[:, cols] = jnp.where(is_r == 1, sp[u][2], sr[u][2]).astype(BF16)
            for ref, (m, l, _) in ((mlr_s, sr[u]), (mlp_s, sp[u])):
                ref[...] = jnp.where(lane == at[u], m, jnp.where(lane == at[u] + GROUP, l, ref[...]))

    for i in range(GROUP // WIDE):
        heads(i)
    keep_ml[...] = jnp.where(is_r == 1, mlr_s[...], mlp_s[...])
    ml = jnp.where(is_r == 1, mlp_s[...], mlr_s[...])
    high = ml.astype(BF16).astype(F32)
    mid = (ml - high).astype(BF16).astype(F32)
    low = ml - high - mid
    parts = high + pltpu.roll(mid, 2 * GROUP, 1) + pltpu.roll(low, 4 * GROUP, 1)
    send[:, GROUP * HD:] = parts.astype(BF16)


def merge_kernel(keep, keep_ml, got, out_ref):
    ext = got[:, GROUP * HD:].astype(F32)
    theirs = ext + pltpu.roll(ext, HD - 2 * GROUP, 1) + pltpu.roll(ext, HD - 4 * GROUP, 1)
    mine = keep_ml[...]
    used = iota((ROWS, HD), 1) < GROUP
    m0, m1 = jnp.where(used, mine, 0.0), jnp.where(used, theirs, 0.0)
    l0, l1 = pltpu.roll(mine, HD - GROUP, 1), pltpu.roll(theirs, HD - GROUP, 1)
    top = jnp.maximum(m0, m1)
    w0, w1 = jnp.exp2((m0 - top) * SCALE), jnp.exp2((m1 - top) * SCALE)
    scale = 1.0 / jnp.where(used, l0 * w0 + l1 * w1, 1.0)
    w0, w1 = w0 * scale, w1 * scale
    for a in range(GROUP):
        cols = slice(a * HD, (a + 1) * HD)
        out = keep[:, cols].astype(F32) * w0[:, a:a + 1] + got[:, cols].astype(F32) * w1[:, a:a + 1]
        out_ref[:, cols] = out.astype(BF16)


def pages_kernel(sc, r0, r1, r2, r3, out_ref):
    c = sc[4]
    row = iota((2 * PAGE, HD), 0)
    lane = iota((2 * PAGE, HD), 1)
    same_row = (lane & (PAGE - 1)) == (row & (PAGE - 1))
    want = (2 * c + (row >> 4)).astype(F32)
    for outer, ref in enumerate((r0, r1, r2, r3)):
        codes = ref[8 * ROWS:8 * ROWS + META, :].astype(F32)
        for n in range(8):
            select = jnp.where(same_row & (codes[n:n + 1, :] == want), 1.0, 0.0).astype(BF16)
            block = range_of(sc, n >> 1, outer, n & 1)
            for part in range(2):
                at = n * ROWS + part * HALF
                pages = jnp.dot(select, ref[at:at + HALF, :], preferred_element_type=F32)
                out_ref[block, :, part * HD:(part + 1) * HD] = pages.astype(BF16)


VMEM_SPEC = pl.BlockSpec(memory_space=pltpu.VMEM)
SMEM_SPEC = pl.BlockSpec(memory_space=pltpu.SMEM)


def call(kernel, out_shape, scratch, flops, sc, *args):
    many = isinstance(out_shape, tuple)
    specs = ([SMEM_SPEC] if sc is not None else []) + [VMEM_SPEC] * len(args)
    operands = ([sc] if sc is not None else []) + list(args)
    return pl.pallas_call(
        kernel,
        out_shape=out_shape,
        in_specs=specs,
        out_specs=(VMEM_SPEC,) * len(out_shape) if many else VMEM_SPEC,
        scratch_shapes=scratch,
        compiler_params=pltpu.CompilerParams(vmem_limit_bytes=16 * 1024 * 1024),
        cost_estimate=pl.CostEstimate(flops=flops, bytes_accessed=4 << 20, transcendentals=flops // 512),
    )(*operands)


def keys(rows):
    return [pltpu.VMEM((rows, 2 * HD), BF16), pltpu.VMEM((rows, 2 * HD), BF16)]


def shards(q, k, v, head_kind, page_owner):
    c = lax.axis_index("ctx")
    tp = lax.axis_index("tp")
    x, z, y = c // 8, (c // 4) % 2, c % 4
    core = tp % 2
    is_r = jnp.sum(jnp.where(lax.iota(jnp.int32, head_kind.shape[0]) == tp, head_kind, 0)) == 1
    sc = jnp.stack([x, y, z, core, c, is_r.astype(jnp.int32), tp, tp]).astype(jnp.int32)

    low = jnp.concatenate([k[:HALF], v[:HALF]])
    high = jnp.concatenate([k[HALF:], v[HALF:]])
    stay = jnp.where(core == 0, low, high)
    came = lax.ppermute(jnp.where(core == 0, high, low), "tp", CORE_SWAP)
    q_other = lax.ppermute(q, "tp", CORE_SWAP)
    ret = jnp.where(is_r, stay, came)
    pas = jnp.where(is_r, came, stay)

    earlier = lax.iota(jnp.int32, 16)[None, :] < lax.iota(jnp.int32, 16)[:, None]
    rank = jnp.sum(((page_owner[:, None] == page_owner[None, :]) & earlier).astype(jnp.int32), axis=1)
    code = page_owner * 2 + rank
    code = jnp.where(core == 0, code[:8], code[8:]).astype(BF16)
    meta = jnp.broadcast_to(jnp.repeat(code, PAGE)[None, :], (META, HD))

    theirs = lax.ppermute(jnp.concatenate([ret, pas, meta]), "ctx", Z_SWAP)
    theirs, q_other = lax.optimization_barrier((theirs, q_other))
    from_x = lax.ppermute(theirs[ROWS:2 * ROWS], "ctx", X_STEP)
    both = jnp.concatenate([ret, theirs[:ROWS]])
    low = jnp.where(z == 0, pas, theirs[ROWS:2 * ROWS])
    sink = jnp.concatenate([low[:SINK], low[HALF:HALF + SINK]])
    line = iota((META, HD), 0)
    meta = jnp.where((line & 1) == 0, meta, theirs[2 * ROWS:])

    axes = ("ctx", "tp")
    message = jnp.concatenate([both, sink, meta])
    got = {s: lax.ppermute(message, axes, STAGE_1[s]) for s in (1, 3, 2)}
    pas, from_x, got[1] = lax.optimization_barrier((pas, from_x, got[1]))
    far = jnp.where(z == 1, theirs[ROWS:2 * ROWS], from_x)
    p = {s: lax.ppermute(jnp.where(y + s < 4, pas, far), "ctx", Y_SHIFT[s]) for s in (1, 3, 2)}

    for s in (1, 2, 3):
        meta = jnp.where((line >> 1) == s, got[s][2 * ROWS + 2 * SINK:], meta)
        sink = jnp.where(y == s, got[s][2 * ROWS:2 * ROWS + 2 * SINK], sink)
    message = jnp.concatenate([both] + [got[s][:2 * ROWS] for s in (1, 2, 3)] + [meta, sink])

    r = {0: message} | {s: lax.ppermute(message, axes, STAGE_2[s]) for s in (1, 3, 2)}
    state = (jax.ShapeDtypeStruct((GROUP, ROWS, HD), F32),) * 3
    unit = 2 * 2048 * 256 * 512
    *now_p, now_m, now_l, now_o = call(
        near_kernel, state + state, keys(5 * HALF) + keys(8 * HALF), 60 * unit,
        sc, q, q_other, message, pas, p[1], p[2], p[3], far)
    for s in (1, 2, 3):
        sink = jnp.where(x == s, r[s][8 * ROWS + META:], sink)
    now_m, now_l, now_o = call(
        middle_kernel, state, keys(16 * HALF), 8 * unit, sc, q, q_other, r[1], r[3], now_m, now_l, now_o)
    sc_l, now_m = lax.optimization_barrier((sc, now_m))
    pages = call(
        pages_kernel, jax.ShapeDtypeStruct((32, 2 * PAGE, 2 * HD), BF16), [], unit // 4,
        sc_l, *[r[s] for s in range(4)])
    got_pages = lax.ppermute(pages, "tp", CORE_SWAP)
    keep, keep_ml, send = call(
        last_kernel,
        (
            jax.ShapeDtypeStruct((ROWS, GROUP * HD), BF16),
            jax.ShapeDtypeStruct((ROWS, HD), F32),
            jax.ShapeDtypeStruct((ROWS, (GROUP + 1) * HD), BF16),
        ),
        keys(8 * HALF) + keys(HALF) + [pltpu.VMEM((ROWS, HD), F32)] * 2,
        5 * unit, sc_l, q, q_other, r[2], sink, *now_p, now_m, now_l, now_o)

    got = lax.ppermute(send, "tp", CORE_SWAP)
    attn_out = call(
        merge_kernel, jax.ShapeDtypeStruct((ROWS, GROUP * HD), BF16), [], unit // 4, None, keep, keep_ml, got)
    decode_cache = jnp.where(is_r, pages + got_pages, jnp.zeros((), BF16)).reshape(64, PAGE, 2 * HD)
    return attn_out, decode_cache


def solution(mesh):
    return jax.shard_map(
        shards,
        mesh=mesh,
        in_specs=(P("ctx", "tp"), P("ctx", "tp"), P("ctx", "tp"), P(), P("ctx")),
        out_specs=(P("ctx", "tp"), P("ctx", None, "tp")),
        check_vma=False,
    )
```

```python
import math

import jax
import jax.numpy as jnp
from jax import lax
from jax.experimental import pallas as pl
from jax.experimental.pallas import tpu as pltpu
from jax.sharding import PartitionSpec as P

GROUP = 8
HD = 128
SINK = 64
RECENT = 1024
PAGE = 16
ROWS = 256
HALF = 128
META = 16
CHUNK = 1024
WIDE = 2
NEG = -1e30
SCALE = math.log2(math.e) / math.sqrt(HD)
F32 = jnp.float32
BF16 = jnp.bfloat16


def ctx_of(x, z, y):
    return (x % 4) * 8 + (z % 2) * 4 + (y % 4)


CHIPS = [(x, z, y) for x in range(4) for z in range(2) for y in range(4)]
CORE_SWAP = [(i, i ^ 1) for i in range(8)]
Z_SWAP = [(ctx_of(x, z, y), ctx_of(x, z + 1, y)) for x, z, y in CHIPS]
X_STEP = [(ctx_of(x, 0, y), ctx_of(x + 1, 0, y)) for x in range(3) for y in range(4)]
Y_SHIFT = {s: [(ctx_of(x, z, y), ctx_of(x, z, y + s)) for x, z, y in CHIPS] for s in (1, 2, 3)}


def two_ways(s, along_y):
    pairs = []
    for x, z, y in CHIPS:
        for tp in range(8):
            there = ctx_of(x, z, y + s) if tp % 2 == along_y else ctx_of(x + s, z, y)
            pairs.append((ctx_of(x, z, y) * 8 + tp, there * 8 + tp))
    return pairs


STAGE_1 = {s: two_ways(s, 0) for s in (1, 2, 3)}
STAGE_2 = {s: two_ways(s, 1) for s in (1, 2, 3)}


def nt_dot(a, b):
    return lax.dot_general(a, b, (((1,), (1,)), ((), ())), preferred_element_type=F32)


def iota(shape, axis):
    return lax.broadcasted_iota(jnp.int32, shape, axis)


def fold(state, q, k, v, left=None, right=None):
    s = nt_dot(q, k)
    if left is not None:
        s = jnp.concatenate([s[:, :HD] + left, s[:, HD:]], axis=1) if s.shape[1] > HD else s + left
    if right is not None:
        s = jnp.concatenate([s[:, :-HD], s[:, -HD:] + right], axis=1)
    high = jnp.max(s, axis=1, keepdims=True)
    top = jnp.broadcast_to(high, (ROWS, HD)) if state is None else jnp.maximum(state[0], high)
    p = jnp.exp2((s - jnp.concatenate([top] * (s.shape[1] // HD), axis=1)) * SCALE).astype(BF16)
    up = jnp.dot(p, v, preferred_element_type=F32)
    if state is None:
        return top, up[:, HD:], up[:, :HD]
    keep = jnp.exp2((state[0] - top) * SCALE)
    return top, state[1] * keep + up[:, HD:], state[2] * keep + up[:, :HD]


def put_keys(k_s, v_s, at, ref, first, rows, gap):
    k_s[pl.ds(at, rows), 0:HD] = ref[first:first + rows, :]
    v_s[pl.ds(at, rows), 0:HD] = ref[first + gap:first + gap + rows, :]


def put_ranges(k_s, v_s, at, ref, count=8):
    for n in range(count):
        put_keys(k_s, v_s, at + n * HALF, ref, n * ROWS, HALF, HALF)


def range_of(sc, inner, outer, far):
    x, y, z, core = sc[0], sc[1], sc[2], sc[3]
    dx = jnp.where(core == 0, outer, inner)
    dy = jnp.where(core == 0, inner, outer)
    zz = jnp.where(far == 0, z, 1 - z)
    return ((x - dx) & 3) * 8 + zz * 4 + ((y - dy) & 3)


def put_range_bias(k_s, v_s, sc, outers):
    first = jnp.where(iota((HALF, HD), 1) == 0, 1.0, 0.0)
    for i, outer in enumerate(outers):
        for n in range(8):
            bias = jnp.where(range_of(sc, n >> 1, outer, n & 1) <= sc[4], 0.0, NEG)
            k_s[pl.ds((i * 8 + n) * HALF, HALF), HD:] = (first * bias).astype(BF16)
    v_s[:, HD:] = jnp.ones((len(outers) * 8 * HALF, HD), BF16)


def put_slot_bias(k_s, v_s, biases):
    first = jnp.where(iota((HALF, HD), 1) == 0, 1.0, 0.0)
    for i, bias in enumerate(biases):
        k_s[pl.ds(i * HALF, HALF), HD:] = (first * bias).astype(BF16)
    v_s[:, HD:] = jnp.ones((len(biases) * HALF, HD), BF16)


def load_head(q_a, q_b, flag, a):
    cols = slice(a * HD, (a + 1) * HD)
    q = jnp.where(flag == 1, q_a[:, cols], q_b[:, cols])
    one = jnp.where(iota((ROWS, HD), 1) == 0, 1.0, 0.0).astype(BF16)
    return jnp.concatenate([q, one], axis=1)


def near_kernel(sc, q_own, q_other, here, pas, p1, p2, p3, far, mp_out, lp_out, op_out,
                m_out, l_out, o_out, kp, vp, kr, vr):
    core, c, is_r = sc[3], sc[4], sc[5]
    put_ranges(kr, vr, 0, here)
    put_range_bias(kr, vr, sc, (0,))
    for n, ref in enumerate((pas, p1, p2, p3, far)):
        put_keys(kp, vp, n * HALF, ref, 0, HALF, HALF)
    put_slot_bias(kp, vp, [jnp.where(n <= c, 0.0, NEG) for n in range(5)])
    row = iota((ROWS, HD), 0)
    key = core * HALF + iota((ROWS, HD), 1)
    own = jnp.where(key > row, NEG, 0.0)
    edge = jnp.where(key <= row, NEG, 0.0)

    def heads(i):
        at = [WIDE * i + u for u in range(WIDE)]
        qp = [load_head(q_other, q_own, is_r, a) for a in at]
        q = [load_head(q_own, q_other, is_r, a) for a in at]
        sp = [fold(None, qp[u], kp[...], vp[...], left=own, right=edge) for u in range(WIDE)]
        sr = [fold(None, q[u], kr[...], vr[...], left=own) for u in range(WIDE)]
        for u in range(WIDE):
            m_out[at[u]], l_out[at[u]], o_out[at[u]] = sr[u]
            mp_out[at[u]], lp_out[at[u]], op_out[at[u]] = sp[u]

    for i in range(GROUP // WIDE):
        heads(i)


def middle_kernel(sc, q_own, q_other, r1, r3, m_in, l_in, o_in, m_out, l_out, o_out, kr, vr):
    is_r = sc[5]
    put_ranges(kr, vr, 0, r1)
    put_ranges(kr, vr, 8 * HALF, r3)
    put_range_bias(kr, vr, sc, (1, 3))

    def heads(i):
        at = [WIDE * i + u for u in range(WIDE)]
        q = [load_head(q_own, q_other, is_r, a) for a in at]
        state = [(m_in[a], l_in[a], o_in[a]) for a in at]
        for n in range(2):
            rows = slice(n * CHUNK, (n + 1) * CHUNK)
            state = [fold(state[u], q[u], kr[rows, :], vr[rows, :]) for u in range(WIDE)]
        for u in range(WIDE):
            m_out[at[u]], l_out[at[u]], o_out[at[u]] = state[u]

    for i in range(GROUP // WIDE):
        heads(i)


def last_kernel(sc, q_own, q_other, r2a, r2b, sink, mp_in, lp_in, op_in, m_in, l_in, o_in, keep, keep_ml, send,
                kr, vr, ks, vs, mlr_s, mlp_s):
    core, c, is_r = sc[3], sc[4], sc[5]
    put_ranges(kr, vr, 0, r2a, 4)
    put_ranges(kr, vr, 4 * HALF, r2b, 4)
    put_range_bias(kr, vr, sc, (2,))
    ks[...] = jnp.zeros((HALF, 2 * HD), BF16)
    vs[...] = jnp.zeros((HALF, 2 * HD), BF16)
    put_keys(ks, vs, 0, sink, 0, SINK, SINK)
    put_slot_bias(ks, vs, [0.0])
    row = iota((ROWS, HD), 0)
    lane = iota((ROWS, HD), 1)
    seen = (core == 0) & (lane < SINK) & (c * ROWS + row - lane >= RECENT)
    sink_bias = jnp.where(seen, 0.0, NEG)
    mlr_s[...] = jnp.zeros((ROWS, HD), F32)
    mlp_s[...] = jnp.zeros((ROWS, HD), F32)

    def heads(i):
        at = [WIDE * i + u for u in range(WIDE)]
        qp = [load_head(q_other, q_own, is_r, a) for a in at]
        qr = [load_head(q_own, q_other, is_r, a) for a in at]
        sr = [(m_in[a], l_in[a], o_in[a]) for a in at]
        sp = [(mp_in[a], lp_in[a], op_in[a]) for a in at]
        sp = [fold(sp[u], qp[u], ks[...], vs[...], left=sink_bias) for u in range(WIDE)]
        sr = [fold(sr[u], qr[u], kr[...], vr[...]) for u in range(WIDE)]
        for u in range(WIDE):
            cols = slice(at[u] * HD, (at[u] + 1) * HD)
            keep[:, cols] = jnp.where(is_r == 1, sr[u][2], sp[u][2]).astype(BF16)
            send[:, cols] = jnp.where(is_r == 1, sp[u][2], sr[u][2]).astype(BF16)
            for ref, (m, l, _) in ((mlr_s, sr[u]), (mlp_s, sp[u])):
                ref[...] = jnp.where(lane == at[u], m, jnp.where(lane == at[u] + GROUP, l, ref[...]))

    for i in range(GROUP // WIDE):
        heads(i)
    keep_ml[...] = jnp.where(is_r == 1, mlr_s[...], mlp_s[...])
    ml = jnp.where(is_r == 1, mlp_s[...], mlr_s[...])
    high = ml.astype(BF16).astype(F32)
    mid = (ml - high).astype(BF16).astype(F32)
    low = ml - high - mid
    parts = high + pltpu.roll(mid, 2 * GROUP, 1) + pltpu.roll(low, 4 * GROUP, 1)
    send[:, GROUP * HD:] = parts.astype(BF16)


def merge_kernel(keep, keep_ml, got, out_ref):
    ext = got[:, GROUP * HD:].astype(F32)
    theirs = ext + pltpu.roll(ext, HD - 2 * GROUP, 1) + pltpu.roll(ext, HD - 4 * GROUP, 1)
    mine = keep_ml[...]
    used = iota((ROWS, HD), 1) < GROUP
    m0, m1 = jnp.where(used, mine, 0.0), jnp.where(used, theirs, 0.0)
    l0, l1 = pltpu.roll(mine, HD - GROUP, 1), pltpu.roll(theirs, HD - GROUP, 1)
    top = jnp.maximum(m0, m1)
    w0, w1 = jnp.exp2((m0 - top) * SCALE), jnp.exp2((m1 - top) * SCALE)
    scale = 1.0 / jnp.where(used, l0 * w0 + l1 * w1, 1.0)
    w0, w1 = w0 * scale, w1 * scale
    for a in range(GROUP):
        cols = slice(a * HD, (a + 1) * HD)
        out = keep[:, cols].astype(F32) * w0[:, a:a + 1] + got[:, cols].astype(F32) * w1[:, a:a + 1]
        out_ref[:, cols] = out.astype(BF16)


def pages_kernel(sc, r0, r1, r2a, r2b, r3, out_ref):
    c = sc[4]
    row = iota((2 * PAGE, HD), 0)
    lane = iota((2 * PAGE, HD), 1)
    same_row = (lane & (PAGE - 1)) == (row & (PAGE - 1))
    want = (2 * c + (row >> 4)).astype(F32)
    for outer, (refa, refb, base) in enumerate(((r0, r0, 0), (r1, r1, 0), (r2a, r2b, 4), (r3, r3, 0))):
        codes = refb[(8 - base) * ROWS:(8 - base) * ROWS + META, :].astype(F32)
        for n in range(8):
            ref, slot = (refa, n) if n < 4 else (refb, n - base)
            select = jnp.where(same_row & (codes[n:n + 1, :] == want), 1.0, 0.0).astype(BF16)
            block = range_of(sc, n >> 1, outer, n & 1)
            for part in range(2):
                at = slot * ROWS + part * HALF
                pages = jnp.dot(select, ref[at:at + HALF, :], preferred_element_type=F32)
                out_ref[block, :, part * HD:(part + 1) * HD] = pages.astype(BF16)


VMEM_SPEC = pl.BlockSpec(memory_space=pltpu.VMEM)
SMEM_SPEC = pl.BlockSpec(memory_space=pltpu.SMEM)


def call(kernel, out_shape, scratch, flops, sc, *args):
    many = isinstance(out_shape, tuple)
    specs = ([SMEM_SPEC] if sc is not None else []) + [VMEM_SPEC] * len(args)
    operands = ([sc] if sc is not None else []) + list(args)
    return pl.pallas_call(
        kernel,
        out_shape=out_shape,
        in_specs=specs,
        out_specs=(VMEM_SPEC,) * len(out_shape) if many else VMEM_SPEC,
        scratch_shapes=scratch,
        compiler_params=pltpu.CompilerParams(vmem_limit_bytes=16 * 1024 * 1024),
        cost_estimate=pl.CostEstimate(flops=flops, bytes_accessed=4 << 20, transcendentals=flops // 512),
    )(*operands)


def keys(rows):
    return [pltpu.VMEM((rows, 2 * HD), BF16), pltpu.VMEM((rows, 2 * HD), BF16)]


def shards(q, k, v, head_kind, page_owner):
    c = lax.axis_index("ctx")
    tp = lax.axis_index("tp")
    x, z, y = c // 8, (c // 4) % 2, c % 4
    core = tp % 2
    is_r = jnp.sum(jnp.where(lax.iota(jnp.int32, head_kind.shape[0]) == tp, head_kind, 0)) == 1
    sc = jnp.stack([x, y, z, core, c, is_r.astype(jnp.int32), tp, tp]).astype(jnp.int32)

    low = jnp.concatenate([k[:HALF], v[:HALF]])
    high = jnp.concatenate([k[HALF:], v[HALF:]])
    stay = jnp.where(core == 0, low, high)
    came = lax.ppermute(jnp.where(core == 0, high, low), "tp", CORE_SWAP)
    q_other = lax.ppermute(q, "tp", CORE_SWAP)
    ret = jnp.where(is_r, stay, came)
    pas = jnp.where(is_r, came, stay)

    earlier = lax.iota(jnp.int32, 16)[None, :] < lax.iota(jnp.int32, 16)[:, None]
    rank = jnp.sum(((page_owner[:, None] == page_owner[None, :]) & earlier).astype(jnp.int32), axis=1)
    code = page_owner * 2 + rank
    code = jnp.where(core == 0, code[:8], code[8:]).astype(BF16)
    meta = jnp.broadcast_to(jnp.repeat(code, PAGE)[None, :], (META, HD))

    theirs = lax.ppermute(jnp.concatenate([ret, pas, meta]), "ctx", Z_SWAP)
    theirs, q_other = lax.optimization_barrier((theirs, q_other))
    from_x = lax.ppermute(theirs[ROWS:2 * ROWS], "ctx", X_STEP)
    both = jnp.concatenate([ret, theirs[:ROWS]])
    low = jnp.where(z == 0, pas, theirs[ROWS:2 * ROWS])
    sink = jnp.concatenate([low[:SINK], low[HALF:HALF + SINK]])
    line = iota((META, HD), 0)
    meta = jnp.where((line & 1) == 0, meta, theirs[2 * ROWS:])

    axes = ("ctx", "tp")
    message = jnp.concatenate([both, sink, meta])
    got = {s: lax.ppermute(message, axes, STAGE_1[s]) for s in (1, 3, 2)}
    pas, from_x, got[1] = lax.optimization_barrier((pas, from_x, got[1]))
    far = jnp.where(z == 1, theirs[ROWS:2 * ROWS], from_x)
    p = {s: lax.ppermute(jnp.where(y + s < 4, pas, far), "ctx", Y_SHIFT[s]) for s in (1, 3, 2)}

    for s in (1, 2, 3):
        meta = jnp.where((line >> 1) == s, got[s][2 * ROWS + 2 * SINK:], meta)
        sink = jnp.where(y == s, got[s][2 * ROWS:2 * ROWS + 2 * SINK], sink)
    message = jnp.concatenate([both] + [got[s][:2 * ROWS] for s in (1, 2, 3)] + [meta, sink])

    r = {0: message} | {s: lax.ppermute(message, axes, STAGE_2[s]) for s in (1, 3)}
    state = (jax.ShapeDtypeStruct((GROUP, ROWS, HD), F32),) * 3
    unit = 2 * 2048 * 256 * 512
    *now_p, now_m, now_l, now_o = call(
        near_kernel, state + state, keys(5 * HALF) + keys(8 * HALF), 60 * unit,
        sc, q, q_other, message, pas, p[1], p[2], p[3], far)
    late, now_m = lax.optimization_barrier((message, now_m))
    part = 4 * ROWS
    two = [lax.ppermute(late[:part], axes, STAGE_2[2]), lax.ppermute(late[part:], axes, STAGE_2[2])]
    now_m, now_l, now_o = call(
        middle_kernel, state, keys(16 * HALF), 8 * unit, sc, q, q_other, r[1], r[3], now_m, now_l, now_o)
    for s in (1, 2, 3):
        tail = r[s][8 * ROWS + META:] if s != 2 else two[1][4 * ROWS + META:]
        sink = jnp.where(x == s, tail, sink)
    sc_l, now_m = lax.optimization_barrier((sc, now_m))
    pages = call(
        pages_kernel, jax.ShapeDtypeStruct((32, 2 * PAGE, 2 * HD), BF16), [], unit // 4,
        sc_l, r[0], r[1], *two, r[3])
    got_pages = lax.ppermute(pages, "tp", CORE_SWAP)
    keep, keep_ml, send = call(
        last_kernel,
        (
            jax.ShapeDtypeStruct((ROWS, GROUP * HD), BF16),
            jax.ShapeDtypeStruct((ROWS, HD), F32),
            jax.ShapeDtypeStruct((ROWS, (GROUP + 1) * HD), BF16),
        ),
        keys(8 * HALF) + keys(HALF) + [pltpu.VMEM((ROWS, HD), F32)] * 2,
        5 * unit, sc_l, q, q_other, *two, sink, *now_p, now_m, now_l, now_o)

    got = lax.ppermute(send, "tp", CORE_SWAP)
    attn_out = call(
        merge_kernel, jax.ShapeDtypeStruct((ROWS, GROUP * HD), BF16), [], unit // 4, None, keep, keep_ml, got)
    decode_cache = jnp.where(is_r, pages + got_pages, jnp.zeros((), BF16)).reshape(64, PAGE, 2 * HD)
    return attn_out, decode_cache


def solution(mesh):
    return jax.shard_map(
        shards,
        mesh=mesh,
        in_specs=(P("ctx", "tp"), P("ctx", "tp"), P("ctx", "tp"), P(), P("ctx")),
        out_specs=(P("ctx", "tp"), P("ctx", None, "tp")),
        check_vma=False,
    )
```

```python
import math

import jax
import jax.numpy as jnp
from jax import lax
from jax.experimental import pallas as pl
from jax.experimental.pallas import tpu as pltpu
from jax.sharding import PartitionSpec as P

GROUP = 8
HD = 128
SINK = 64
RECENT = 1024
PAGE = 16
ROWS = 256
HALF = 128
META = 16
CHUNK = 1024
WIDE = 4
MIDDLE_WIDE = 2
NEG = -1e30
SCALE = math.log2(math.e) / math.sqrt(HD)
F32 = jnp.float32
BF16 = jnp.bfloat16


def ctx_of(x, z, y):
    return (x % 4) * 8 + (z % 2) * 4 + (y % 4)


CHIPS = [(x, z, y) for x in range(4) for z in range(2) for y in range(4)]
CORE_SWAP = [(i, i ^ 1) for i in range(8)]
Z_SWAP = [(ctx_of(x, z, y), ctx_of(x, z + 1, y)) for x, z, y in CHIPS]
X_STEP = [(ctx_of(x, 0, y), ctx_of(x + 1, 0, y)) for x in range(3) for y in range(4)]
Y_SHIFT = {s: [(ctx_of(x, z, y), ctx_of(x, z, y + s)) for x, z, y in CHIPS] for s in (1, 2, 3)}


def two_ways(s, along_y):
    pairs = []
    for x, z, y in CHIPS:
        for tp in range(8):
            there = ctx_of(x, z, y + s) if tp % 2 == along_y else ctx_of(x + s, z, y)
            pairs.append((ctx_of(x, z, y) * 8 + tp, there * 8 + tp))
    return pairs


STAGE_1 = {s: two_ways(s, 0) for s in (1, 2, 3)}
STAGE_2 = {s: two_ways(s, 1) for s in (1, 2, 3)}


def nt_dot(a, b):
    return lax.dot_general(a, b, (((1,), (1,)), ((), ())), preferred_element_type=F32)


def iota(shape, axis):
    return lax.broadcasted_iota(jnp.int32, shape, axis)


def fold(state, q, k, v, left=None, right=None):
    s = nt_dot(q, k)
    if left is not None:
        s = jnp.concatenate([s[:, :HD] + left, s[:, HD:]], axis=1) if s.shape[1] > HD else s + left
    if right is not None:
        s = jnp.concatenate([s[:, :-HD], s[:, -HD:] + right], axis=1)
    high = jnp.max(s, axis=1, keepdims=True)
    top = jnp.broadcast_to(high, (ROWS, HD)) if state is None else jnp.maximum(state[0], high)
    p = jnp.exp2((s - jnp.concatenate([top] * (s.shape[1] // HD), axis=1)) * SCALE).astype(BF16)
    up = jnp.dot(p, v, preferred_element_type=F32)
    if state is None:
        return top, up[:, HD:], up[:, :HD]
    keep = jnp.exp2((state[0] - top) * SCALE)
    return top, state[1] * keep + up[:, HD:], state[2] * keep + up[:, :HD]


def put_keys(k_s, v_s, at, ref, first, rows, gap):
    k_s[pl.ds(at, rows), 0:HD] = ref[first:first + rows, :]
    v_s[pl.ds(at, rows), 0:HD] = ref[first + gap:first + gap + rows, :]


def put_ranges(k_s, v_s, at, ref, count=8):
    for n in range(count):
        put_keys(k_s, v_s, at + n * HALF, ref, n * ROWS, HALF, HALF)


def range_of(sc, inner, outer, far):
    x, y, z, core = sc[0], sc[1], sc[2], sc[3]
    dx = jnp.where(core == 0, outer, inner)
    dy = jnp.where(core == 0, inner, outer)
    zz = jnp.where(far == 0, z, 1 - z)
    return ((x - dx) & 3) * 8 + zz * 4 + ((y - dy) & 3)


def put_range_bias(k_s, v_s, sc, outers):
    first = jnp.where(iota((HALF, HD), 1) == 0, 1.0, 0.0)
    for i, outer in enumerate(outers):
        for n in range(8):
            bias = jnp.where(range_of(sc, n >> 1, outer, n & 1) <= sc[4], 0.0, NEG)
            k_s[pl.ds((i * 8 + n) * HALF, HALF), HD:] = (first * bias).astype(BF16)
    v_s[:, HD:] = jnp.ones((len(outers) * 8 * HALF, HD), BF16)


def put_slot_bias(k_s, v_s, biases):
    first = jnp.where(iota((HALF, HD), 1) == 0, 1.0, 0.0)
    for i, bias in enumerate(biases):
        k_s[pl.ds(i * HALF, HALF), HD:] = (first * bias).astype(BF16)
    v_s[:, HD:] = jnp.ones((len(biases) * HALF, HD), BF16)


def load_head(q_a, q_b, flag, a):
    cols = slice(a * HD, (a + 1) * HD)
    q = jnp.where(flag == 1, q_a[:, cols], q_b[:, cols])
    one = jnp.where(iota((ROWS, HD), 1) == 0, 1.0, 0.0).astype(BF16)
    return jnp.concatenate([q, one], axis=1)


def near_kernel(sc, q_own, q_other, here, pas, p1, p2, p3, far, mp_out, lp_out, op_out,
                m_out, l_out, o_out, kp, vp, kr, vr):
    core, c, is_r = sc[3], sc[4], sc[5]
    put_ranges(kr, vr, 0, here)
    put_range_bias(kr, vr, sc, (0,))
    for n, ref in enumerate((pas, p1, p2, p3, far)):
        put_keys(kp, vp, n * HALF, ref, 0, HALF, HALF)
    put_slot_bias(kp, vp, [jnp.where(n <= c, 0.0, NEG) for n in range(5)])
    row = iota((ROWS, HD), 0)
    key = core * HALF + iota((ROWS, HD), 1)
    own = jnp.where(key > row, NEG, 0.0)
    edge = jnp.where(key <= row, NEG, 0.0)

    def heads(i):
        at = [WIDE * i + u for u in range(WIDE)]
        qp = [load_head(q_other, q_own, is_r, a) for a in at]
        q = [load_head(q_own, q_other, is_r, a) for a in at]
        sp = [fold(None, qp[u], kp[...], vp[...], left=own, right=edge) for u in range(WIDE)]
        sr = [fold(None, q[u], kr[...], vr[...], left=own) for u in range(WIDE)]
        for u in range(WIDE):
            m_out[at[u]], l_out[at[u]], o_out[at[u]] = sr[u]
            mp_out[at[u]], lp_out[at[u]], op_out[at[u]] = sp[u]

    for i in range(GROUP // WIDE):
        heads(i)


def middle_kernel(sc, q_own, q_other, r1, r3, m_in, l_in, o_in, m_out, l_out, o_out, kr, vr):
    is_r = sc[5]
    put_ranges(kr, vr, 0, r1)
    put_ranges(kr, vr, 8 * HALF, r3)
    put_range_bias(kr, vr, sc, (1, 3))

    def heads(i):
        at = [MIDDLE_WIDE * i + u for u in range(MIDDLE_WIDE)]
        q = [load_head(q_own, q_other, is_r, a) for a in at]
        state = [(m_in[a], l_in[a], o_in[a]) for a in at]
        for n in range(2):
            rows = slice(n * CHUNK, (n + 1) * CHUNK)
            state = [fold(state[u], q[u], kr[rows, :], vr[rows, :]) for u in range(MIDDLE_WIDE)]
        for u in range(MIDDLE_WIDE):
            m_out[at[u]], l_out[at[u]], o_out[at[u]] = state[u]

    for i in range(GROUP // MIDDLE_WIDE):
        heads(i)


def last_kernel(sc, q_own, q_other, r2a, r2b, sink, mp_in, lp_in, op_in, m_in, l_in, o_in, keep, keep_ml, send,
                kr, vr, ks, vs, mlr_s, mlp_s):
    core, c, is_r = sc[3], sc[4], sc[5]
    put_ranges(kr, vr, 0, r2a, 4)
    put_ranges(kr, vr, 4 * HALF, r2b, 4)
    put_range_bias(kr, vr, sc, (2,))
    ks[...] = jnp.zeros((HALF, 2 * HD), BF16)
    vs[...] = jnp.zeros((HALF, 2 * HD), BF16)
    put_keys(ks, vs, 0, sink, 0, SINK, SINK)
    put_slot_bias(ks, vs, [0.0])
    row = iota((ROWS, HD), 0)
    lane = iota((ROWS, HD), 1)
    seen = (core == 0) & (lane < SINK) & (c * ROWS + row - lane >= RECENT)
    sink_bias = jnp.where(seen, 0.0, NEG)
    mlr_s[...] = jnp.zeros((ROWS, HD), F32)
    mlp_s[...] = jnp.zeros((ROWS, HD), F32)

    def heads(i):
        at = [WIDE * i + u for u in range(WIDE)]
        qp = [load_head(q_other, q_own, is_r, a) for a in at]
        qr = [load_head(q_own, q_other, is_r, a) for a in at]
        sr = [(m_in[a], l_in[a], o_in[a]) for a in at]
        sp = [(mp_in[a], lp_in[a], op_in[a]) for a in at]
        sp = [fold(sp[u], qp[u], ks[...], vs[...], left=sink_bias) for u in range(WIDE)]
        sr = [fold(sr[u], qr[u], kr[...], vr[...]) for u in range(WIDE)]
        for u in range(WIDE):
            cols = slice(at[u] * HD, (at[u] + 1) * HD)
            keep[:, cols] = jnp.where(is_r == 1, sr[u][2], sp[u][2]).astype(BF16)
            send[:, cols] = jnp.where(is_r == 1, sp[u][2], sr[u][2]).astype(BF16)
            for ref, (m, l, _) in ((mlr_s, sr[u]), (mlp_s, sp[u])):
                ref[...] = jnp.where(lane == at[u], m, jnp.where(lane == at[u] + GROUP, l, ref[...]))

    for i in range(GROUP // WIDE):
        heads(i)
    keep_ml[...] = jnp.where(is_r == 1, mlr_s[...], mlp_s[...])
    ml = jnp.where(is_r == 1, mlp_s[...], mlr_s[...])
    high = ml.astype(BF16).astype(F32)
    mid = (ml - high).astype(BF16).astype(F32)
    low = ml - high - mid
    parts = high + pltpu.roll(mid, 2 * GROUP, 1) + pltpu.roll(low, 4 * GROUP, 1)
    send[:, GROUP * HD:] = parts.astype(BF16)


def merge_kernel(keep, keep_ml, got, out_ref):
    ext = got[:, GROUP * HD:].astype(F32)
    theirs = ext + pltpu.roll(ext, HD - 2 * GROUP, 1) + pltpu.roll(ext, HD - 4 * GROUP, 1)
    mine = keep_ml[...]
    used = iota((ROWS, HD), 1) < GROUP
    m0, m1 = jnp.where(used, mine, 0.0), jnp.where(used, theirs, 0.0)
    l0, l1 = pltpu.roll(mine, HD - GROUP, 1), pltpu.roll(theirs, HD - GROUP, 1)
    top = jnp.maximum(m0, m1)
    w0, w1 = jnp.exp2((m0 - top) * SCALE), jnp.exp2((m1 - top) * SCALE)
    scale = 1.0 / jnp.where(used, l0 * w0 + l1 * w1, 1.0)
    w0, w1 = w0 * scale, w1 * scale
    for a in range(GROUP):
        cols = slice(a * HD, (a + 1) * HD)
        out = keep[:, cols].astype(F32) * w0[:, a:a + 1] + got[:, cols].astype(F32) * w1[:, a:a + 1]
        out_ref[:, cols] = out.astype(BF16)


def pages_kernel(sc, r0, r1, r2a, r2b, r3, out_ref):
    c = sc[4]
    row = iota((2 * PAGE, HD), 0)
    lane = iota((2 * PAGE, HD), 1)
    same_row = (lane & (PAGE - 1)) == (row & (PAGE - 1))
    want = (2 * c + (row >> 4)).astype(F32)
    for outer, (refa, refb, base) in enumerate(((r0, r0, 0), (r1, r1, 0), (r2a, r2b, 4), (r3, r3, 0))):
        codes = refb[(8 - base) * ROWS:(8 - base) * ROWS + META, :].astype(F32)
        for n in range(8):
            ref, slot = (refa, n) if n < 4 else (refb, n - base)
            select = jnp.where(same_row & (codes[n:n + 1, :] == want), 1.0, 0.0).astype(BF16)
            block = range_of(sc, n >> 1, outer, n & 1)
            for part in range(2):
                at = slot * ROWS + part * HALF
                pages = jnp.dot(select, ref[at:at + HALF, :], preferred_element_type=F32)
                out_ref[block, :, part * HD:(part + 1) * HD] = pages.astype(BF16)


VMEM_SPEC = pl.BlockSpec(memory_space=pltpu.VMEM)
SMEM_SPEC = pl.BlockSpec(memory_space=pltpu.SMEM)


def call(kernel, out_shape, scratch, flops, sc, *args):
    many = isinstance(out_shape, tuple)
    specs = ([SMEM_SPEC] if sc is not None else []) + [VMEM_SPEC] * len(args)
    operands = ([sc] if sc is not None else []) + list(args)
    return pl.pallas_call(
        kernel,
        out_shape=out_shape,
        in_specs=specs,
        out_specs=(VMEM_SPEC,) * len(out_shape) if many else VMEM_SPEC,
        scratch_shapes=scratch,
        compiler_params=pltpu.CompilerParams(vmem_limit_bytes=16 * 1024 * 1024),
        cost_estimate=pl.CostEstimate(flops=flops, bytes_accessed=4 << 20, transcendentals=flops // 512),
    )(*operands)


def keys(rows):
    return [pltpu.VMEM((rows, 2 * HD), BF16), pltpu.VMEM((rows, 2 * HD), BF16)]


def shards(q, k, v, head_kind, page_owner):
    c = lax.axis_index("ctx")
    tp = lax.axis_index("tp")
    x, z, y = c // 8, (c // 4) % 2, c % 4
    core = tp % 2
    is_r = jnp.sum(jnp.where(lax.iota(jnp.int32, head_kind.shape[0]) == tp, head_kind, 0)) == 1
    sc = jnp.stack([x, y, z, core, c, is_r.astype(jnp.int32), tp, tp]).astype(jnp.int32)

    low = jnp.concatenate([k[:HALF], v[:HALF]])
    high = jnp.concatenate([k[HALF:], v[HALF:]])
    stay = jnp.where(core == 0, low, high)
    came = lax.ppermute(jnp.where(core == 0, high, low), "tp", CORE_SWAP)
    q_other = lax.ppermute(q, "tp", CORE_SWAP)
    ret = jnp.where(is_r, stay, came)
    pas = jnp.where(is_r, came, stay)

    earlier = lax.iota(jnp.int32, 16)[None, :] < lax.iota(jnp.int32, 16)[:, None]
    rank = jnp.sum(((page_owner[:, None] == page_owner[None, :]) & earlier).astype(jnp.int32), axis=1)
    code = page_owner * 2 + rank
    code = jnp.where(core == 0, code[:8], code[8:]).astype(BF16)
    meta = jnp.broadcast_to(jnp.repeat(code, PAGE)[None, :], (META, HD))

    theirs = lax.ppermute(jnp.concatenate([ret, pas, meta]), "ctx", Z_SWAP)
    theirs, q_other = lax.optimization_barrier((theirs, q_other))
    from_x = lax.ppermute(theirs[ROWS:2 * ROWS], "ctx", X_STEP)
    both = jnp.concatenate([ret, theirs[:ROWS]])
    low = jnp.where(z == 0, pas, theirs[ROWS:2 * ROWS])
    sink = jnp.concatenate([low[:SINK], low[HALF:HALF + SINK]])
    line = iota((META, HD), 0)
    meta = jnp.where((line & 1) == 0, meta, theirs[2 * ROWS:])

    axes = ("ctx", "tp")
    message = jnp.concatenate([both, sink, meta])
    got = {s: lax.ppermute(message, axes, STAGE_1[s]) for s in (1, 3, 2)}
    pas, from_x, got[1] = lax.optimization_barrier((pas, from_x, got[1]))
    far = jnp.where(z == 1, theirs[ROWS:2 * ROWS], from_x)
    p = {s: lax.ppermute(jnp.where(y + s < 4, pas, far), "ctx", Y_SHIFT[s]) for s in (1, 3, 2)}

    for s in (1, 2, 3):
        meta = jnp.where((line >> 1) == s, got[s][2 * ROWS + 2 * SINK:], meta)
        sink = jnp.where(y == s, got[s][2 * ROWS:2 * ROWS + 2 * SINK], sink)
    message = jnp.concatenate([both] + [got[s][:2 * ROWS] for s in (1, 2, 3)] + [meta, sink])

    r = {0: message} | {s: lax.ppermute(message, axes, STAGE_2[s]) for s in (1, 3)}
    state = (jax.ShapeDtypeStruct((GROUP, ROWS, HD), F32),) * 3
    unit = 2 * 2048 * 256 * 512
    *now_p, now_m, now_l, now_o = call(
        near_kernel, state + state, keys(5 * HALF) + keys(8 * HALF), 60 * unit,
        sc, q, q_other, message, pas, p[1], p[2], p[3], far)
    late, now_m = lax.optimization_barrier((message, now_m))
    part = 4 * ROWS
    two = [lax.ppermute(late[:part], axes, STAGE_2[2]), lax.ppermute(late[part:], axes, STAGE_2[2])]
    now_m, now_l, now_o = call(
        middle_kernel, state, keys(16 * HALF), 8 * unit, sc, q, q_other, r[1], r[3], now_m, now_l, now_o)
    for s in (1, 2, 3):
        tail = r[s][8 * ROWS + META:] if s != 2 else two[1][4 * ROWS + META:]
        sink = jnp.where(x == s, tail, sink)
    sc_l, now_m = lax.optimization_barrier((sc, now_m))
    pages = call(
        pages_kernel, jax.ShapeDtypeStruct((32, 2 * PAGE, 2 * HD), BF16), [], unit // 4,
        sc_l, r[0], r[1], *two, r[3])
    got_pages = lax.ppermute(pages, "tp", CORE_SWAP)
    keep, keep_ml, send = call(
        last_kernel,
        (
            jax.ShapeDtypeStruct((ROWS, GROUP * HD), BF16),
            jax.ShapeDtypeStruct((ROWS, HD), F32),
            jax.ShapeDtypeStruct((ROWS, (GROUP + 1) * HD), BF16),
        ),
        keys(8 * HALF) + keys(HALF) + [pltpu.VMEM((ROWS, HD), F32)] * 2,
        5 * unit, sc_l, q, q_other, *two, sink, *now_p, now_m, now_l, now_o)

    got = lax.ppermute(send, "tp", CORE_SWAP)
    attn_out = call(
        merge_kernel, jax.ShapeDtypeStruct((ROWS, GROUP * HD), BF16), [], unit // 4, None, keep, keep_ml, got)
    decode_cache = jnp.where(is_r, pages + got_pages, jnp.zeros((), BF16)).reshape(64, PAGE, 2 * HD)
    return attn_out, decode_cache


def solution(mesh):
    return jax.shard_map(
        shards,
        mesh=mesh,
        in_specs=(P("ctx", "tp"), P("ctx", "tp"), P("ctx", "tp"), P(), P("ctx")),
        out_specs=(P("ctx", "tp"), P("ctx", None, "tp")),
        check_vma=False,
    )
```
